32 devices in a mesh: bins: 4 (over z), mp: 2 (over core), batch: 4 (over y, x).
Axes of the slice: x: 2, y: 2, z: 4, core: 2. Of those that a mesh axis runs over, the one named last changes fastest.
Arguments:
- signal: bfloat16 [64, 1024, 768], P('batch', 'bins', 'mp'), may hold values from -12 to 12
- segment_number_index: int32 [64, 1024], P('batch'), may hold values from 0 to 3, as said below
- cotangent: bfloat16 [64, 512, 768], P('batch', 'bins', 'mp'), may hold values from -12 to 12
- conv_wide: bfloat16 [5, 768, 768], P(None, None, 'mp'), may hold values from -0.09375 to 0.09375
- dilated_kernel_taps: bfloat16 [3, 768, 384], P(None, None, 'mp'), may hold values from -0.125 to 0.125
- pointwise: bfloat16 [384, 768], P(None, 'mp'), may hold values from -0.3125 to 0.3125
- gain_in: float32 [768], P('mp'), may hold values from 0.25 to 1.75
- shift_in: float32 [768], P('mp'), may hold values from -3 to 3
- gain_mid: float32 [768], P('mp'), may hold values from 0.25 to 1.75
- shift_mid: float32 [768], P('mp'), may hold values from -3 to 3
- hidden_norm_gain: float32 [384], P('mp'), may hold values from 0.25 to 1.75
- hidden_norm_bias: float32 [384], P('mp'), may hold values from -3 to 3
Outputs:
- output: bfloat16 [64, 512, 768], P('batch', 'bins', 'mp')
- grad_signal: float32 [64, 1024, 768], P('batch', 'bins', 'mp')
- grad_conv_wide: float32 [5, 768, 768], P(None, None, 'mp')
- dilated_kernel_gradient: float32 [3, 768, 384], P(None, None, 'mp')
- grad_pointwise: float32 [384, 768], P(None, 'mp')
- grad_gain_in: float32 [768], P('mp')
- grad_shift_in: float32 [768], P('mp')
- grad_gain_mid: float32 [768], P('mp')
- grad_shift_mid: float32 [768], P('mp')
- hidden_gain_gradient: float32 [384], P('mp')
- hidden_bias_gradient: float32 [384], P('mp')
The draws below stay inside these ranges and needn't reach their ends.
Inputs may be any that keep to these rules, and one draw needn't show every extreme that they name: `segment_number_index`: each row holds four sequences 0, 1, 2, 3 in order; sequence j (j < 3) ends at an even bin within 64 bins of (j + 1) * 256.
All inputs are finite; a program needn't handle non-finite values.
Results may differ from the reference program's by a relative error of at most 0.017.
Values may be sent and summed in bfloat16 or wider, within the bound.
A program may use at most 192 MiB of HBM per device.

```python
import jax
import jax.numpy as jnp
from jax import lax

C = 768
C2 = 384
K1 = 5
K2 = 3
DILATION_STRIDE = 57
B0_DEV = 256
GROUPS = 64
BINS = 1024
POOLED = 512


def ramped(key, base, length, width):
    key_mean, key_rough, key_row, key_tilt, key_size = jax.random.split(key, 5)
    row_count = base.shape[0]
    position_index = jnp.arange(length, dtype=jnp.float32) / (length - 1)
    row_index = jnp.arange(row_count, dtype=jnp.float32) / (row_count - 1)
    mean_chan = 0.5 * jax.random.normal(key_mean, (width,), jnp.float32)
    row_tilt = jax.random.normal(key_tilt, (width,), jnp.float32)
    row_mean = (2.0 * row_index - 1.0)[:, None, None] * row_tilt[None, None, :] + 0.5 * jax.random.normal(key_row, (row_count, 1, width), jnp.float32)
    row_size = (0.5 + row_index[:, None, None]) * jnp.exp(jax.random.uniform(key_size, (row_count, 1, 1), jnp.float32, -0.2, 0.2))
    rough = jnp.exp(jax.random.uniform(key_rough, base.shape[:2] + (1,), jnp.float32, -0.35, 0.35))
    ramp = 0.6 + 1.2 * position_index[None, :, None]
    values = (base + mean_chan * (0.5 + position_index[None, :, None]) + row_mean) * ramp * rough * row_size
    return jnp.clip(values, -12.0, 12.0)


def draw_signal(key, part):
    key = jax.random.fold_in(key, 1)
    key_base, key_ramp = jax.random.split(key, 2)
    base = jax.random.truncated_normal(key_base, -4.0, 4.0, (GROUPS, BINS, C), jnp.float32)
    return ramped(key_ramp, base, BINS, C).astype(jnp.bfloat16)


def draw_cotangent(key, part):
    key = jax.random.fold_in(key, 2)
    key_base, key_ramp = jax.random.split(key, 2)
    base = jax.random.truncated_normal(key_base, -4.0, 4.0, (GROUPS, POOLED, C), jnp.float32)
    return ramped(key_ramp, base, POOLED, C).astype(jnp.bfloat16)


def draw_segment_number_index(key, part):
    key = jax.random.fold_in(key, 3)
    jitter = 2 * jax.random.randint(key, (GROUPS, 3), -(B0_DEV // 8), B0_DEV // 8 + 1)
    ends = (jnp.arange(1, 4, dtype=jnp.int32) * (BINS // 4))[None, :] + jitter
    position_index = jnp.arange(BINS, dtype=jnp.int32)
    return jnp.sum((position_index[None, :, None] >= ends[:, None, :]).astype(jnp.int32), axis=2)


def shard_levels(key, shape, cuts, least, high):
    level, own = 1.0, jax.random.fold_in(key, 6)
    for position, shards_of in cuts:
        draws = jnp.exp(jax.random.uniform(jax.random.fold_in(own, position), (shards_of,), jnp.float32, least / len(cuts), high / len(cuts)))
        level = level * jnp.repeat(draws, shape[position] // shards_of).reshape([-1 if axis == position else 1 for axis in range(len(shape))])
    return level


def scatter_about(stream_key, dims, scale, bound, cuts=(), held_as=jnp.bfloat16):
    array = jax.random.normal(stream_key, dims, jnp.float32) * scale
    if len(cuts) > 0:
        array = shard_levels(stream_key, dims, cuts, -0.22, 0.18) * array
    return jnp.clip(array, min=-bound, max=bound).astype(held_as)


def setup_inputs(seed: int = 0) -> dict:
    seeds = jax.random.split(jax.random.key(seed), 13)
    signal = draw_signal(jax.random.fold_in(seeds[12], 71), 0)
    segment_number_index = draw_segment_number_index(jax.random.fold_in(seeds[12], 71), 0)
    cotangent = draw_cotangent(jax.random.fold_in(seeds[12], 71), 0)
    conv_wide = scatter_about(seeds[3], (K1, C, C), (K1 * C) ** -0.5, 0.09375, ((2, 2),))
    dilated_kernel_taps = scatter_about(seeds[4], (K2, C, C2), (K2 * C) ** -0.5, 0.125, ((2, 2),))
    pointwise = scatter_about(seeds[5], (C2, C), C2 ** -0.5, 0.3125, ((1, 2),))
    gain_in = jnp.clip(1.0 + 0.15 * jax.random.normal(seeds[6], (C,), jnp.float32), 0.25, 1.75)
    shift_in = scatter_about(seeds[7], (C,), 0.5, 3.0, ((0, 2),), jnp.float32)
    gain_mid = jnp.clip(1.0 + 0.15 * jax.random.normal(seeds[8], (C,), jnp.float32), 0.25, 1.75)
    shift_mid = scatter_about(seeds[9], (C,), 0.5, 3.0, ((0, 2),), jnp.float32)
    hidden_norm_gain = jnp.clip(1.0 + 0.15 * jax.random.normal(seeds[10], (C2,), jnp.float32), 0.25, 1.75)
    hidden_norm_bias = scatter_about(seeds[11], (C2,), 0.5, 3.0, ((0, 2),), jnp.float32)
    return dict(signal=signal, segment_number_index=segment_number_index, cotangent=cotangent, conv_wide=conv_wide, dilated_kernel_taps=dilated_kernel_taps, pointwise=pointwise, gain_in=gain_in, shift_in=shift_in, gain_mid=gain_mid, shift_mid=shift_mid, hidden_norm_gain=hidden_norm_gain, hidden_norm_bias=hidden_norm_bias)


@jax.custom_vjp
def lower_bound_value(v):
    return lax.optimization_barrier(v.astype(jnp.bfloat16)).astype(jnp.float32)

@jax.custom_vjp
def lower_backward_value(v):
    return v

def low_keep(v):
    return (lower_bound_value(v), None)

def low_pass(kept, grad):
    return (grad,)

def back_keep(v):
    return (v, None)

def back_low(kept, grad):
    return (lower_bound_value(grad),)
lower_bound_value.defvjp(low_keep, low_pass)
lower_backward_value.defvjp(back_keep, back_low)
EPSILON = 1e-05

def normalized_values(values, gain, shift):
    centre = lax.optimization_barrier(jnp.mean(values, axis=(0, 1)))
    spread = values - centre
    variance = lax.optimization_barrier(jnp.mean(spread * spread, axis=(0, 1)))
    return gain * spread * lax.rsqrt(variance + EPSILON) + shift

def shifted(values, offset, fill):
    width = abs(offset)
    length = values.shape[1]
    pads = [(0, 0)] * values.ndim
    pads[1] = (width, width)
    padded = jnp.pad(values, pads, constant_values=fill)
    return padded[:, width + offset:width + offset + length]

def masked_convolution(hidden, taps, segments, offsets):
    total = None
    for index, offset in enumerate(offsets):
        same = (shifted(segments, offset, -1) == segments).astype(jnp.float32)
        moved = shifted(hidden, offset, 0.0) * same[..., None]
        term = jnp.einsum('gtc,cd->gtd', moved, taps[index], precision=lax.Precision.HIGHEST)
        total = term if total is None else total + term
    return total

def reference(signal, segment_number_index, cotangent, conv_wide, dilated_kernel_taps, pointwise, gain_in, shift_in, gain_mid, shift_mid, hidden_norm_gain, hidden_norm_bias):
    pooled_segment_index = segment_number_index[:, ::2]

    def forward(source, taps_wide, dilated_taps_local, project, g_in, b_in, g_mid, b_mid, hidden_gain_term, hidden_bias_term):
        hidden_in = lower_bound_value(jax.nn.gelu(normalized_values(source, g_in, b_in)))
        conv_out = lower_backward_value(masked_convolution(hidden_in, taps_wide, segment_number_index, (-2, -1, 0, 1, 2)))
        pooled = jnp.logaddexp(conv_out[:, 0::2], conv_out[:, 1::2])
        middle_hidden_state = lower_bound_value(jax.nn.gelu(normalized_values(pooled, g_mid, b_mid)))
        dilated_output = lower_backward_value(masked_convolution(middle_hidden_state, dilated_taps_local, pooled_segment_index, (-DILATION_STRIDE, 0, DILATION_STRIDE)))
        upper_hidden_state = lower_bound_value(jax.nn.gelu(normalized_values(dilated_output, hidden_gain_term, hidden_bias_term)))
        branch = jnp.einsum('gtc,cd->gtd', upper_hidden_state, project, precision=lax.Precision.HIGHEST)
        return pooled + branch
    result, pull = jax.vjp(forward, signal.astype(jnp.float32), conv_wide.astype(jnp.float32), dilated_kernel_taps.astype(jnp.float32), pointwise.astype(jnp.float32), gain_in, shift_in, gain_mid, shift_mid, hidden_norm_gain, hidden_norm_bias)
    grads = pull(cotangent.astype(jnp.float32))
    return (result.astype(jnp.bfloat16), grads[0], grads[1], grads[2], grads[3], grads[4], grads[5], grads[6], grads[7], grads[8], grads[9])
```

```python
import functools

import jax
import jax.numpy as jnp
from jax import lax
from jax.experimental import pallas as pl
from jax.experimental.pallas import tpu as pltpu
from jax.sharding import PartitionSpec as P

DIL = 57
EPSILON = 1e-05
TAPS = 5
BF = jnp.bfloat16
F32 = jnp.float32
MESH = pl.DeviceIdType.MESH
K0 = 0.7978845608028654
K3 = 0.044715
ROWS = 8
VMEM_BYTES = 63 * 2**20


def gelu_up(x):
    t = jnp.tanh(x * (K0 + (K0 * K3) * (x * x)))
    h = 0.5 * x
    return h + h * t


def gelu_both(x):
    x2 = x * x
    t = jnp.tanh(x * (K0 + (K0 * K3) * x2))
    h = 0.5 * x
    return h + h * t, 0.5 + 0.5 * t + h * (1.0 - t * t) * (K0 + (3.0 * K0 * K3) * x2)


def dot(a, b, ca, cb):
    return lax.dot_general(a, b, (((ca,), (cb,)), ((), ())), preferred_element_type=F32)


def wide(mask, times):
    return jnp.concatenate([mask] * times, axis=1)


def al(x, n):
    return pl.multiple_of(x, n)


class Place:
    def __init__(self, nb, nm, na):
        self.nb, self.nm, self.na = nb, nm, na
        self.b = lax.axis_index("bins")
        self.m = lax.axis_index("mp")
        self.a = lax.axis_index("batch")
        self.layer = nm * na
        self.q = self.m * na + self.a

    def in_layer(self, q):
        return (self.b, q // self.na, lax.rem(q, self.na))

    def in_bins(self, b):
        return (b, self.m, self.a)

    @property
    def partner(self):
        return (self.b, 1 - self.m, self.a)

    def others(self, me, n):
        return [lax.rem(me + i, n) for i in range(1, n)]


def remote(src, dst, ss, rs, dev):
    return pltpu.make_async_remote_copy(
        src_ref=src, dst_ref=dst, send_sem=ss, recv_sem=rs, device_id=dev, device_id_type=MESH
    )


class Exchange:
    def __init__(self, buf, me, n, dev_of, ss, rs, others):
        self.buf, self.me, self.n, self.dev_of, self.ss, self.rs, self.others = (
            buf, me, n, dev_of, ss, rs, others,
        )

    def start(self, value):
        self.buf[self.me] = value
        for q in self.others:
            remote(self.buf.at[self.me], self.buf.at[self.me], self.ss.at[q], self.rs.at[self.me], self.dev_of(q)).start()

    def wait(self):
        for q in self.others:
            remote(self.buf.at[q], self.buf.at[q], self.ss.at[q], self.rs.at[q], self.dev_of(q)).wait_recv()
        return [self.buf[i] for i in range(self.n)]

    def drain(self):
        for q in self.others:
            remote(self.buf.at[self.me], self.buf.at[self.me], self.ss.at[q], self.rs.at[q], self.dev_of(q)).wait_send()


def merged(parts, count):
    means = [p[0:1] for p in parts]
    total = functools.reduce(jnp.add, means)
    mean = total / len(parts)
    squares = functools.reduce(jnp.add, [p[1:2] for p in parts])
    apart = functools.reduce(jnp.add, [(x - mean) * (x - mean) for x in means])
    return mean, squares + count * apart


def row_sum(x):
    return jnp.sum(x, axis=0, keepdims=True)


def greet(place):
    barrier = pltpu.get_barrier_semaphore()
    devices = [place.in_layer(q) for q in place.others(place.q, place.layer)]
    devices += [place.in_bins(b) for b in place.others(place.b, place.nb)]
    for d in devices:
        pl.semaphore_signal(barrier, inc=1, device_id=d, device_id_type=MESH)
    pl.semaphore_wait(barrier, len(devices))


def k1_body(dims, names, *refs):
    nb, nm, na, T, S, CH, HC = dims
    C = 2 * CH
    HR = T * ROWS
    PR = S * ROWS
    r = dict(zip(names, refs, strict=True))
    place = Place(nb, nm, na)
    b, m = place.b, place.m
    other = 1 - m
    total_in = float(HR * nb * nm * na)
    total_mid = float(PR * nb * nm * na)
    rim = (DIL + 1) * ROWS
    RT = r["XFC"].shape[0]

    sig, cot = r["sig"], r["cot"]
    lsem, csem_s, csem_r = r["lsem"], r["csem_s"], r["csem_r"]

    def local(src, dst, i):
        return pltpu.make_async_copy(src, dst, lsem.at[i])

    ld_sto = local(sig.at[pl.ds(al(other * HR, HR), HR)], r["STO"], 0)
    ld_raw = local(sig.at[pl.ds(al(m * HR, HR), HR)], r["RAW"].at[pl.ds(al(m * HR, HR), HR)], 1)
    ld_par = local(r["par"], r["PAR"].at[m], 2)
    ld_segw = local(r["segw"], r["SEGW"], 3)
    ld_w = local(r["wide"], r["W"].at[:, :, pl.ds(al(m * CH, CH), CH)], 4)
    ld_d = local(r["taps"], r["D2"].at[m], 5)
    ld_pw = local(r["pw"], r["PW"].at[:, pl.ds(al(m * CH, CH), CH)], 6)
    ld_cot = local(cot.at[pl.ds(al(m * PR, PR), PR)], r["COTR"].at[m], 7)
    ld_segp = local(r["segp"], r["SEGP"], 8)
    loads = [ld_sto, ld_raw, ld_par, ld_segw, ld_w, ld_d, ld_pw, ld_cot, ld_segp]
    for c in loads:
        c.start()
    greet(place)

    def cross(src, dst, i):
        return remote(src, dst, csem_s.at[i], csem_r.at[i], place.partner)

    x_sig = cross(sig.at[pl.ds(al(other * HR, HR), HR)], r["RAW"].at[pl.ds(al(m * HR, HR), HR)], 0)
    x_par = cross(r["par"], r["PAR"].at[m], 1)
    x_w = cross(r["wide"], r["W"].at[:, :, pl.ds(al(m * CH, CH), CH)], 2)
    x_d = cross(r["taps"], r["D2"].at[m], 3)
    x_pw = cross(r["pw"], r["PW"].at[:, pl.ds(al(m * CH, CH), CH)], 4)
    x_cot = cross(cot.at[pl.ds(al(other * PR, PR), PR)], r["COTR"].at[m], 5)
    crosses = [x_sig, x_par, x_w, x_d, x_pw, x_cot]
    for c in crosses:
        c.start()

    def exchange(i, name):
        return (
            Exchange(r[name + "A"], place.q, place.layer, place.in_layer, r["as_"].at[i], r["ar_"].at[i], place.others(place.q, place.layer)),
            Exchange(r[name + "B"], b, nb, place.in_bins, r["bs_"].at[i], r["br_"].at[i], place.others(b, nb)),
        )

    def finish_stats(ex, count):
        la = ex[0].wait()
        mean, squares = merged(la, count)
        ex[1].start(jnp.concatenate([mean, squares], axis=0))
        lb = ex[1].wait()
        return merged(lb, count * place.layer)

    def finish_sums(ex):
        v = functools.reduce(jnp.add, ex[0].wait())
        ex[1].start(v)
        v = functools.reduce(jnp.add, ex[1].wait())
        return v[0:1], v[1:2]

    ex_in, ex_mid, ex_hid, ex_bh, ex_bm = [
        exchange(i, n) for i, n in enumerate(["XI", "XM", "XH", "XG", "XD"])
    ]

    RAW, STO, X, XFC = r["RAW"], r["STO"], r["X"], r["XFC"]
    ld_sto.wait()
    ld_raw.wait()
    CHK = 128

    def own_raw(i):
        return RAW[pl.ds(al(m * HR + i * CHK, CHK), CHK), :].astype(F32).reshape(CHK // 8, 8, CH)

    def sto(i):
        return STO[pl.ds(al(i * CHK, CHK), CHK), :].astype(F32).reshape(CHK // 8, 8, CH)

    def s1(i, acc):
        return acc + jnp.sum(own_raw(i), axis=0) + jnp.sum(sto(i), axis=0)

    acc = lax.fori_loop(0, HR // CHK, s1, jnp.zeros((8, CH), F32))
    mean = row_sum(acc) / float(2 * HR)

    def s2(i, acc):
        u = own_raw(i) - mean
        v = sto(i) - mean
        return acc + jnp.sum(u * u, axis=0) + jnp.sum(v * v, axis=0)

    acc = lax.fori_loop(0, HR // CHK, s2, jnp.zeros((8, CH), F32))
    ex_in[0].start(jnp.concatenate([mean, row_sum(acc)], axis=0))

    ld_segw.wait()
    SEGW, MASK = r["SEGW"], r["MASK"]

    def make_masks(i, _):
        mid = SEGW[pl.ds(al(i * 128 + 16, 16), 128), :]
        for j, o in enumerate((-2, -1, 1, 2)):
            off = SEGW[pl.ds(al(i * 128 + 16 + o * 8, 8), 128), :]
            MASK[j, pl.ds(al(i * 128, 128), 128), :] = jnp.where(off == mid, 1.0, 0.0).astype(BF)
        return 0

    lax.fori_loop(0, HR // 128, make_masks, 0)
    x_sig.wait_recv()
    BB = RT // ROWS

    def turn(src, stride, dst, i):
        LANES = r["LANES"]
        for h in range(2):
            for row in range(ROWS):
                v = src(h, row * stride + i * BB).astype(F32)
                for j in range(CH // 128):
                    LANES[pl.ds((h * (CH // 128) + j) * RT + row, BB, stride=ROWS), :] = v[:, j * 128 : (j + 1) * 128]
        for j in range(C // 128):
            dst[pl.ds(al(i * RT, RT), RT), j * 128 : (j + 1) * 128] = LANES[j * RT : (j + 1) * RT, :].astype(BF)

    def turn_x(i, _):
        turn(lambda h, at: RAW[pl.ds(al(h * HR + at, BB), BB), :], T, X, i)
        return 0

    lax.fori_loop(0, T // BB, turn_x, 0)
    for c in (ld_par,):
        c.wait()
    x_par.wait_recv()
    PAR = r["PAR"]

    def vec(i):
        return jnp.concatenate([PAR[0, i : i + 1, :], PAR[1, i : i + 1, :]], axis=1)

    def hvec(i):
        return PAR[0, i : i + 1, :] + PAR[1, i : i + 1, :]

    la = ex_in[0].wait()
    n_own = float(2 * HR)
    lo = merged(la[0:na], n_own)
    hi = merged(la[na : 2 * na], n_own)
    ex_in[1].start(
        jnp.concatenate([jnp.concatenate([lo[0], hi[0]], axis=1), jnp.concatenate([lo[1], hi[1]], axis=1)], axis=0)
    )
    mu_in, sq = merged(ex_in[1].wait(), n_own * na)
    inv_in = lax.rsqrt(sq / total_in + EPSILON)
    gain_in, shift_in = vec(0), vec(1)
    scale_in = gain_in * inv_in
    ST = r["ST"]
    ST[0:1] = mu_in
    ST[1:2] = inv_in
    ST[2:3] = gain_in
    ST[3:4] = shift_in
    H0, H1 = r["H0"], r["H1"]
    HB = 256

    def make_hidden(i, last):
        at = al(i * HB, HB)
        pre = (X[pl.ds(at, HB), :].astype(F32) - mu_in) * scale_in + shift_in
        h = gelu_up(pre)
        H0[pl.ds(at + 16, HB), :] = h.astype(BF)
        H1[pl.ds(at, HB), :] = jnp.concatenate([last, h[: HB - 8]], axis=0).astype(BF)
        return h[HB - 8 :]

    lax.fori_loop(0, HR // HB, make_hidden, jnp.zeros((8, C), F32))
    hs, hr = r["hs"], r["hr"]
    down = (jnp.maximum(b - 1, 0), m, place.a)
    up = (jnp.minimum(b + 1, nb - 1), m, place.a)
    has_down, has_up = b > 0, b < nb - 1
    h_down = remote(H0.at[pl.ds(16, 16)], H0.at[pl.ds(HR + 16, 16)], hs.at[0], hr.at[0], down)
    h_up = remote(H0.at[pl.ds(HR, 16)], H0.at[pl.ds(0, 16)], hs.at[1], hr.at[1], up)

    @pl.when(has_down)
    def _():
        h_down.start()

    @pl.when(has_up)
    def _():
        h_up.start()

    @pl.when(jnp.logical_not(has_down))
    def _():
        H0[0:16, :] = jnp.zeros((16, C), BF)

    @pl.when(jnp.logical_not(has_up))
    def _():
        H0[pl.ds(HR + 16, 16), :] = jnp.zeros((16, C), BF)

    ld_w.wait()
    x_w.wait_recv()
    W, POOL, DIFF, SUM = r["W"], r["POOL"], r["DIFF"], r["SUM"]
    SUM[...] = jnp.zeros_like(SUM)

    def conv_tile(i):
        at = al(i * RT, RT)
        acc = None
        for k in range(TAPS):
            o = k - 2
            if o % 2 == 0:
                h = H0[pl.ds(al(at + (o + 2) * 8, 16), RT), :]
            else:
                h = H1[pl.ds(al(at + (o + 1) * 8, 16), RT), :]
            if o != 0:
                h = h * wide(MASK[k if k < 2 else k - 1, pl.ds(at, RT), :], C // 128)
            d = dot(h, W[k], 1, 0)
            acc = d if acc is None else acc + d
        XFC[...] = acc

        def pool(j, s):
            v = XFC[pl.ds(al(j * 128, 128), 128), :].reshape(8, 2, 8, C)
            c0, c1 = v[:, 0], v[:, 1]
            d = c0 - c1
            p = jnp.maximum(c0, c1) + jnp.log(1.0 + jnp.exp(-jnp.abs(d)))
            to = pl.ds(al(i * (RT // 2) + j * 64, 64), 64)
            POOL[to, :] = p.reshape(64, C)
            DIFF[to, :] = d.reshape(64, C)
            return s + jnp.sum(p, axis=0)

        SUM[...] += lax.fori_loop(0, RT // 128, pool, jnp.zeros((8, C), F32))

    NT = HR // RT

    def conv_loop(i, _):
        conv_tile(i)
        return 0

    lax.fori_loop(1, NT - 1, conv_loop, 0)

    @pl.when(has_up)
    def _():
        h_down.wait_recv()

    @pl.when(has_down)
    def _():
        h_up.wait_recv()

    first = H0[0:32, :].astype(F32)
    H1[0:16, :] = first[8:24].astype(BF)
    final = H0[pl.ds(HR, 32), :].astype(F32)
    H1[pl.ds(HR, 16), :] = final[8:24].astype(BF)
    lax.fori_loop(0, 2, lambda i, _: (conv_tile(i * (NT - 1)), 0)[1], 0)
    out_h = local(H0, r["oH"], 9)
    out_h.start()
    out_w = local(W, r["oW"], 10)
    out_w.start()
    out_x = local(X, r["oX"], 11)
    out_x.start()
    out_m = local(MASK, r["oM"], 12)
    out_m.start()
    out_st = local(ST, r["oST"], 13)
    out_st.start()

    mean = row_sum(SUM[...]) / float(PR)

    def m2_mid(i, acc):
        v = POOL[pl.ds(al(i * 128, 128), 128), :].reshape(16, 8, C) - mean
        return acc + jnp.sum(v * v, axis=0)

    acc = lax.fori_loop(0, PR // 128, m2_mid, jnp.zeros((8, C), F32))
    ex_mid[0].start(jnp.concatenate([mean, row_sum(acc)], axis=0))

    ld_cot.wait()
    x_cot.wait_recv()
    COTR, CT, GT, PW = r["COTR"], r["CT"], r["GT"], r["PW"]

    def turn_ct(i, _):
        turn(lambda h, at: COTR[h, pl.ds(al(at, BB), BB), :], S, CT, i)
        return 0

    lax.fori_loop(0, S // BB, turn_ct, 0)
    ld_pw.wait()
    x_pw.wait_recv()
    GT[...] = dot(CT[...], PW[...], 1, 1)
    ld_d.wait()
    x_d.wait_recv()
    D2, D = r["D2"], r["D"]
    for k in range(3):
        D[k] = jnp.concatenate([D2[0, k].astype(F32), D2[1, k].astype(F32)], axis=1).astype(BF)

    mu_mid, sq = finish_stats(ex_mid, float(PR))
    inv_mid = lax.rsqrt(sq / total_mid + EPSILON)
    gain_mid, shift_mid = vec(2), vec(3)
    scale_mid = gain_mid * inv_mid
    HM = r["HM"]

    def make_mid(i, _):
        at = pl.ds(al(i * 128, 128), 128)
        HM[at, :] = gelu_up((POOL[at, :] - mu_mid) * scale_mid + shift_mid).astype(BF)
        return 0

    lax.fori_loop(0, PR // 128, make_mid, 0)

    E0, E1, DO = r["E0"], r["E1"], r["DO"]
    RS, RR = r["RS"], r["RR"]
    prod = dot(HM[PR - rim :, :], D[0], 1, 0)
    RS[0] = prod.astype(BF)
    p_up = remote(RS.at[0], RR.at[0], hs.at[2], hr.at[2], up)

    @pl.when(has_up)
    def _():
        p_up.start()

    E0[PR : PR + rim, :] = prod
    prod = dot(HM[0:rim, :], D[2], 1, 0)
    RS[1] = prod.astype(BF)
    p_down = remote(RS.at[1], RR.at[1], hs.at[3], hr.at[3], down)

    @pl.when(has_down)
    def _():
        p_down.start()

    E1[0:rim, :] = prod
    E0[rim:PR, :] = dot(HM[0 : PR - rim, :], D[0], 1, 0)
    E1[rim:PR, :] = dot(HM[rim:, :], D[2], 1, 0)
    DO[...] = dot(HM[...], D[1], 1, 0)
    ld_segp.wait()
    SEGP = r["SEGP"]

    @pl.when(has_down)
    def _():
        p_up.wait_recv()
        E0[0:rim, :] = RR[0].astype(F32)

    @pl.when(jnp.logical_not(has_down))
    def _():
        E0[0:rim, :] = jnp.zeros((rim, HC), F32)

    @pl.when(has_up)
    def _():
        p_down.wait_recv()
        E1[PR : PR + rim, :] = RR[1].astype(F32)

    @pl.when(jnp.logical_not(has_up))
    def _():
        E1[PR : PR + rim, :] = jnp.zeros((rim, HC), F32)

    def same(i, n, by):
        here = SEGP[pl.ds(al(i * n + DIL * 8, 8), n), :]
        there = SEGP[pl.ds(al(i * n + (DIL + by) * 8, 8), n), :]
        return wide(jnp.where(here == there, 1.0, 0.0), HC // 128)

    def add_dil(i, s):
        at = pl.ds(al(i * 128, 128), 128)
        v = DO[at, :]
        v += same(i, 128, -DIL) * E0[pl.ds(al(i * 128 + 8, 8), 128), :]
        v += same(i, 128, DIL) * E1[pl.ds(al(i * 128 + DIL * 8, 8), 128), :]
        DO[at, :] = v
        return s + jnp.sum(v.reshape(16, 8, HC), axis=0)

    acc = lax.fori_loop(0, PR // 128, add_dil, jnp.zeros((8, HC), F32))
    mean = row_sum(acc) / float(PR)

    def m2_hid(i, acc):
        v = DO[pl.ds(al(i * 128, 128), 128), :].reshape(16, 8, HC) - mean
        return acc + jnp.sum(v * v, axis=0)

    acc = lax.fori_loop(0, PR // 128, m2_hid, jnp.zeros((8, HC), F32))
    ex_hid[0].start(jnp.concatenate([mean, row_sum(acc)], axis=0))
    mu_hid, sq = finish_stats(ex_hid, float(PR))
    inv_hid = lax.rsqrt(sq / total_mid + EPSILON)
    gain_hid, shift_hid = hvec(4), hvec(5)
    HT = r["HT"]

    def make_top(i, s):
        at = pl.ds(al(i * 128, 128), 128)
        xhat = (DO[at, :] - mu_hid) * inv_hid
        h, slope = gelu_both(xhat * gain_hid + shift_hid)
        HT[at, :] = h.astype(BF)
        da = slope * GT[at, :]
        GT[at, :] = da
        DO[at, :] = xhat
        return (
            s[0] + jnp.sum((da * xhat).reshape(16, 8, HC), axis=0),
            s[1] + jnp.sum(da.reshape(16, 8, HC), axis=0),
        )

    zero = jnp.zeros((8, HC), F32)
    sg, sb = lax.fori_loop(0, PR // 128, make_top, (zero, zero))
    ex_bh[0].start(jnp.concatenate([row_sum(sg), row_sum(sb)], axis=0))

    OB = 256

    def make_out(i, _):
        at = pl.ds(al(i * OB, OB), OB)
        v = (POOL[at, :] + dot(HT[at, :], PW[...], 1, 0)).astype(BF)
        COTR[0, at, :] = v[:, :CH]
        COTR[1, at, :] = v[:, CH:]
        return 0

    lax.fori_loop(0, PR // OB, make_out, 0)
    o_own = local(COTR.at[m], r["oOUT"].at[m], 14)
    o_own.start()
    o_cross = cross(COTR.at[other], r["oOUT"].at[m], 6)
    o_cross.start()
    gp = dot(HT[...], CT[...], 0, 0).astype(BF)
    RAW[3 * C : 3 * C + HC, :] = gp[:, :CH]
    RAW[3 * C + HC : 3 * C + 2 * HC, :] = gp[:, CH:]

    gg, gb = finish_sums(ex_bh)
    SM = r["SM"]
    SM[0:1, 0:HC] = gg
    SM[1:2, 0:HC] = gb
    SM[0:2, HC:] = jnp.zeros((2, C - HC), F32)
    scale = gain_hid * inv_hid
    mb, mg = gb / total_mid, gg / total_mid

    def make_gd(i, _):
        at = pl.ds(al(i * 128, 128), 128)
        g = scale * (GT[at, :] - mb - DO[at, :] * mg)
        gbf = g.astype(BF)
        r["GD1"][at, :] = gbf
        E0[pl.ds(al(i * 128 + rim, 16), 128), :] = gbf.astype(F32)
        return 0

    lax.fori_loop(0, PR // 128, make_gd, 0)
    GD1, GD0, GD2 = r["GD1"], r["GD0"], r["GD2"]
    g_up = remote(GD1.at[pl.ds(PR - rim, rim)], RR.at[2], hs.at[4], hr.at[4], up)
    g_down = remote(GD1.at[pl.ds(0, rim)], RR.at[3], hs.at[5], hr.at[5], down)

    @pl.when(has_up)
    def _():
        g_up.start()

    @pl.when(has_down)
    def _():
        g_down.start()

    GM = r["GM"]
    GM[...] = dot(GD1[...], D[1], 1, 1)

    @pl.when(has_down)
    def _():
        g_up.wait_recv()
        E0[0:rim, :] = RR[2].astype(F32)

    @pl.when(jnp.logical_not(has_down))
    def _():
        E0[0:rim, :] = jnp.zeros((rim, HC), F32)

    @pl.when(has_up)
    def _():
        g_down.wait_recv()
        E0[PR + rim : PR + 2 * rim, :] = RR[3].astype(F32)

    @pl.when(jnp.logical_not(has_up))
    def _():
        E0[PR + rim : PR + 2 * rim, :] = jnp.zeros((rim, HC), F32)

    def mask_gd(i, _):
        at = pl.ds(al(i * 128, 128), 128)
        GD0[at, :] = (same(i, 128, DIL) * E0[pl.ds(al(i * 128 + rim + DIL * 8, 8), 128), :]).astype(BF)
        GD2[at, :] = (same(i, 128, -DIL) * E0[pl.ds(al(i * 128 + rim - DIL * 8, 8), 128), :]).astype(BF)
        return 0

    lax.fori_loop(0, PR // 128, mask_gd, 0)
    GM[...] += dot(GD0[...], D[0], 1, 1) + dot(GD2[...], D[2], 1, 1)

    def make_dmid(i, s):
        at = pl.ds(al(i * 64, 64), 64)
        xhat = (POOL[at, :] - mu_mid) * inv_mid
        _, slope = gelu_both(xhat * gain_mid + shift_mid)
        da = slope * GM[at, :]
        GM[at, :] = da
        return (
            s[0] + jnp.sum((da * xhat).reshape(8, 8, C), axis=0),
            s[1] + jnp.sum(da.reshape(8, 8, C), axis=0),
        )

    zero = jnp.zeros((8, C), F32)
    sg, sb = lax.fori_loop(0, PR // 64, make_dmid, (zero, zero))
    ex_bm[0].start(jnp.concatenate([row_sum(sg), row_sum(sb)], axis=0))
    for k, g in enumerate((GD0, GD1, GD2)):
        RAW[k * C : (k + 1) * C, :] = dot(HM[...], g[...], 0, 0).astype(BF)
    out_dp = local(RAW.at[pl.ds(0, 3 * C + 2 * HC)], r["oDP"], 15)
    out_dp.start()
    gg, gb = finish_sums(ex_bm)
    SM[2:3, :] = gg
    SM[3:4, :] = gb
    SM[4:8, :] = jnp.zeros((4, C), F32)
    mb, mg = gb / total_mid, gg / total_mid
    GC = H1

    def make_gc(i, _):
        at = pl.ds(al(i * 64, 64), 64)
        xhat = (POOL[at, :] - mu_mid) * inv_mid
        g = CT[at, :].astype(F32) + scale_mid * (GM[at, :] - mb - xhat * mg)
        d = DIFF[at, :]
        e = jnp.exp(-jnp.abs(d))
        big = 1.0 / (1.0 + e)
        small = e * big
        g0 = g * jnp.where(d >= 0, big, small)
        g1 = g * jnp.where(d >= 0, small, big)
        v = jnp.stack([g0.reshape(8, 8, C), g1.reshape(8, 8, C)], axis=1).reshape(128, C)
        GC[pl.ds(al(i * 128, 128), 128), :] = v.astype(BF)
        return 0

    lax.fori_loop(0, PR // 64, make_gc, 0)
    out_gc = local(GC.at[pl.ds(0, HR)], r["oGC"], 16)
    out_gc.start()
    out_sm = local(SM, r["oSM"], 17)
    out_sm.start()

    for c in (out_h, out_w, out_x, out_m, out_st, o_own, out_dp, out_gc, out_sm):
        c.wait()
    for c in crosses:
        c.wait_send()
    o_cross.wait()
    for e in (ex_in, ex_mid, ex_hid, ex_bh, ex_bm):
        e[0].drain()
        e[1].drain()

    @pl.when(has_up)
    def _():
        h_up.wait_send()
        p_up.wait_send()
        g_up.wait_send()

    @pl.when(has_down)
    def _():
        h_down.wait_send()
        p_down.wait_send()
        g_down.wait_send()


def call_k1(axes, sig, cot, wide_taps, taps, pw, par, segw, segp):
    nb, nm, na = axes
    CH = sig.shape[1]
    C = 2 * CH
    HC = pw.shape[0]
    HR = sig.shape[0] // 2
    PR = cot.shape[0] // 2
    T, S = HR // ROWS, PR // ROWS
    rim = (DIL + 1) * ROWS
    RT = 512
    NA = nm * na
    inputs = dict(sig=sig, cot=cot, wide=wide_taps, taps=taps, pw=pw, par=par, segw=segw, segp=segp)
    sd = jax.ShapeDtypeStruct
    outs = dict(
        oH=sd((HR + 32, C), BF),
        oGC=sd((HR, C), BF),
        oX=sd((HR, C), BF),
        oW=sd((TAPS, C, C), BF),
        oM=sd((4, HR, 128), BF),
        oST=sd((8, C), F32),
        oOUT=sd((2, PR, CH), BF),
        oDP=sd((3 * C + 2 * HC, CH), BF),
        oSM=sd((8, C), F32),
    )
    V = pltpu.VMEM
    DMA = pltpu.SemaphoreType.DMA
    scratch = dict(
        RAW=V((2 * HR, CH), BF),
        STO=V((HR, CH), BF),
        XFC=V((RT, C), F32),
        LANES=V((C // 128 * RT, 128), F32),
        X=V((HR, C), BF),
        H0=V((HR + 32, C), BF),
        H1=V((HR + 32, C), BF),
        MASK=V((4, HR, 128), BF),
        SEGW=V(segw.shape, F32),
        SEGP=V(segp.shape, F32),
        PAR=V((2, 8, CH), F32),
        ST=V((8, C), F32),
        SM=V((8, C), F32),
        SUM=V((8, C), F32),
        W=V((TAPS, C, C), BF),
        D2=V((2, 3, C, HC // 2), BF),
        D=V((3, C, HC), BF),
        PW=V((HC, C), BF),
        COTR=V((2, PR, CH), BF),
        CT=V((PR, C), BF),
        POOL=V((PR, C), F32),
        DIFF=V((PR, C), F32),
        GM=V((PR, C), F32),
        HM=V((PR, C), BF),
        E0=V((PR + 2 * rim, HC), F32),
        E1=V((PR + rim, HC), F32),
        DO=V((PR, HC), F32),
        GT=V((PR, HC), F32),
        HT=V((PR, HC), BF),
        GD0=V((PR, HC), BF),
        GD1=V((PR, HC), BF),
        GD2=V((PR, HC), BF),
        RS=V((2, rim, HC), BF),
        RR=V((4, rim, HC), BF),
        XIA=V((NA, 2, CH), F32), XIB=V((nb, 2, C), F32),
        XMA=V((NA, 2, C), F32), XMB=V((nb, 2, C), F32),
        XHA=V((NA, 2, HC), F32), XHB=V((nb, 2, HC), F32),
        XGA=V((NA, 2, HC), F32), XGB=V((nb, 2, HC), F32),
        XDA=V((NA, 2, C), F32), XDB=V((nb, 2, C), F32),
        lsem=DMA((18,)),
        csem_s=DMA((7,)), csem_r=DMA((7,)),
        as_=DMA((5, NA)), ar_=DMA((5, NA)),
        bs_=DMA((5, nb)), br_=DMA((5, nb)),
        hs=DMA((6,)), hr=DMA((6,)),
    )
    names = list(inputs) + list(outs) + list(scratch)
    anyspec = pl.BlockSpec(memory_space=pl.ANY)
    res = pl.pallas_call(
        functools.partial(k1_body, (nb, nm, na, T, S, CH, HC), names),
        out_shape=list(outs.values()),
        in_specs=[anyspec] * len(inputs),
        out_specs=[anyspec] * len(outs),
        scratch_shapes=list(scratch.values()),
        compiler_params=pltpu.CompilerParams(
            collective_id=0, has_side_effects=True, vmem_limit_bytes=VMEM_BYTES
        ),
        cost_estimate=pl.CostEstimate(flops=19_000_000_000, bytes_accessed=40_000_000, transcendentals=6_000_000),
        name="forward_and_back",
    )(*inputs.values())
    return dict(zip(outs, res, strict=True))


def prepare(axes, seg, vectors):
    nb, nm, na = axes
    length = seg.shape[1]
    T = length // nb
    S = T // 2
    b, m = lax.axis_index("bins"), lax.axis_index("mp")
    rows = lax.dynamic_slice_in_dim(seg, m * ROWS, ROWS, 0).astype(F32)
    pad = 2 * DIL + 2
    rows = jnp.pad(rows, ((0, 0), (pad, pad)), constant_values=-1.0)
    window = lax.dynamic_slice_in_dim(rows, b * T, T + 2 * pad, 1)
    near = window[:, pad - 2 : pad + T + 2]
    far = window[:, 2 : 2 + 2 * (S + 2 * DIL) : 2]

    def spread(x):
        return jnp.broadcast_to(x.T[:, :, None], (x.shape[1], ROWS, 128)).reshape(-1, 128)

    half = vectors[0].shape[0]
    hh = vectors[4].shape[0]
    wide_rows = [v.reshape(1, half) for v in vectors[:4]]
    hid_rows = [lax.dynamic_update_slice(jnp.zeros((1, 2 * hh), F32), v.reshape(1, hh), (0, m * hh)) for v in vectors[4:]]
    par = jnp.concatenate(wide_rows + hid_rows + [jnp.zeros((2, half), F32)], axis=0)
    return spread(near), spread(far), par


def k2_body(dims, names, *refs):
    nb, nm, na, T, S, CH, HC = dims
    C = 2 * CH
    HR = T * ROWS
    r = dict(zip(names, refs, strict=True))
    place = Place(nb, nm, na)
    b, m, a = place.b, place.m, place.a
    other = 1 - m
    total_in = float(HR * nb * nm * na)
    RT = r["XFC"].shape[0]
    lsem = r["lsem"]

    def local(src, dst, i):
        return pltpu.make_async_copy(src, dst, lsem.at[i])

    H0, GC0, GC1, X, W, MASK = r["H0"], r["GC0"], r["GC1"], r["X"], r["W"], r["MASK"]
    ld_h = local(r["oH"].at[pl.ds(16, HR)], H0, 0)
    ld_gc = local(r["oGC"], GC0.at[pl.ds(16, HR)], 1)
    ld_m = local(r["oM"], MASK, 2)
    ld_st = local(r["oST"], r["ST"], 3)
    ld_w = local(r["oW"], W, 4)
    ld_x = local(r["oX"], X, 5)
    R, PRV = r["R"], r["PRV"]
    NP = R.shape[0]
    PIECE = C
    ld_dp = [
        local(r["oDP"].at[pl.ds(al(j * C + m * CH, CH), CH)], R.at[TAPS + j // 2, pl.ds(j % 2 * CH, CH)], 6 + j)
        for j in range(4)
    ]
    for c in [ld_h, ld_gc, ld_m, ld_st, *ld_dp, ld_w, ld_x]:
        c.start()
    greet(place)
    down = (jnp.maximum(b - 1, 0), m, a)
    up = (jnp.minimum(b + 1, nb - 1), m, a)
    has_down, has_up = b > 0, b < nb - 1
    hs, hr = r["hs"], r["hr"]
    g_down = remote(r["oGC"].at[pl.ds(0, 16)], GC0.at[pl.ds(HR + 16, 16)], hs.at[0], hr.at[0], down)
    g_up = remote(r["oGC"].at[pl.ds(HR - 16, 16)], GC0.at[pl.ds(0, 16)], hs.at[1], hr.at[1], up)

    @pl.when(has_down)
    def _():
        g_down.start()

    @pl.when(has_up)
    def _():
        g_up.start()

    @pl.when(jnp.logical_not(has_down))
    def _():
        GC0[0:16, :] = jnp.zeros((16, C), BF)

    @pl.when(jnp.logical_not(has_up))
    def _():
        GC0[pl.ds(HR + 16, 16), :] = jnp.zeros((16, C), BF)

    ps, pr, zs, zr = r["ps"], r["pr"], r["zs"], r["zr"]
    XB, YB, ZB, PS, OWN, TAPF = r["XB"], r["YB"], r["ZB"], r["PS"], r["OWN"], r["TAPF"]
    INNER = 4
    outer = nb // INNER
    inner = lax.rem(b, INNER)
    base = b - inner
    bits = (lax.rem(a, 2), a // 2)
    flip = (
        (b, m, a + 1 - 2 * bits[0]),
        (b, m, lax.rem(a + 2, 4)),
    )
    drains = []
    HALF, QUART, SMALL = PIECE // 2, PIECE // 4, PIECE // 16

    class Piece:
        def __init__(self, p):
            self.p = p
            self.first = p % 2
            b1, b2 = bits[self.first], bits[1 - self.first]
            self.n1, self.n2 = flip[self.first], flip[1 - self.first]
            self.k1 = al(b1 * HALF, HALF)
            self.s1 = al((1 - b1) * HALF, HALF)
            self.k2 = al(b1 * HALF + b2 * QUART, QUART)
            self.s2 = al(b1 * HALF + (1 - b2) * QUART, QUART)
            self.phase = 0

        def rows(self, at, n):
            return R.at[self.p, pl.ds(at, n)]

        def done(self, at, n):
            return PRV.at[self.p, pl.ds(at, n)]

        def send(self, src, dst, i, dev):
            c = remote(src, dst, ps.at[self.p, i], pr.at[self.p, i], dev)
            c.start()
            drains.append(c)
            self.cur = c

        def add(self, at, n, buf):
            sl = pl.ds(at, n)
            R[self.p, sl, :] = (R[self.p, sl, :].astype(F32) + buf.astype(F32)).astype(BF)

        def chunk(self, j):
            return al(self.k2 + j * SMALL, SMALL)

        def spread(self, which, make):
            self.zc = []
            for i in range(1, INNER):
                j = lax.rem(inner + i, INNER)
                src, dst = make(j)
                c = remote(src, dst, zs.at[self.p, which, j], zr.at[self.p, which, inner], (base + j, m, a))
                c.start()
                drains.append(c)
            self.which = which

        def gather_wait(self, make):
            for i in range(1, INNER):
                j = lax.rem(inner + i, INNER)
                ref = make(j)
                remote(ref, ref, zs.at[self.p, self.which, j], zr.at[self.p, self.which, j], (base + j, m, a)).wait_recv()

        def step(self):
            p, ph = self.p, self.phase
            self.phase += 1
            if ph == 0:
                self.cur.wait_recv()
                if p < TAPS:
                    R[p] = (OWN[p % 2] + PRV[p].astype(F32)).astype(BF)
                else:
                    R[p] = (R[p].astype(F32) + PRV[p].astype(F32)).astype(BF)
                self.send(self.rows(self.s1, HALF), XB.at[p], 1, self.n1)
            elif ph == 1:
                self.cur.wait_recv()
                self.add(self.k1, HALF, XB[p])
                self.send(self.rows(self.s2, QUART), YB.at[p], 2, self.n2)
            elif ph == 2:
                self.cur.wait_recv()
                self.add(self.k2, QUART, YB[p])
                self.spread(0, lambda j: (self.rows(self.chunk(j), SMALL), ZB.at[p, inner]))
            elif ph == 3:
                self.gather_wait(lambda j: ZB.at[p, j])
                at = self.chunk(inner)
                ZB[p, inner] = R[p, pl.ds(at, SMALL), :]
                v = ZB[p, 0].astype(F32)
                for j in range(1, INNER):
                    v += ZB[p, j].astype(F32)
                PRV[p, pl.ds(at, SMALL), :] = v.astype(BF)
                if outer > 1:
                    OB, osem_s, osem_r = r["OB"], r["os_"], r["or_"]
                    mine = b // INNER
                    OB[p, mine] = v.astype(BF)
                    for i in range(1, outer):
                        q = lax.rem(mine + i, outer)
                        c = remote(OB.at[p, mine], OB.at[p, mine], osem_s.at[p, q], osem_r.at[p, mine], (q * INNER + inner, m, a))
                        c.start()
                        drains.append(c)
                    for i in range(1, outer):
                        q = lax.rem(mine + i, outer)
                        remote(OB.at[p, q], OB.at[p, q], osem_s.at[p, q], osem_r.at[p, q], (q * INNER + inner, m, a)).wait_recv()
                    v = OB[p, 0].astype(F32)
                    for j in range(1, outer):
                        v += OB[p, j].astype(F32)
                    PRV[p, pl.ds(at, SMALL), :] = v.astype(BF)
                self.spread(1, lambda j: (self.done(at, SMALL), self.done(at, SMALL)))
            elif ph == 4:
                self.gather_wait(lambda j: self.done(self.chunk(j), SMALL))
                self.send(self.done(self.k2, QUART), self.done(self.k2, QUART), 3, self.n2)
            elif ph == 5:
                self.cur.wait_recv()
                self.send(self.done(self.k1, HALF), self.done(self.k1, HALF), 4, self.n1)
            elif ph == 6:
                self.cur.wait_recv()
                if p < TAPS:
                    c = local(PRV.at[p], r["oR"].at[ORDER[p]], 10 + p)
                    c.start()
                    self.outs = [c]
                else:
                    self.outs = []
                    for h in range(2):
                        j = (p - TAPS) * 2 + h
                        src = PRV.at[p, pl.ds(h * CH, CH)]
                        if j < 3:
                            c = local(src, r["oDK"].at[j, m], 10 + TAPS + j)
                            c2 = remote(src, r["oDK"].at[j, m], ps.at[p, 5 + h], pr.at[p, 5 + h], place.partner)
                            c2.start()
                            self.outs.append(c2)
                        else:
                            c = local(src, r["oPW"], 10 + TAPS + j)
                        c.start()
                        self.outs.append(c)

    ORDER = (2, 1, 3, 0, 4)
    pieces = [Piece(p) for p in range(NP)]
    for j in range(4):
        p = pieces[TAPS + j // 2]
    for p in pieces[TAPS:]:
        p.cur2 = []
        for h in range(2):
            j = (p.p - TAPS) * 2 + h
            c = remote(
                r["oDP"].at[pl.ds(al(j * C + other * CH, CH), CH)],
                PRV.at[p.p, pl.ds(h * CH, CH)],
                ps.at[p.p, 7 + h], pr.at[p.p, 7 + h], place.partner,
            )
            c.start()
            drains.append(c)
            p.cur2.append(c)

    class Both:
        def __init__(self, cs):
            self.cs = cs

        def wait_recv(self):
            for c in self.cs:
                c.wait_recv()

    for p in pieces[TAPS:]:
        p.cur = Both(p.cur2)

    def shifted(k, at, n):
        o = 2 - k
        if o % 2 == 0:
            g = GC0[pl.ds(al(at + (o + 2) * 8, 16), n), :]
        else:
            g = GC1[pl.ds(al(at + (o + 1) * 8, 16), n), :]
        if o != 0:
            j = {-2: 0, -1: 1, 1: 2, 2: 3}[o]
            g = g * wide(MASK[j, pl.ds(at, n), :], C // 128)
        return g

    def tap(i):
        k = ORDER[i]
        TAPF[...] = dot(H0[...], shifted(k, 0, HR), 0, 0)
        OWN[i % 2] = TAPF[:, pl.ds(al(m * CH, CH), CH)]
        PS[i] = TAPF[:, pl.ds(al(other * CH, CH), CH)].astype(BF)
        pieces[i].send(PS.at[i], PRV.at[i], 0, place.partner)

    ld_h.wait()
    ld_gc.wait()
    tap(0)
    for c in ld_dp:
        c.wait()
    pieces[5].step()
    pieces[6].step()

    @pl.when(has_up)
    def _():
        g_down.wait_recv()

    @pl.when(has_down)
    def _():
        g_up.wait_recv()

    GB = 256

    def make_gc1(i, _):
        v = GC0[pl.ds(al(i * GB, GB), GB + 16), :].astype(F32)
        GC1[pl.ds(al(i * GB, GB), GB), :] = v[8 : GB + 8].astype(BF)
        return 0

    lax.fori_loop(0, HR // GB, make_gc1, 0)
    v = GC0[pl.ds(HR, 32), :].astype(F32)
    GC1[pl.ds(HR, 16), :] = v[8:24].astype(BF)
    ld_m.wait()
    tap(1)
    pieces[0].step()
    tap(2)
    pieces[1].step()
    pieces[5].step()
    pieces[6].step()
    tap(3)
    pieces[2].step()
    pieces[0].step()
    tap(4)
    pieces[3].step()
    pieces[1].step()
    pieces[5].step()
    pieces[6].step()

    ld_w.wait()
    ld_x.wait()
    ld_st.wait()
    XFC, DA, ST = r["XFC"], r["DA"], r["ST"]
    mu, inv, gain, shift = ST[0:1], ST[1:2], ST[2:3], ST[3:4]

    def tile(i, s):
        at = al(i * RT, RT)
        acc = None
        for k in range(TAPS):
            d = dot(shifted(k, at, RT), W[k], 1, 1)
            acc = d if acc is None else acc + d
        XFC[...] = acc

        def back(j, s):
            to = pl.ds(al(i * RT + j * 64, 64), 64)
            xhat = (X[to, :].astype(F32) - mu) * inv
            _, slope = gelu_both(xhat * gain + shift)
            da = slope * XFC[pl.ds(al(j * 64, 64), 64), :]
            DA[0, to, :] = da[:, :CH].astype(BF)
            DA[1, to, :] = da[:, CH:].astype(BF)
            return (
                s[0] + jnp.sum((da * xhat).reshape(8, 8, C), axis=0),
                s[1] + jnp.sum(da.reshape(8, 8, C), axis=0),
            )

        return lax.fori_loop(0, RT // 64, back, s)

    zero = jnp.zeros((8, C), F32)
    s = (zero, zero)
    NT = HR // RT
    pumps = [[4, 2, 0], [3, 1, 5, 6], [4, 2, 0], [3, 1, 5, 6]]
    for i in range(NT):
        s = tile(i, s)
        for p in pumps[i % len(pumps)]:
            pieces[p].step()
    ex = (
        Exchange(r["XSA"], place.q, place.layer, place.in_layer, r["as_"], r["ar_"], place.others(place.q, place.layer)),
        Exchange(r["XSB"], b, nb, place.in_bins, r["bs_"], r["br_"], place.others(b, nb)),
    )
    ex[0].start(jnp.concatenate([row_sum(s[0]), row_sum(s[1])], axis=0))
    d_own = local(DA.at[m], r["oDA"].at[m], 18)
    d_own.start()
    d_cross = remote(DA.at[other], r["oDA"].at[m], hs.at[2], hr.at[2], place.partner)
    d_cross.start()
    v = functools.reduce(jnp.add, ex[0].wait())
    ex[1].start(v)
    for p in (4, 2, 0):
        pieces[p].step()
    v = functools.reduce(jnp.add, ex[1].wait())
    SM = r["SM"]
    SM[...] = jnp.zeros_like(SM)
    SM[0:2, :] = v
    o_sm = local(SM, r["oSM2"], 19)
    o_sm.start()
    while any(p.phase < 7 for p in pieces):
        low = min(p.phase for p in pieces)
        for p in (5, 6, 0, 1, 2, 3, 4):
            if pieces[p].phase == low:
                pieces[p].step()
    for p in pieces:
        for c in p.outs:
            c.wait()
    for c in drains:
        c.wait_send()
    for c in (d_own, o_sm):
        c.wait()
    d_cross.wait()
    ex[0].drain()
    ex[1].drain()

    @pl.when(has_up)
    def _():
        g_up.wait_send()

    @pl.when(has_down)
    def _():
        g_down.wait_send()


def call_k2(axes, k1, CH, HC):
    nb, nm, na = axes
    C = 2 * CH
    HR = k1["oGC"].shape[0]
    T = HR // ROWS
    RT = 512
    NA = nm * na
    names_in = ["oH", "oGC", "oX", "oW", "oM", "oST", "oDP"]
    sd = jax.ShapeDtypeStruct
    outs = dict(
        oDA=sd((2, HR, CH), BF),
        oR=sd((TAPS, C, CH), BF),
        oDK=sd((3, 2, CH, HC), BF),
        oPW=sd((HC, CH), BF),
        oSM2=sd((8, C), F32),
    )
    V = pltpu.VMEM
    DMA = pltpu.SemaphoreType.DMA
    NP = TAPS + 2
    outer = nb // 4
    scratch = dict(
        H0=V((HR, C), BF),
        GC0=V((HR + 32, C), BF),
        GC1=V((HR + 32, C), BF),
        X=V((HR, C), BF),
        W=V((TAPS, C, C), BF),
        MASK=V((4, HR, 128), BF),
        ST=V((8, C), F32),
        SM=V((8, C), F32),
        R=V((NP, C, CH), BF),
        PRV=V((NP, C, CH), BF),
        PS=V((TAPS, C, CH), BF),
        OWN=V((2, C, CH), F32),
        TAPF=V((C, C), F32),
        XB=V((NP, C // 2, CH), BF),
        YB=V((NP, C // 4, CH), BF),
        ZB=V((NP, 4, C // 16, CH), BF),
        XFC=V((RT, C), F32),
        DA=V((2, HR, CH), BF),
        XSA=V((NA, 2, C), F32), XSB=V((nb, 2, C), F32),
        lsem=DMA((20,)),
        ps=DMA((NP, 9)), pr=DMA((NP, 9)),
        zs=DMA((NP, 2, 4)), zr=DMA((NP, 2, 4)),
        as_=DMA((NA,)), ar_=DMA((NA,)),
        bs_=DMA((nb,)), br_=DMA((nb,)),
        hs=DMA((3,)), hr=DMA((3,)),
    )
    if outer > 1:
        scratch.update(OB=V((NP, outer, C // 16, CH), BF), os_=DMA((NP, outer)), or_=DMA((NP, outer)))
    names = names_in + list(outs) + list(scratch)
    anyspec = pl.BlockSpec(memory_space=pl.ANY)
    res = pl.pallas_call(
        functools.partial(k2_body, (nb, nm, na, T, T // 2, CH, HC), names),
        out_shape=list(outs.values()),
        in_specs=[anyspec] * len(names_in),
        out_specs=[anyspec] * len(outs),
        scratch_shapes=list(scratch.values()),
        compiler_params=pltpu.CompilerParams(
            collective_id=1, has_side_effects=True, vmem_limit_bytes=VMEM_BYTES
        ),
        cost_estimate=pl.CostEstimate(flops=25_000_000_000, bytes_accessed=40_000_000, transcendentals=2_000_000),
        name="weight_sums_and_input_gradient",
    )(*[k1[n] for n in names_in])
    return dict(zip(outs, res, strict=True))


def k3_body(dims, sig, da, out, rr, dk, pw, stats, gs_ref, out_ref, gw_ref, dk_ref, pw_ref, lanes, lanes2):
    CH, total_in = dims
    m = lax.axis_index("mp")
    n = da.shape[1]
    BB = n // ROWS
    v = da[0].astype(F32)
    u = out[0].astype(F32)
    n2 = out.shape[1]
    B2 = n2 // ROWS
    for j in range(CH // 128):
        lanes[j * n : (j + 1) * n, :] = v[:, j * 128 : (j + 1) * 128]
        lanes2[j * n2 : (j + 1) * n2, :] = u[:, j * 128 : (j + 1) * 128]
    st = stats[...]
    mu, inv, gain, gg, gb = st[0:1], st[1:2], st[2:3], st[4:5], st[5:6]
    scale = gain * inv
    mg, mb = gg / total_in, gb / total_in
    for row in range(ROWS):
        for j in range(CH // 128):
            c = slice(j * 128, (j + 1) * 128)
            d = lanes[pl.ds(j * n + row, BB, stride=ROWS), :]
            xhat = (sig[row, :, c].astype(F32) - mu[:, c]) * inv[:, c]
            gs_ref[row, :, c] = scale[:, c] * (d - mb[:, c] - xhat * mg[:, c])
            out_ref[row, :, c] = lanes2[pl.ds(j * n2 + row, B2, stride=ROWS), :].astype(BF)
    gw_ref[...] = rr[...].astype(F32)
    d = dk[...].astype(F32)
    hh = d.shape[1] // 2
    dk_ref[...] = jnp.where(m == 0, d[:, :hh], d[:, hh:])
    pw_ref[...] = pw[...].astype(F32)


def call_k3(axes, sig, k1, k2, stats):
    nb, nm, na = axes
    rows, T, CH = sig.shape
    S = T // 2
    HC = k2["oDK"].shape[3]
    C = 2 * CH
    NC = 4
    steps = 2 * NC
    sd = jax.ShapeDtypeStruct
    total_in = float(rows * T * nb * na)
    rr = k2["oR"].reshape(-1, CH)
    dk = k2["oDK"].reshape(-1, HC)
    pw = k2["oPW"]
    nr, nd, npw = rr.shape[0] // steps, dk.shape[0] // steps, pw.shape[0] // steps
    flat = lambda n, w: pl.BlockSpec((n, w), lambda h, c: (h * NC + c, 0))
    return pl.pallas_call(
        functools.partial(k3_body, (CH, total_in)),
        grid=(2, NC),
        out_shape=[
            sd((rows, T, CH), F32),
            sd((rows, S, CH), BF),
            sd(rr.shape, F32),
            sd((dk.shape[0], HC // 2), F32),
            sd(pw.shape, F32),
        ],
        in_specs=[
            pl.BlockSpec((ROWS, T // NC, CH), lambda h, c: (h, c, 0)),
            pl.BlockSpec((1, T * ROWS // NC, CH), lambda h, c: (h, c, 0)),
            pl.BlockSpec((1, S * ROWS // NC, CH), lambda h, c: (h, c, 0)),
            flat(nr, CH), flat(nd, HC), flat(npw, CH),
            pl.BlockSpec((8, CH), lambda h, c: (0, 0)),
        ],
        out_specs=[
            pl.BlockSpec((ROWS, T // NC, CH), lambda h, c: (h, c, 0)),
            pl.BlockSpec((ROWS, S // NC, CH), lambda h, c: (h, c, 0)),
            flat(nr, CH), flat(nd, HC // 2), flat(npw, CH),
        ],
        scratch_shapes=[
            pltpu.VMEM((CH // 128 * T * ROWS // NC, 128), F32),
            pltpu.VMEM((CH // 128 * S * ROWS // NC, 128), F32),
        ],
        compiler_params=pltpu.CompilerParams(vmem_limit_bytes=40 * 2**20),
        name="last_pass",
    )(sig, k2["oDA"], k1["oOUT"], rr, dk, pw, stats)


def local(axes, signal, seg, cotangent, conv_wide, taps, pointwise, *vectors):
    CH = signal.shape[2]
    HC = pointwise.shape[0]
    m = lax.axis_index("mp")
    segw, segp, par = prepare(axes, seg, vectors)
    o1 = call_k1(
        axes, signal.reshape(-1, CH), cotangent.reshape(-1, CH), conv_wide, taps, pointwise, par, segw, segp
    )
    o2 = call_k2(axes, o1, CH, HC)
    mine = lambda x, n: lax.dynamic_slice_in_dim(x, m * n, n, 1)
    stats = mine(jnp.concatenate([o1["oST"][0:4], o2["oSM2"][0:4]], axis=0), CH)
    gs, out, gw, dk, pw = call_k3(axes, signal, o1, o2, stats)
    sm = mine(o1["oSM"], CH)
    hid = lax.dynamic_slice_in_dim(o1["oSM"], m * (HC // 2), HC // 2, 1)
    return (
        out,
        gs,
        gw.reshape(conv_wide.shape),
        dk.reshape(taps.shape),
        pw,
        stats[4], stats[5],
        sm[2], sm[3],
        hid[0], hid[1],
    )


def solution(mesh):
    axes = (mesh.shape["bins"], mesh.shape["mp"], mesh.shape["batch"])
    cut = P("batch", "bins", "mp")
    tap = P(None, None, "mp")
    return jax.shard_map(
        functools.partial(local, axes),
        mesh=mesh,
        in_specs=(cut, P("batch", None), cut, tap, tap, P(None, "mp")) + (P("mp"),) * 6,
        out_specs=(cut, cut, tap, tap, P(None, "mp")) + (P("mp"),) * 6,
        check_vma=False,
    )
```

```python
import functools

import jax
import jax.numpy as jnp
from jax import lax
from jax.experimental import pallas as pl
from jax.experimental.pallas import tpu as pltpu
from jax.sharding import PartitionSpec as P

DIL = 57
EPSILON = 1e-05
TAPS = 5
BF = jnp.bfloat16
F32 = jnp.float32
MESH = pl.DeviceIdType.MESH
K0 = 0.7978845608028654
K3 = 0.044715
ROWS = 8
VMEM_BYTES = 63 * 2**20


def gelu_up(x):
    t = jnp.tanh(x * (K0 + (K0 * K3) * (x * x)))
    h = 0.5 * x
    return h + h * t


def gelu_both(x):
    x2 = x * x
    t = jnp.tanh(x * (K0 + (K0 * K3) * x2))
    h = 0.5 * x
    return h + h * t, 0.5 + 0.5 * t + h * (1.0 - t * t) * (K0 + (3.0 * K0 * K3) * x2)


def dot(a, b, ca, cb):
    return lax.dot_general(a, b, (((ca,), (cb,)), ((), ())), preferred_element_type=F32)


def wide(mask, times):
    return jnp.concatenate([mask] * times, axis=1)


def al(x, n):
    return pl.multiple_of(x, n)


class Place:
    def __init__(self, nb, nm, na):
        self.nb, self.nm, self.na = nb, nm, na
        self.b = lax.axis_index("bins")
        self.m = lax.axis_index("mp")
        self.a = lax.axis_index("batch")
        self.layer = nm * na
        self.q = self.m * na + self.a

    def in_layer(self, q):
        return (self.b, q // self.na, lax.rem(q, self.na))

    def in_bins(self, b):
        return (b, self.m, self.a)

    @property
    def partner(self):
        return (self.b, 1 - self.m, self.a)

    def others(self, me, n):
        return [lax.rem(me + i, n) for i in range(1, n)]


def remote(src, dst, ss, rs, dev):
    return pltpu.make_async_remote_copy(
        src_ref=src, dst_ref=dst, send_sem=ss, recv_sem=rs, device_id=dev, device_id_type=MESH
    )


class Exchange:
    def __init__(self, buf, me, n, dev_of, ss, rs, others):
        self.buf, self.me, self.n, self.dev_of, self.ss, self.rs, self.others = (
            buf, me, n, dev_of, ss, rs, others,
        )

    def start(self, value):
        self.buf[self.me] = value
        for q in self.others:
            remote(self.buf.at[self.me], self.buf.at[self.me], self.ss.at[q], self.rs.at[self.me], self.dev_of(q)).start()

    def wait(self):
        for q in self.others:
            remote(self.buf.at[q], self.buf.at[q], self.ss.at[q], self.rs.at[q], self.dev_of(q)).wait_recv()
        return [self.buf[i] for i in range(self.n)]

    def drain(self):
        for q in self.others:
            remote(self.buf.at[self.me], self.buf.at[self.me], self.ss.at[q], self.rs.at[q], self.dev_of(q)).wait_send()


def merged(parts, count):
    means = [p[0:1] for p in parts]
    total = functools.reduce(jnp.add, means)
    mean = total / len(parts)
    squares = functools.reduce(jnp.add, [p[1:2] for p in parts])
    apart = functools.reduce(jnp.add, [(x - mean) * (x - mean) for x in means])
    return mean, squares + count * apart


class Marker:
    def __init__(self):
        self.scope = None

    def __call__(self, name=None):
        if self.scope is not None:
            self.scope.__exit__(None, None, None)
        self.scope = jax.named_scope(name) if name else None
        if name:
            self.scope.__enter__()


def row_sum(x):
    return jnp.sum(x, axis=0, keepdims=True)


def greet(place):
    barrier = pltpu.get_barrier_semaphore()
    devices = [place.in_layer(q) for q in place.others(place.q, place.layer)]
    devices += [place.in_bins(b) for b in place.others(place.b, place.nb)]
    for d in devices:
        pl.semaphore_signal(barrier, inc=1, device_id=d, device_id_type=MESH)
    pl.semaphore_wait(barrier, len(devices))


def main_body(dims, names, spans, *refs):
    nb, nm, na, T, S, CH, HC = dims
    C = 2 * CH
    HR = T * ROWS
    PR = S * ROWS
    rim = (DIL + 1) * ROWS
    r = dict(zip(names, refs, strict=True))
    place = Place(nb, nm, na)
    b, m, a = place.b, place.m, place.a
    other = 1 - m
    total_in = float(HR * nb * nm * na)
    total_mid = float(PR * nb * nm * na)
    LANES = r["LANES"]
    RT = LANES.shape[0] // (C // 128)
    mark = Marker()

    def part(name, at=0, n=None):
        pool, start, rows = spans[name]
        return r[pool].at[pl.ds(start + at, rows if n is None else n)]

    def local(src, dst, i):
        return pltpu.make_async_copy(src, dst, r["lsem"].at[i])

    def cross(src, dst, i):
        return remote(src, dst, r["csem_s"].at[i], r["csem_r"].at[i], place.partner)

    RAW, STO, X, CT, HM = part("RAW"), part("STO"), part("X"), part("CT"), part("HM")
    H0, H1, W, PW, DT = part("H0"), part("H1"), part("W"), part("PW"), part("DT")
    COT = [part("COTR", 0, PR), part("COTR", PR, PR)]
    PAR, SEG, SEGX, MASK, ST = r["PAR"], r["SEG"], r["SEGX"], r["MASK"], r["ST"]
    half = lambda at, n: pl.ds(al(at + m * n, n), n)

    mark("loads")
    sig, cot = r["sig"], r["cot"]
    mine, theirs = pl.ds(al(m * HR, HR), HR), pl.ds(al(other * HR, HR), HR)
    raw_mine = r["N"].at[pl.ds(al(spans["RAW"][1] + m * HR, 16), HR)]
    cot_mine = r["N"].at[pl.ds(al(spans["COTR"][1] + m * PR, 16), PR)]
    lanes = pl.ds(al(m * CH, CH), CH)
    w0, pw0, dt0 = spans["W"][1], spans["PW"][1], spans["DT"][1]
    HH = HC // 2

    def weight(k):
        return r["M"].at[pl.ds(w0 + k * C, C), lanes]

    def tap_rows(k):
        return r["M"].at[pl.ds(al(dt0 + k * HC + m * HH, 16), HH)]

    pw_mine = r["M"].at[pl.ds(pw0, HC), lanes]
    ld_sto = local(sig.at[theirs], STO, 0)
    ld_raw = local(sig.at[mine], raw_mine, 1)
    ld_seg = local(r["seg"], SEG, 2)
    ld_w = [local(r["wide"].at[k], weight(k), 3 + k) for k in range(TAPS)]
    ld_d = [local(r["taps"].at[k], tap_rows(k), 8 + k) for k in range(3)]
    ld_pw = local(r["pw"], pw_mine, 11)
    ld_cot = local(cot.at[pl.ds(al(m * PR, PR), PR)], cot_mine, 12)
    for c in [ld_sto, ld_raw, ld_seg, *ld_w, *ld_d, ld_pw, ld_cot]:
        c.start()
    for i in range(4):
        PAR[m, i : i + 1, :] = r[f"v{i}"][...].reshape(1, CH)
    for i in range(4, 6):
        PAR[m, i : i + 1, 0:HH] = r[f"v{i}"][...].reshape(1, HH)
    mark("greet")
    greet(place)
    x_sig = cross(sig.at[theirs], raw_mine, 0)
    x_par = cross(PAR.at[m], PAR.at[m], 1)
    x_w = [cross(r["wide"].at[k], weight(k), 2 + k) for k in range(TAPS)]
    x_d = [cross(r["taps"].at[k], tap_rows(k), 7 + k) for k in range(3)]
    x_pw = cross(r["pw"], pw_mine, 10)
    x_cot = cross(cot.at[pl.ds(al(other * PR, PR), PR)], cot_mine, 11)
    crosses = [x_sig, x_par, *x_w, x_cot, x_pw, *x_d]
    for c in crosses:
        c.start()

    def exchange(i, name):
        return (
            Exchange(r[name + "A"], place.q, place.layer, place.in_layer, r["as_"].at[i], r["ar_"].at[i], place.others(place.q, place.layer)),
            Exchange(r[name + "B"], b, nb, place.in_bins, r["bs_"].at[i], r["br_"].at[i], place.others(b, nb)),
        )

    def finish_stats(ex, count):
        mean, squares = merged(ex[0].wait(), count)
        ex[1].start(jnp.concatenate([mean, squares], axis=0))
        return merged(ex[1].wait(), count * place.layer)

    def finish_sums(ex, between=lambda: None):
        ex[1].start(functools.reduce(jnp.add, ex[0].wait()))
        between()
        mark("sum_wait")
        return functools.reduce(jnp.add, ex[1].wait())

    ex_in, ex_mid, ex_hid, ex_bh, ex_bm, ex_bi = exchanges = [
        exchange(i, n) for i, n in enumerate(["XI", "XM", "XH", "XG", "XD", "XS"])
    ]

    mark("signal_load")
    ld_sto.wait()
    ld_raw.wait()
    mark("signal_stats")
    CHK = 128
    raw_at = spans["RAW"][1] + m * HR

    def own_raw(i):
        return r["N"][pl.ds(al(raw_at + i * CHK, 16), CHK), :].astype(F32).reshape(CHK // 8, 8, CH)

    def sto(i):
        return STO[pl.ds(al(i * CHK, CHK), CHK), :].astype(F32).reshape(CHK // 8, 8, CH)

    def s1(i, acc):
        return acc + jnp.sum(own_raw(i), axis=0) + jnp.sum(sto(i), axis=0)

    acc = lax.fori_loop(0, HR // CHK, s1, jnp.zeros((8, CH), F32))
    mean = row_sum(acc) / float(2 * HR)

    def s2(i, acc):
        u = own_raw(i) - mean
        v = sto(i) - mean
        return acc + jnp.sum(u * u, axis=0) + jnp.sum(v * v, axis=0)

    acc = lax.fori_loop(0, HR // CHK, s2, jnp.zeros((8, CH), F32))
    ex_in[0].start(jnp.concatenate([mean, row_sum(acc)], axis=0))

    mark("segments")
    ld_seg.wait()
    blocks = SEG.shape[1] // 128

    def make_segs(i, _):
        at = b * (T // 128) - 1 + i
        v = SEG[pl.ds(al(m * ROWS, ROWS), ROWS), pl.ds(al(jnp.clip(at, 0, blocks - 1) * 128, 128), 128)].astype(F32)
        v = jnp.where(jnp.logical_and(at >= 0, at < blocks), v, -1.0)
        for j in range(128):
            SEGX[pl.ds(al(i * 1024 + j * 8, 8), 8), :] = jnp.broadcast_to(v[:, j : j + 1], (8, 128))
        return 0

    lax.fori_loop(0, T // 128 + 2, make_segs, 0)
    mark("masks")
    BIN0 = 128 * 8

    def make_masks(i, _):
        mid = SEGX[pl.ds(al(i * 128 + BIN0, 128), 128), :]
        for j, o in enumerate((-2, -1, 1, 2)):
            off = SEGX[pl.ds(al(i * 128 + BIN0 + o * 8, 8), 128), :]
            MASK[j, pl.ds(al(i * 128, 128), 128), :] = jnp.where(off == mid, 1.0, 0.0).astype(BF)
        return 0

    lax.fori_loop(0, HR // 128, make_masks, 0)
    mark("wait_signal")
    x_sig.wait_recv()
    mark("turn_signal")
    BB = RT // ROWS

    def turn(src, dst, i):
        for h in range(2):
            for row in range(ROWS):
                v = src(h, row).astype(F32)
                for j in range(CH // 128):
                    LANES[pl.ds((h * (CH // 128) + j) * RT + row, BB, stride=ROWS), :] = v[:, j * 128 : (j + 1) * 128]
        for j in range(C // 128):
            dst[pl.ds(al(i * RT, RT), RT), j * 128 : (j + 1) * 128] = LANES[j * RT : (j + 1) * RT, :].astype(BF)

    def turn_x(i, _):
        turn(lambda h, row: RAW[pl.ds(al(h * HR + row * T + i * BB, BB), BB), :], X, i)
        return 0

    lax.fori_loop(0, T // BB, turn_x, 0)
    keep_x = local(X, r["oX"], 13)
    keep_x.start()
    x_par.wait_recv()

    def vec(i):
        return jnp.concatenate([PAR[0, i : i + 1, :], PAR[1, i : i + 1, :]], axis=1)

    def hvec(i):
        return jnp.concatenate([PAR[0, i : i + 1, 0:HH], PAR[1, i : i + 1, 0:HH]], axis=1)

    mark("sum_in")
    la = ex_in[0].wait()
    n_own = float(2 * HR)
    lo = merged(la[0:na], n_own)
    hi = merged(la[na : 2 * na], n_own)
    ex_in[1].start(
        jnp.concatenate([jnp.concatenate([lo[0], hi[0]], axis=1), jnp.concatenate([lo[1], hi[1]], axis=1)], axis=0)
    )
    mu_in, sq = merged(ex_in[1].wait(), n_own * na)
    inv_in = lax.rsqrt(sq / total_in + EPSILON)
    gain_in, shift_in = vec(0), vec(1)
    scale_in = gain_in * inv_in
    ST[0:1, :] = mu_in
    ST[1:2, :] = inv_in
    ST[2:3, :] = gain_in
    mark("hidden_in")
    HB = 256

    def make_hidden(i, last):
        at = al(i * HB, HB)
        pre = (X[pl.ds(at, HB), :].astype(F32) - mu_in) * scale_in + shift_in
        h = gelu_up(pre)
        H0[pl.ds(al(at + 16, 16), HB), :] = h.astype(BF)
        H1[pl.ds(at, HB), :] = jnp.concatenate([last, h[: HB - 8]], axis=0).astype(BF)
        return h[HB - 8 :]

    lax.fori_loop(0, HR // HB, make_hidden, jnp.zeros((8, C), F32))
    hs, hr = r["hs"], r["hr"]
    down = (jnp.maximum(b - 1, 0), m, a)
    up = (jnp.minimum(b + 1, nb - 1), m, a)
    has_down, has_up = b > 0, b < nb - 1

    def when_down(f):
        pl.when(has_down)(f)

    def when_up(f):
        pl.when(has_up)(f)

    class Rims:
        def __init__(self, to_down, from_up, to_up, from_down, i):
            self.down = remote(to_down, from_up, hs.at[i], hr.at[i], down)
            self.up = remote(to_up, from_down, hs.at[i + 1], hr.at[i + 1], up)

        def start_down(self):
            when_down(self.down.start)

        def start_up(self):
            when_up(self.up.start)

        def wait_from_up(self):
            when_up(self.down.wait_recv)

        def wait_from_down(self):
            when_down(self.up.wait_recv)

        def drain(self):
            when_down(self.down.wait_send)
            when_up(self.up.wait_send)

    def clear_halo(ref):
        @pl.when(jnp.logical_not(has_down))
        def _():
            ref[0:16, :] = jnp.zeros((16, C), BF)

        @pl.when(jnp.logical_not(has_up))
        def _():
            ref[pl.ds(HR + 16, 16), :] = jnp.zeros((16, C), BF)

    def halos(ref, i):
        return Rims(ref.at[pl.ds(16, 16)], ref.at[pl.ds(HR + 16, 16)], ref.at[pl.ds(HR, 16)], ref.at[pl.ds(0, 16)], i)

    h_halo = halos(H0, 0)
    h_halo.start_down()
    h_halo.start_up()
    clear_halo(H0)

    def by_one_bin(even, odd):
        v = even[0:32, :].astype(F32)
        odd[0:16, :] = v[8:24].astype(BF)
        v = even[pl.ds(HR, 32), :].astype(F32)
        odd[pl.ds(HR, 16), :] = v[8:24].astype(BF)

    MJ = {-2: 0, -1: 1, 1: 2, 2: 3}

    def shifted(even, odd, o, at, n):
        if o % 2 == 0:
            v = even[pl.ds(al(at + (o + 2) * 8, 16), n), :]
        else:
            v = odd[pl.ds(al(at + (o + 1) * 8, 16), n), :]
        if o != 0:
            v = v * wide(MASK[MJ[o], pl.ds(al(at, 16), n), :], C // 128)
        return v

    def w(k):
        return W[k * C : (k + 1) * C, :]

    def put_lanes(v, n):
        for j in range(C // 128):
            LANES[j * RT : j * RT + n, :] = v[:, j * 128 : (j + 1) * 128]

    def get_lanes(at, n):
        return jnp.concatenate([LANES[pl.ds(al(j * RT + at, 8), n), :] for j in range(C // 128)], axis=1)

    mark("wait_weights")
    for c in (*ld_w,):
        c.wait()
    for c in x_w:
        c.wait_recv()
    POOL, DIFF, SUM = r["POOL"], r["DIFF"], r["SUM"]
    SUM[...] = jnp.zeros_like(SUM)

    def conv_tile(i):
        at = al(i * RT, RT)
        acc = None
        for k in range(TAPS):
            d = dot(shifted(H0, H1, k - 2, at, RT), w(k), 1, 0)
            acc = d if acc is None else acc + d
        put_lanes(acc, RT)

        def pool(j, s):
            v = get_lanes(j * 128, 128).reshape(8, 2, 8, C)
            c0, c1 = v[:, 0], v[:, 1]
            d = c0 - c1
            p = jnp.maximum(c0, c1) + jnp.log(1.0 + jnp.exp(-jnp.abs(d)))
            to = pl.ds(al(i * (RT // 2) + j * 64, 64), 64)
            POOL[to, :] = p.reshape(64, C)
            DIFF[to, :] = d.reshape(64, C)
            return s + jnp.sum(p, axis=0)

        SUM[...] += lax.fori_loop(0, RT // 128, pool, jnp.zeros((8, C), F32))

    NT = HR // RT

    def conv_loop(i, _):
        conv_tile(i)
        return 0

    mark("conv")
    lax.fori_loop(1, NT - 1, conv_loop, 0)
    h_halo.wait_from_up()
    h_halo.wait_from_down()
    by_one_bin(H0, H1)
    mark("conv_ends")
    lax.fori_loop(0, 2, lambda i, _: (conv_tile(i * (NT - 1)), 0)[1], 0)

    mark("mid_stats")
    mean = row_sum(SUM[...]) / float(PR)

    def m2_mid(i, acc):
        v = POOL[pl.ds(al(i * 128, 128), 128), :].reshape(16, 8, C) - mean
        return acc + jnp.sum(v * v, axis=0)

    acc = lax.fori_loop(0, PR // 128, m2_mid, jnp.zeros((8, C), F32))
    ex_mid[0].start(jnp.concatenate([mean, row_sum(acc)], axis=0))

    mark("turn_cotangent")
    ld_cot.wait()
    x_cot.wait_recv()

    def turn_ct(i, _):
        turn(lambda h, row: COT[h][pl.ds(al(row * S + i * BB, BB), BB), :], CT, i)
        return 0

    lax.fori_loop(0, S // BB, turn_ct, 0)
    ld_pw.wait()
    x_pw.wait_recv()
    GT, DO, E0 = part("GT"), part("DO"), part("E0")
    E1, GML = part("GM"), [part("GM", 0, PR), part("GM", PR, PR)]
    GT[...] = dot(CT[...], PW[...], 1, 1)
    for c in ld_d:
        c.wait()
    for c in x_d:
        c.wait_recv()

    def dt(k):
        return DT[k * HC : (k + 1) * HC, :]

    mark("sum_mid")
    mu_mid, sq = finish_stats(ex_mid, float(PR))
    inv_mid = lax.rsqrt(sq / total_mid + EPSILON)
    gain_mid, shift_mid = vec(2), vec(3)
    scale_mid = gain_mid * inv_mid
    mark("hidden_mid")

    def make_mid(i, _):
        at = pl.ds(al(i * 128, 128), 128)
        HM[at, :] = gelu_up((POOL[at, :] - mu_mid) * scale_mid + shift_mid).astype(BF)
        return 0

    lax.fori_loop(0, PR // 128, make_mid, 0)

    mark("dil_products")
    RS = [part("RS", 0, rim), part("RS", rim, rim)]
    RR = [part("RR", 0, rim), part("RR", rim, rim)]
    p_rims = Rims(RS[1], RR[1], RS[0], RR[0], 2)
    prod = dot(HM[PR - rim :, :], dt(0), 1, 1)
    RS[0][...] = prod.astype(BF)
    p_rims.start_up()
    E0[PR : PR + rim, :] = prod
    prod = dot(HM[0:rim, :], dt(2), 1, 1)
    RS[1][...] = prod.astype(BF)
    p_rims.start_down()
    E1[0:rim, :] = prod
    E0[rim:PR, :] = dot(HM[0 : PR - rim, :], dt(0), 1, 1)
    E1[rim:PR, :] = dot(HM[rim:, :], dt(2), 1, 1)
    DO[...] = dot(HM[...], dt(1), 1, 1)

    def take_rims(rims, low, high):
        rims.wait_from_down()
        rims.wait_from_up()

        @pl.when(has_down)
        def _():
            low[...] = RR[0][...].astype(F32)

        @pl.when(jnp.logical_not(has_down))
        def _():
            low[...] = jnp.zeros((rim, HC), F32)

        @pl.when(has_up)
        def _():
            high[...] = RR[1][...].astype(F32)

        @pl.when(jnp.logical_not(has_up))
        def _():
            high[...] = jnp.zeros((rim, HC), F32)

    mark("dil_wait")
    take_rims(p_rims, part("E0", 0, rim), part("GM", PR, rim))
    mark("dil_add")

    def same(i, by):
        def pick(off):
            return SEGX[pl.ds(al(i * 256 + BIN0 + off * 16, 16), 256), :].reshape(16, 2, 8, 128)[:, 0]

        return wide(jnp.where(pick(0) == pick(by), 1.0, 0.0).reshape(128, 128), HC // 128)

    def add_dil(i, s):
        at = pl.ds(al(i * 128, 128), 128)
        v = DO[at, :]
        v += same(i, -DIL) * E0[pl.ds(al(i * 128 + 8, 8), 128), :]
        v += same(i, DIL) * E1[pl.ds(al(i * 128 + DIL * 8, 8), 128), :]
        DO[at, :] = v
        return s + jnp.sum(v.reshape(16, 8, HC), axis=0)

    acc = lax.fori_loop(0, PR // 128, add_dil, jnp.zeros((8, HC), F32))
    mean = row_sum(acc) / float(PR)

    def m2_hid(i, acc):
        v = DO[pl.ds(al(i * 128, 128), 128), :].reshape(16, 8, HC) - mean
        return acc + jnp.sum(v * v, axis=0)

    acc = lax.fori_loop(0, PR // 128, m2_hid, jnp.zeros((8, HC), F32))
    ex_hid[0].start(jnp.concatenate([mean, row_sum(acc)], axis=0))
    mark("sum_hid")
    mu_hid, sq = finish_stats(ex_hid, float(PR))
    inv_hid = lax.rsqrt(sq / total_mid + EPSILON)
    gain_hid, shift_hid = hvec(4), hvec(5)
    HT = part("HT")
    mark("hidden_top")

    def make_top(i, s):
        at = pl.ds(al(i * 128, 128), 128)
        xhat = (DO[at, :] - mu_hid) * inv_hid
        h, slope = gelu_both(xhat * gain_hid + shift_hid)
        HT[at, :] = h.astype(BF)
        da = slope * GT[at, :]
        GT[at, :] = da
        DO[at, :] = xhat
        return (
            s[0] + jnp.sum((da * xhat).reshape(16, 8, HC), axis=0),
            s[1] + jnp.sum(da.reshape(16, 8, HC), axis=0),
        )

    zero = jnp.zeros((8, HC), F32)
    sg, sb = lax.fori_loop(0, PR // 128, make_top, (zero, zero))
    ex_bh[0].start(jnp.concatenate([row_sum(sg), row_sum(sb)], axis=0))

    mark("output")
    OB = 256

    def make_out(i, _):
        at = pl.ds(al(i * OB, OB), OB)
        v = (POOL[at, :] + dot(HT[at, :], PW[...], 1, 0)).astype(BF)
        COT[0][at, :] = v[:, :CH]
        COT[1][at, :] = v[:, CH:]
        return 0

    lax.fori_loop(0, PR // OB, make_out, 0)
    cot_other = r["N"].at[pl.ds(al(spans["COTR"][1] + other * PR, 16), PR)]
    o_own = local(cot_mine, r["oOUT"].at[m], 14)
    o_own.start()
    o_cross = cross(cot_other, r["oOUT"].at[m], 12)
    o_cross.start()
    DPR, DPS = part("R", TAPS * C, 2 * C), part("DPS")
    gp = dot(HT[...], CT[...], 0, 0)
    DPR[3 * CH : 3 * CH + HC, :] = jnp.where(m == 0, gp[:, :CH], gp[:, CH:]).astype(BF)
    DPS[3 * CH : 3 * CH + HC, :] = jnp.where(m == 0, gp[:, CH:], gp[:, :CH]).astype(BF)

    mark("sum_bh")
    v = finish_sums(ex_bh)
    ST[8:10, 0:HC] = v
    ST[8:10, HC:] = jnp.zeros((2, C - HC), F32)
    scale = gain_hid * inv_hid
    mg, mb = v[0:1] / total_mid, v[1:2] / total_mid
    mark("grad_dil")
    GD = [part("GD", k * PR, PR) for k in range(3)]

    def make_gd(i, _):
        at = pl.ds(al(i * 128, 128), 128)
        g = (scale * (GT[at, :] - mb - DO[at, :] * mg)).astype(BF)
        GD[1][at, :] = g
        E0[pl.ds(al(i * 128 + rim, 16), 128), :] = g.astype(F32)
        return 0

    lax.fori_loop(0, PR // 128, make_gd, 0)
    p_rims.drain()
    g_rims = Rims(part("GD", PR, rim), RR[1], part("GD", 2 * PR - rim, rim), RR[0], 4)
    g_rims.start_up()
    g_rims.start_down()

    mark("mid_center")

    def to_gm(make, add):
        for i in range(2):
            at = slice(i * (PR // 2), (i + 1) * (PR // 2))
            v = make(at)
            for h in range(2):
                u = v[:, h * CH : (h + 1) * CH]
                GML[h][at, :] = GML[h][at, :] + u if add else u

    to_gm(lambda at: dot(GD[1][at, :], dt(1), 1, 0), False)
    mark("gd_wait")
    take_rims(g_rims, part("E0", 0, rim), part("E0", PR + rim, rim))
    mark("mid_rest")

    def mask_gd(i, _):
        at = pl.ds(al(i * 128, 128), 128)
        GD[0][at, :] = (same(i, DIL) * E0[pl.ds(al(i * 128 + rim + DIL * 8, 8), 128), :]).astype(BF)
        GD[2][at, :] = (same(i, -DIL) * E0[pl.ds(al(i * 128 + rim - DIL * 8, 8), 128), :]).astype(BF)
        return 0

    lax.fori_loop(0, PR // 128, mask_gd, 0)
    to_gm(lambda at: dot(GD[0][at, :], dt(0), 1, 0) + dot(GD[2][at, :], dt(2), 1, 0), True)
    mark("mid_norm_back")

    def gm(at):
        return jnp.concatenate([GML[0][at, :], GML[1][at, :]], axis=1)

    def make_dmid(i, s):
        at = pl.ds(al(i * 64, 64), 64)
        xhat = (POOL[at, :] - mu_mid) * inv_mid
        _, slope = gelu_both(xhat * gain_mid + shift_mid)
        da = slope * gm(at)
        GML[0][at, :] = da[:, :CH]
        GML[1][at, :] = da[:, CH:]
        return (
            s[0] + jnp.sum((da * xhat).reshape(8, 8, C), axis=0),
            s[1] + jnp.sum(da.reshape(8, 8, C), axis=0),
        )

    zero = jnp.zeros((8, C), F32)
    sg, sb = lax.fori_loop(0, PR // 64, make_dmid, (zero, zero))
    g_rims.drain()
    o_own.wait()
    o_cross.wait_send()
    keep_x.wait()
    ex_bm[0].start(jnp.concatenate([row_sum(sg), row_sum(sb)], axis=0))

    ps, pr, zs, zr = r["ps"], r["pr"], r["zs"], r["zr"]
    N = r["N"]
    INNER = 4
    outer = nb // INNER
    inner = lax.rem(b, INNER)
    base = b - inner
    bits = (lax.rem(a, 2), a // 2)
    flip = ((b, m, a + 1 - 2 * bits[0]), (b, m, lax.rem(a + 2, 4)))
    drains = []
    HALF, QUART, SMALL = C // 2, C // 4, C // 16
    PSLOTS = spans["PS"][2] // C

    class Piece:
        def __init__(self, p):
            self.p = p
            self.first = p % 2
            b1, b2 = bits[self.first], bits[1 - self.first]
            self.n1, self.n2 = flip[self.first], flip[1 - self.first]
            self.k1 = b1 * HALF
            self.s1 = (1 - b1) * HALF
            self.k2 = b1 * HALF + b2 * QUART
            self.s2 = b1 * HALF + (1 - b2) * QUART
            self.phase = 0
            self.R = spans["R"][1] + p * C
            self.F = spans[f"F{p}"][1]
            self.XB, self.YB, self.ZB = [spans[f"{n}{p}"][1] for n in ("XB", "YB", "ZB")]

        def rows(self, start, at, n):
            return N.at[pl.ds(al(start + at, 16), n)]

        def get(self, start, at, n):
            return N[pl.ds(al(start + at, 16), n), :].astype(F32)

        def put(self, start, at, n, v):
            N[pl.ds(al(start + at, 16), n), :] = v.astype(BF)

        def send(self, src, dst, i, dev):
            c = remote(src, dst, ps.at[self.p, i], pr.at[self.p, i], dev)
            c.start()
            if i > 1:
                drains.append(c)
            self.cur = c
            return c

        def own(self, at):
            return self.get(self.R, at, HALF)

        def spread(self, which, make):
            for i in range(1, INNER):
                j = lax.rem(inner + i, INNER)
                src, dst = make(j)
                c = remote(src, dst, zs.at[self.p, which, j], zr.at[self.p, which, inner], (base + j, m, a))
                c.start()
                drains.append(c)
            self.which = which

        def gather(self, make):
            for i in range(1, INNER):
                j = lax.rem(inner + i, INNER)
                ref = make(j)
                remote(ref, ref, zs.at[self.p, self.which, j], zr.at[self.p, self.which, j], (base + j, m, a)).wait_recv()

        def step(self):
            p, ph = self.p, self.phase
            mark(f"piece{p}_phase{ph}")
            self.phase += 1
            if ph == 0:
                self.shares[0].wait_recv()
                self.put(self.R, self.s1, HALF, self.own(self.s1) + self.get(self.F, self.s1, HALF))
                self.send(self.rows(self.R, self.s1, HALF), self.rows(self.XB, 0, HALF), 2, self.n1)
                for c in self.shares[1:]:
                    c.wait_recv()
                self.put(self.R, self.k1, HALF, self.own(self.k1) + self.get(self.F, self.k1, HALF))
            elif ph == 1:
                self.cur.wait_recv()
                self.put(self.R, self.k1, HALF, self.get(self.R, self.k1, HALF) + self.get(self.XB, 0, HALF))
                self.send(self.rows(self.R, self.s2, QUART), self.rows(self.YB, 0, QUART), 3, self.n2)
            elif ph == 2:
                self.cur.wait_recv()
                self.put(self.R, self.k2, QUART, self.get(self.R, self.k2, QUART) + self.get(self.YB, 0, QUART))
                self.spread(0, lambda j: (self.rows(self.R, self.k2 + j * SMALL, SMALL), self.rows(self.ZB, inner * SMALL, SMALL)))
            elif ph == 3:
                self.gather(lambda j: self.rows(self.ZB, j * SMALL, SMALL))
                at = self.k2 + inner * SMALL
                v = self.get(self.R, at, SMALL)
                for i in range(1, INNER):
                    v += self.get(self.ZB, lax.rem(inner + i, INNER) * SMALL, SMALL)
                if outer > 1:
                    osem_s, osem_r = r["os_"], r["or_"]
                    mine = b // INNER
                    slot = lambda q: pl.ds(al(spans[f"OB{p}"][1] + q * SMALL, 8), SMALL)
                    r["F"][slot(mine), :] = v
                    for i in range(1, outer):
                        q = lax.rem(mine + i, outer)
                        ref = r["F"].at[slot(mine)]
                        c = remote(ref, ref, osem_s.at[p, q], osem_r.at[p, mine], (q * INNER + inner, m, a))
                        c.start()
                        drains.append(c)
                    for i in range(1, outer):
                        q = lax.rem(mine + i, outer)
                        ref = r["F"].at[slot(q)]
                        remote(ref, ref, osem_s.at[p, q], osem_r.at[p, q], (q * INNER + inner, m, a)).wait_recv()
                    v = r["F"][slot(0), :]
                    for j in range(1, outer):
                        v += r["F"][slot(j), :]
                self.put(self.F, at, SMALL, v)
                self.spread(1, lambda j: (self.rows(self.F, at, SMALL), self.rows(self.F, at, SMALL)))
            elif ph == 4:
                self.gather(lambda j: self.rows(self.F, self.k2 + j * SMALL, SMALL))
                ref = self.rows(self.F, self.k2, QUART)
                self.send(ref, ref, 4, self.n2)
            elif ph == 5:
                self.cur.wait_recv()
                ref = self.rows(self.F, self.k1, HALF)
                self.send(ref, ref, 5, self.n1)
            elif ph == 6:
                self.cur.wait_recv()
                to = r["oR"].at[ORDER[p]] if p < TAPS else r["oDP"].at[pl.ds((p - TAPS) * C, C)]
                self.out = local(self.rows(self.F, 0, C), to, 15 + p)
                self.out.start()

    ORDER = (2, 1, 3, 0, 4)
    pieces = [Piece(p) for p in range(TAPS + 2)]

    def pump(*which):
        for p in which:
            pieces[p].step()

    mark("dil_taps_grad")
    for k in range(3):
        g = dot(GD[k][...], HM[...], 0, 0)
        own = jnp.where(m == 0, g[:HH], g[HH:]).astype(BF)
        for_partner = jnp.where(m == 0, g[HH:], g[:HH]).astype(BF)
        for h in range(2):
            at = (h * 3 + k) * HH
            DPR[at : at + HH, :] = own[:, h * CH : (h + 1) * CH]
            DPS[at : at + HH, :] = for_partner[:, h * CH : (h + 1) * CH]
    for p in (TAPS, TAPS + 1):
        pc = pieces[p]
        pc.shares = [pc.send(part("DPS", (p - TAPS) * C, C), pc.rows(pc.F, 0, C), 0, place.partner)]
        drains.append(pc.cur)
    mark("sum_bm")
    v = finish_sums(ex_bm, lambda: pump(5, 6))
    ST[6:8, :] = v
    mg, mb = v[0:1] / total_mid, v[1:2] / total_mid
    mark("grad_conv")
    GC0, GC1 = part("GC0"), H1

    def make_gc(i, last):
        at = pl.ds(al(i * 64, 64), 64)
        xhat = (POOL[at, :] - mu_mid) * inv_mid
        g = CT[at, :].astype(F32) + scale_mid * (gm(at) - mb - xhat * mg)
        d = DIFF[at, :]
        e = jnp.exp(-jnp.abs(d))
        big = 1.0 / (1.0 + e)
        small = e * big
        g0 = g * jnp.where(d >= 0, big, small)
        g1 = g * jnp.where(d >= 0, small, big)
        v = jnp.stack([g0.reshape(8, 8, C), g1.reshape(8, 8, C)], axis=1).reshape(128, C)
        GC0[pl.ds(al(i * 128 + 16, 16), 128), :] = v.astype(BF)
        GC1[pl.ds(al(i * 128, 128), 128), :] = jnp.concatenate([last, v[:120]], axis=0).astype(BF)
        return v[120:]

    lax.fori_loop(0, PR // 64, make_gc, jnp.zeros((8, C), F32))
    g_halo = halos(GC0, 6)
    g_halo.start_down()
    g_halo.start_up()
    clear_halo(GC0)
    XX = part("XX")
    back_x = local(r["oX"], XX, 22)

    own_at = [spans["GM"][1], spans["GM"][1] + PR]
    h0_at = spans["H0"][1] + 16

    def tap(i, between):
        k = ORDER[i]
        mark(f"tap{k}")
        pc = pieces[i]
        start = own_at[i % 2]
        pc.own = lambda at: r["F"][pl.ds(al(start + at, 8), HALF), :]
        if i >= PSLOTS:
            for c in pieces[i - PSLOTS].shares:
                c.wait_send()
        if k == 2:
            g = GC0.at[pl.ds(16, HR)]
        else:
            g = XX

            def masked(j, _):
                XX[pl.ds(al(j * 256, 256), 256), :] = shifted(GC0, GC1, 2 - k, j * 256, 256)
                return 0

            lax.fori_loop(0, HR // 256, masked, 0)
        pc.shares = []
        ps_at = spans["PS"][1] + i % PSLOTS * C
        for j, at in enumerate((pc.s1, pc.k1)):
            v = dot(r["M"][h0_at : h0_at + HR, pl.ds(al(at, 128), HALF)], g[...], 0, 0)
            r["F"][pl.ds(al(start + at, 8), HALF), :] = jnp.where(m == 0, v[:, :CH], v[:, CH:])
            pc.put(ps_at, at, HALF, jnp.where(m == 0, v[:, CH:], v[:, :CH]))
            pc.shares.append(pc.send(pc.rows(ps_at, at, HALF), pc.rows(pc.F, at, HALF), j, place.partner))
            if j == 0:
                between()
                mark(f"tap{k}b")

    def halo_in():
        mark("halo_grad_conv")
        g_halo.wait_from_up()
        g_halo.wait_from_down()
        by_one_bin(GC0, GC1)

    tap(0, halo_in)
    pump(0)
    tap(1, lambda: pump(5, 6))
    pump(1)
    tap(2, lambda: pump(5, 6))
    pump(2)
    tap(3, lambda: pump(0))
    pump(3)
    tap(4, lambda: pump(1, 5, 6))
    pump(4)

    back_x.start()
    for pc in pieces[TAPS - PSLOTS : TAPS]:
        for c in pc.shares:
            c.wait_send()
    mu, inv, gain, shift = ST[0:1, :], ST[1:2, :], gain_in, shift_in
    RB = 256
    DA = [part("RAW", 0, HR), part("RAW", HR, HR)]

    def tile(i, s):
        mark("input_grad")
        at = i * RB
        acc = None
        for k in range(TAPS):
            d = dot(shifted(GC0, GC1, 2 - k, at, RB), w(k), 1, 1)
            acc = d if acc is None else acc + d
        put_lanes(acc, RB)
        if i == 0:
            back_x.wait()
        mark("input_grad_norm")

        def back(j, s):
            to = pl.ds(al(at + j * 64, 64), 64)
            xhat = (XX[to, :].astype(F32) - mu) * inv
            _, slope = gelu_both(xhat * gain + shift)
            da = slope * get_lanes(j * 64, 64)
            DA[0][to, :] = da[:, :CH].astype(BF)
            DA[1][to, :] = da[:, CH:].astype(BF)
            return (
                s[0] + jnp.sum((da * xhat).reshape(8, 8, C), axis=0),
                s[1] + jnp.sum(da.reshape(8, 8, C), axis=0),
            )

        return lax.fori_loop(0, RB // 64, back, s)

    s = (zero, zero)
    pumps = [[2, 0], [3, 1, 5, 6], [4, 2, 0], [3, 1], [4, 2, 0], [5, 6, 3, 1], [4, 2], [0, 5, 6]]
    for i in range(HR // RB):
        s = tile(i, s)
        pump(*pumps[i % len(pumps)])
    ex_bi[0].start(jnp.concatenate([row_sum(s[0]), row_sum(s[1])], axis=0))
    d_own = local(raw_mine, r["oDA"].at[m], 23)
    d_own.start()
    d_cross = cross(r["N"].at[pl.ds(al(spans["RAW"][1] + other * HR, 16), HR)], r["oDA"].at[m], 13)
    d_cross.start()
    rest = []
    left = [pc.phase for pc in pieces]
    while min(left) < 7:
        low = min(left)
        for p in (5, 6, 0, 1, 2, 3, 4):
            if left[p] == low:
                rest.append(p)
                left[p] += 1
    cut = min(6, len(rest))
    pump(*rest[:cut])
    mark("sum_bi")
    ST[4:6, :] = finish_sums(ex_bi)
    ST[3:4, :] = jnp.zeros((1, C), F32)
    ST[10:16, :] = jnp.zeros((6, C), F32)
    o_st = local(ST, r["oST"], 24)
    o_st.start()
    pump(*rest[cut:])
    mark("drain")
    for pc in pieces:
        pc.out.wait()
    for c in drains:
        c.wait_send()
    d_own.wait()
    o_st.wait()
    d_cross.wait()
    o_cross.wait_recv()
    for c in crosses:
        c.wait_send()
    for e in exchanges:
        e[0].drain()
        e[1].drain()
    h_halo.drain()
    g_halo.drain()
    mark()


def call_main(axes, sig, seg, cot, wide_taps, taps, pw, vectors):
    nb, nm, na = axes
    CH = sig.shape[1]
    C = 2 * CH
    HC = pw.shape[0]
    assert HC == CH
    HR = sig.shape[0] // 2
    PR = cot.shape[0] // 2
    T, S = HR // ROWS, PR // ROWS
    rim = (DIL + 1) * ROWS
    RT = 512
    NA = nm * na
    NP = TAPS + 2
    inputs = dict(sig=sig, seg=seg, cot=cot, wide=wide_taps, taps=taps, pw=pw)
    inputs.update({f"v{i}": v for i, v in enumerate(vectors)})
    sd = jax.ShapeDtypeStruct
    outs = dict(
        oX=sd((HR, C), BF),
        oDA=sd((2, HR, CH), BF),
        oOUT=sd((2, PR, CH), BF),
        oR=sd((TAPS, C, CH), BF),
        oDP=sd((2 * C, CH), BF),
        oST=sd((16, C), F32),
    )
    spans = {}

    def lay(pool, start, items):
        for name, n in items:
            spans[name] = (pool, start, n)
            start += n
        return start

    end = lay("N", 0, [("RAW", 2 * HR), ("STO", HR), ("COTR", 2 * PR), ("HT", PR), ("RS", 2 * rim), ("RR", 2 * rim)])
    lay("N", spans["STO"][1], [("DPS", 2 * C)])
    lay("N", spans["COTR"][1], [(f"XB{p}", C // 2) for p in range(TAPS)])
    lay("N", spans["HT"][1], [(f"YB{p}", C // 4) for p in range(TAPS)])
    lay("N", spans["RS"][1], [(f"F{p}", C) for p in range(2)])
    end = lay("N", end, [("GD", 3 * PR)])
    lay("N", spans["GD"][1], [("R", NP * C)])
    end = max(end, spans["R"][1] + NP * C)
    end = lay("N", end, [(f"F{p}", C) for p in range(2, NP)])
    lay("N", spans["RAW"][1] + HR, [("PS", 2 * C)])
    end = lay("N", end, [(f"XB{p}", C // 2) for p in range(TAPS, NP)] + [(f"YB{p}", C // 4) for p in range(TAPS, NP)])
    n_rows = lay("N", end, [(f"ZB{p}", C // 4) for p in range(NP)])
    end = lay("M", 0, [("X", HR), ("gap", 32), ("HM", PR), ("CT", PR), ("H0", HR + 32), ("H1", HR + 32)])
    lay("M", 0, [("GC0", HR + 32)])
    lay("M", spans["HM"][1], [("XX", HR)])
    m_rows = lay("M", end, [("W", TAPS * C), ("PW", HC), ("DT", 3 * HC)])
    f_rows = lay("F", 0, [("E0", PR + 2 * rim), ("GM", 2 * PR), ("DO", PR), ("GT", PR)])
    V = pltpu.VMEM
    DMA = pltpu.SemaphoreType.DMA
    scratch = dict(
        N=V((n_rows, CH), BF),
        M=V((m_rows, C), BF),
        F=V((f_rows, CH), F32),
        LANES=V((C // 128 * RT, 128), F32),
        MASK=V((4, HR, 128), BF),
        SEG=V(seg.shape, jnp.int32),
        SEGX=V(((T + 256) * ROWS, 128), F32),
        PAR=V((2, 8, CH), F32),
        ST=V((16, C), F32),
        SUM=V((8, C), F32),
        POOL=V((PR, C), F32),
        DIFF=V((PR, C), F32),
        XIA=V((NA, 2, CH), F32), XIB=V((nb, 2, C), F32),
        XMA=V((NA, 2, C), F32), XMB=V((nb, 2, C), F32),
        XHA=V((NA, 2, HC), F32), XHB=V((nb, 2, HC), F32),
        XGA=V((NA, 2, HC), F32), XGB=V((nb, 2, HC), F32),
        XDA=V((NA, 2, C), F32), XDB=V((nb, 2, C), F32),
        XSA=V((NA, 2, C), F32), XSB=V((nb, 2, C), F32),
        lsem=DMA((25,)),
        csem_s=DMA((14,)), csem_r=DMA((14,)),
        as_=DMA((6, NA)), ar_=DMA((6, NA)),
        bs_=DMA((6, nb)), br_=DMA((6, nb)),
        hs=DMA((8,)), hr=DMA((8,)),
        ps=DMA((NP, 6)), pr=DMA((NP, 6)),
        zs=DMA((NP, 2, 4)), zr=DMA((NP, 2, 4)),
    )
    outer = nb // 4
    if outer > 1:
        scratch.update(os_=DMA((NP, outer)), or_=DMA((NP, outer)))
        n = outer * (C // 16)
        assert lay("F", spans["E0"][1], [(f"OB{p}", n) for p in range(TAPS)]) <= spans["GM"][1]
        assert lay("F", spans["DO"][1], [(f"OB{p}", n) for p in range(TAPS, NP)]) <= f_rows
    names = list(inputs) + list(outs) + list(scratch)
    anyspec = pl.BlockSpec(memory_space=pl.ANY)
    vmem = pl.BlockSpec(memory_space=pltpu.VMEM)
    res = pl.pallas_call(
        functools.partial(main_body, (nb, nm, na, T, S, CH, HC), names, spans),
        out_shape=list(outs.values()),
        in_specs=[vmem if n.startswith("v") else anyspec for n in inputs],
        out_specs=[anyspec] * len(outs),
        scratch_shapes=list(scratch.values()),
        compiler_params=pltpu.CompilerParams(
            collective_id=0, has_side_effects=True, vmem_limit_bytes=VMEM_BYTES
        ),
        cost_estimate=pl.CostEstimate(flops=44_000_000_000, bytes_accessed=40_000_000, transcendentals=8_000_000),
        name="forward_and_backward",
    )(*inputs.values())
    return dict(zip(outs, res, strict=True))


def last_body(dims, sig, da, out, rr, dk0, dk1, pw, stats, gs_ref, out_ref, gw_ref, dk_ref, pw_ref,
              g0, g1, g2, g3, g4, g5, lanes, lanes2):
    CH, total_in = dims
    m = lax.axis_index("mp")
    step = pl.program_id(0)
    n = da.shape[1]
    BB = n // ROWS
    v = da[0].astype(F32)
    u = out[0].astype(F32)
    n2 = out.shape[1]
    B2 = n2 // ROWS
    for j in range(CH // 128):
        lanes[j * n : (j + 1) * n, :] = v[:, j * 128 : (j + 1) * 128]
        lanes2[j * n2 : (j + 1) * n2, :] = u[:, j * 128 : (j + 1) * 128]
    st = stats[:, pl.ds(al(m * CH, CH), CH)]
    mu, inv, gain, gg, gb = [st[i : i + 1] for i in (0, 1, 2, 4, 5)]
    scale = gain * inv
    mg, mb = gg / total_in, gb / total_in
    for row in range(ROWS):
        for j in range(CH // 128):
            c = slice(j * 128, (j + 1) * 128)
            d = lanes[pl.ds(j * n + row, BB, stride=ROWS), :]
            xhat = (sig[row, :, c].astype(F32) - mu[:, c]) * inv[:, c]
            gs_ref[row, :, c] = scale[:, c] * (d - mb[:, c] - xhat * mg[:, c])
            out_ref[row, :, c] = lanes2[pl.ds(j * n2 + row, B2, stride=ROWS), :].astype(BF)
    gw_ref[...] = rr[...].astype(F32)
    dk_ref[...] = jnp.concatenate([dk0[...].astype(F32), dk1[...].astype(F32)], axis=1)
    pw_ref[...] = pw[...].astype(F32)

    @pl.when(step == 0)
    def _():
        for ref, i in ((g0, 4), (g1, 5), (g2, 6), (g3, 7)):
            ref[...] = st[i : i + 1].reshape(CH)
        HH = g4.shape[0]
        hid = stats[8:10, : 2 * HH]
        hid = jnp.where(m == 0, hid[:, :HH], hid[:, HH:])
        g4[...] = hid[0:1].reshape(HH)
        g5[...] = hid[1:2].reshape(HH)


def call_last(axes, sig, o):
    nb, nm, na = axes
    rows, T, CH = sig.shape
    S = T // 2
    C = 2 * CH
    HC = CH
    HH = HC // 2
    NC = 4
    steps = 2 * NC
    sd = jax.ShapeDtypeStruct
    total_in = float(rows * T * nb * na)
    rr = o["oR"].reshape(-1, CH)
    dp = o["oDP"]
    flat = lambda n, w: pl.BlockSpec((n, w), lambda i: (i, 0))
    whole1 = pl.BlockSpec(memory_space=pltpu.VMEM)
    nr, npw, nd = rr.shape[0] // steps, HC // steps, 3 * HH // NC
    return pl.pallas_call(
        functools.partial(last_body, (CH, total_in)),
        grid=(steps,),
        out_shape=[
            sd((rows, T, CH), F32),
            sd((rows, S, CH), BF),
            sd(rr.shape, F32),
            sd((3 * HH, C), F32),
            sd((HC, CH), F32),
            *[sd((CH,), F32)] * 4,
            *[sd((HH,), F32)] * 2,
        ],
        in_specs=[
            pl.BlockSpec((ROWS, T // NC, CH), lambda i: (i // NC, i % NC, 0)),
            pl.BlockSpec((1, T * ROWS // NC, CH), lambda i: (i // NC, i % NC, 0)),
            pl.BlockSpec((1, S * ROWS // NC, CH), lambda i: (i // NC, i % NC, 0)),
            flat(nr, CH),
            pl.BlockSpec((nd, CH), lambda i: (i // 2, 0)),
            pl.BlockSpec((nd, CH), lambda i: (NC + i // 2, 0)),
            pl.BlockSpec((npw, CH), lambda i: (6 * HH // npw + i, 0)),
            pl.BlockSpec((16, C), lambda i: (0, 0)),
        ],
        out_specs=[
            pl.BlockSpec((ROWS, T // NC, CH), lambda i: (i // NC, i % NC, 0)),
            pl.BlockSpec((ROWS, S // NC, CH), lambda i: (i // NC, i % NC, 0)),
            flat(nr, CH),
            pl.BlockSpec((nd, C), lambda i: (i // 2, 0)),
            flat(npw, CH),
            *[pl.BlockSpec((CH,), lambda i: (0,))] * 4,
            *[pl.BlockSpec((HH,), lambda i: (0,))] * 2,
        ],
        scratch_shapes=[
            pltpu.VMEM((CH // 128 * T * ROWS // NC, 128), F32),
            pltpu.VMEM((CH // 128 * S * ROWS // NC, 128), F32),
        ],
        compiler_params=pltpu.CompilerParams(vmem_limit_bytes=VMEM_BYTES),
        name="last_pass",
    )(sig, o["oDA"], o["oOUT"], rr, dp, dp, dp, o["oST"])


def on_device(axes, signal, seg, cotangent, conv_wide, taps, pointwise, *vectors):
    CH = signal.shape[2]
    o = call_main(
        axes, signal.reshape(-1, CH), seg, cotangent.reshape(-1, CH), conv_wide, jnp.swapaxes(taps, 1, 2), pointwise, vectors
    )
    gs, out, gw, dk, pw, *small = call_last(axes, signal, o)
    K, C, HH = taps.shape
    return (out, gs, gw.reshape(conv_wide.shape), jnp.swapaxes(dk.reshape(K, HH, C), 1, 2), pw, *small)


def solution(mesh):
    axes = (mesh.shape["bins"], mesh.shape["mp"], mesh.shape["batch"])
    cut = P("batch", "bins", "mp")
    tap = P(None, None, "mp")
    return jax.shard_map(
        functools.partial(on_device, axes),
        mesh=mesh,
        in_specs=(cut, P("batch", None), cut, tap, tap, P(None, "mp")) + (P("mp"),) * 6,
        out_specs=(cut, cut, tap, tap, P(None, "mp")) + (P("mp"),) * 6,
        check_vma=False,
    )
```

```python
import functools
import types

import jax
import jax.numpy as jnp
from jax import lax
from jax.experimental import pallas as pl
from jax.experimental.pallas import tpu as pltpu
from jax.sharding import PartitionSpec as P

DIL = 57
EPSILON = 1e-05
TAPS = 5
BF = jnp.bfloat16
F32 = jnp.float32
MESH = pl.DeviceIdType.MESH
K0 = 0.7978845608028654
K3 = 0.044715
ROWS = 8
VMEM_BYTES = 63 * 2**20


def gelu_up(x):
    t = jnp.tanh(x * (K0 + (K0 * K3) * (x * x)))
    h = 0.5 * x
    return h + h * t


def gelu_both(x):
    x2 = x * x
    t = jnp.tanh(x * (K0 + (K0 * K3) * x2))
    h = 0.5 * x
    return h + h * t, 0.5 + 0.5 * t + h * (1.0 - t * t) * (K0 + (3.0 * K0 * K3) * x2)


def dot(a, b, ca, cb):
    return lax.dot_general(a, b, (((ca,), (cb,)), ((), ())), preferred_element_type=F32)


def wide(mask, times):
    return jnp.concatenate([mask] * times, axis=1)


def al(x, n):
    return pl.multiple_of(x, n)


class Place:
    def __init__(self, nb, nm, na):
        self.nb, self.nm, self.na = nb, nm, na
        self.b = lax.axis_index("bins")
        self.m = lax.axis_index("mp")
        self.a = lax.axis_index("batch")
        self.layer = nm * na
        self.q = self.m * na + self.a

    def in_layer(self, q):
        return (self.b, q // self.na, lax.rem(q, self.na))

    def in_bins(self, b):
        return (b, self.m, self.a)

    @property
    def partner(self):
        return (self.b, 1 - self.m, self.a)

    def others(self, me, n):
        return [lax.rem(me + i, n) for i in range(1, n)]


def remote(src, dst, ss, rs, dev):
    return pltpu.make_async_remote_copy(
        src_ref=src, dst_ref=dst, send_sem=ss, recv_sem=rs, device_id=dev, device_id_type=MESH
    )


class Exchange:
    def __init__(self, buf, me, n, dev_of, ss, rs, others):
        self.buf, self.me, self.n, self.dev_of, self.ss, self.rs, self.others = (
            buf, me, n, dev_of, ss, rs, others,
        )

    def start(self, value):
        self.buf[self.me] = value
        for q in self.others:
            remote(self.buf.at[self.me], self.buf.at[self.me], self.ss.at[q], self.rs.at[self.me], self.dev_of(q)).start()

    def wait(self):
        for q in self.others:
            remote(self.buf.at[q], self.buf.at[q], self.ss.at[q], self.rs.at[q], self.dev_of(q)).wait_recv()
        return [self.buf[i] for i in range(self.n)]

    def drain(self):
        for q in self.others:
            remote(self.buf.at[self.me], self.buf.at[self.me], self.ss.at[q], self.rs.at[q], self.dev_of(q)).wait_send()


def merged(parts, count):
    means = [p[0:1] for p in parts]
    total = functools.reduce(jnp.add, means)
    mean = total / len(parts)
    squares = functools.reduce(jnp.add, [p[1:2] for p in parts])
    apart = functools.reduce(jnp.add, [(x - mean) * (x - mean) for x in means])
    return mean, squares + count * apart


def row_sum(x):
    return jnp.sum(x, axis=0, keepdims=True)


def greet(place):
    barrier = pltpu.get_barrier_semaphore()
    devices = [place.in_layer(q) for q in place.others(place.q, place.layer)]
    devices += [place.in_bins(b) for b in place.others(place.b, place.nb)]
    for d in devices:
        pl.semaphore_signal(barrier, inc=1, device_id=d, device_id_type=MESH)
    pl.semaphore_wait(barrier, len(devices))


PLAN = (
    ("bh", [18]),
    ("center", [18]),
    ("center2", [19]),
    ("rims", [18]),
    ("bm", [19, 15, 16, 17]),
    ("bm2", [18]),
    ("tap0", [19, 15, 16, 17]),
    ("tap1", [18, 0, 2]),
    ("tap2", [1]),
    ("tap3", [15, 16, 17, 4]),
    ("tap4", [3, 5]),
    ("tap5", [18, 1, 6, 8]),
    ("tap6", [19, 0, 15, 7]),
    ("tap7", [16, 2, 3, 10]),
    ("tap8", [17, 4, 5, 9, 11]),
    ("tap9", [1, 0, 15, 12, 14]),
    ("taps", [6, 7, 16, 13]),
    ("tile0", [2, 8, 4, 17]),
    ("tile1", [19]),
    ("tile2", [1, 9, 3, 0]),
    ("tile3", [11]),
    ("tile4", [10, 6, 2, 5]),
    ("tile5", [16, 4, 15]),
    ("tile6", [1, 13, 12]),
    ("tile7", [3, 8]),
    ("tile8", [0, 14, 6]),
    ("tile9", [7, 2, 19]),
    ("tile10", [17, 5, 10, 9, 4]),
    ("tile11", [11]),
    ("tile12", [3, 15, 8, 12, 16]),
    ("tile13", [6, 0]),
    ("tile14", [1, 7, 14, 13, 5, 2]),
    ("tile15", [10, 3]),
    ("end0", [9, 17, 11, 4, 0, 8, 6, 5, 12, 7, 1, 2, 14]),
    ("end1", [13, 3, 4, 10, 8, 9, 6, 11, 5, 7, 12, 10, 14, 8, 13, 9, 11, 7, 12, 10, 14, 13, 9, 12, 11, 14, 13]),
)


def main_body(dims, names, spans, *refs):
    nb, nm, na, T, S, CH, HC = dims
    C = 2 * CH
    HR = T * ROWS
    PR = S * ROWS
    rim = (DIL + 1) * ROWS
    r = types.SimpleNamespace(**dict(zip(names, refs, strict=True)))
    place = Place(nb, nm, na)
    b, m, a = place.b, place.m, place.a
    other = 1 - m
    total_in = float(HR * nb * nm * na)
    total_mid = float(PR * nb * nm * na)
    LANES = r.LANES
    RT = LANES.shape[0] // (C // 128)

    def part(name, at=0, n=None):
        pool, start, rows = spans[name]
        return getattr(r, pool).at[pl.ds(start + at, rows if n is None else n)]

    def local(src, dst, i):
        return pltpu.make_async_copy(src, dst, r.lsem.at[i])

    def cross(src, dst, i):
        return remote(src, dst, r.csem_s.at[i], r.csem_r.at[i], place.partner)

    RAW, STO, X, CT, HM = part("RAW"), part("STO"), part("X"), part("CT"), part("HM")
    H0, H1, W, PW, DT = part("H0"), part("H1"), part("W"), part("PW"), part("DT")
    COT = [part("COTR", 0, PR), part("COTR", PR, PR)]
    vectors = [r.v0, r.v1, r.v2, r.v3, r.v4, r.v5]
    PAR, SEG, SEGX, MASK, ST = r.PAR, r.SEG, r.SEGX, r.MASK, r.ST
    half = lambda at, n: pl.ds(al(at + m * n, n), n)

    sig, cot = r.sig, r.cot
    mine, theirs = pl.ds(al(m * HR, HR), HR), pl.ds(al(other * HR, HR), HR)
    raw_mine = r.N.at[pl.ds(al(spans["RAW"][1] + m * HR, 16), HR)]
    cot_mine = r.N.at[pl.ds(al(spans["COTR"][1] + m * PR, 16), PR)]
    lanes = pl.ds(al(m * CH, CH), CH)
    w0, pw0, dt0 = spans["W"][1], spans["PW"][1], spans["DT"][1]
    HH = HC // 2

    def weight(k):
        return r.M.at[pl.ds(w0 + k * C, C), lanes]

    def tap_rows(k):
        return r.M.at[pl.ds(al(dt0 + k * HC + m * HH, 16), HH)]

    pw_mine = r.M.at[pl.ds(pw0, HC), lanes]
    ld_sto = local(sig.at[theirs], STO, 0)
    ld_raw = local(sig.at[mine], raw_mine, 1)
    ld_seg = local(r.seg, SEG, 2)
    ld_w = [local(r.wide.at[k], weight(k), 3 + k) for k in range(TAPS)]
    ld_d = [local(r.taps.at[k], tap_rows(k), 8 + k) for k in range(3)]
    ld_pw = local(r.pw, pw_mine, 11)
    ld_cot = local(cot.at[pl.ds(al(m * PR, PR), PR)], cot_mine, 12)
    for c in [ld_sto, ld_raw, ld_seg, *ld_w, *ld_d, ld_pw, ld_cot]:
        c.start()
    for i in range(4):
        PAR[m, i : i + 1, :] = vectors[i][...].reshape(1, CH)
    for i in range(4, 6):
        PAR[m, i : i + 1, 0:HH] = vectors[i][...].reshape(1, HH)
    greet(place)
    x_sig = cross(sig.at[theirs], raw_mine, 0)
    x_par = cross(PAR.at[m], PAR.at[m], 1)
    x_w = [cross(r.wide.at[k], weight(k), 2 + k) for k in range(TAPS)]
    x_d = [cross(r.taps.at[k], tap_rows(k), 7 + k) for k in range(3)]
    x_pw = cross(r.pw, pw_mine, 10)
    x_cot = cross(cot.at[pl.ds(al(other * PR, PR), PR)], cot_mine, 11)
    crosses = [x_sig, x_par, *x_w, x_cot, x_pw, *x_d]
    for c in crosses:
        c.start()

    def exchange(i, name):
        return (
            Exchange(getattr(r, name + "A"), place.q, place.layer, place.in_layer, r.as_.at[i], r.ar_.at[i], place.others(place.q, place.layer)),
            Exchange(getattr(r, name + "B"), b, nb, place.in_bins, r.bs_.at[i], r.br_.at[i], place.others(b, nb)),
        )

    def finish_stats(ex, count):
        mean, squares = merged(ex[0].wait(), count)
        ex[1].start(jnp.concatenate([mean, squares], axis=0))
        return merged(ex[1].wait(), count * place.layer)

    def finish_sums(ex, between=lambda: None):
        ex[1].start(functools.reduce(jnp.add, ex[0].wait()))
        between()
        return functools.reduce(jnp.add, ex[1].wait())

    ex_in, ex_mid, ex_hid, ex_bh, ex_bm, ex_bi = exchanges = [
        exchange(i, n) for i, n in enumerate(["XI", "XM", "XH", "XG", "XD", "XS"])
    ]

    ps, pr, zs, zr = r.ps, r.pr, r.zs, r.zr
    N = r.N
    INNER = 4
    outer = nb // INNER
    inner = lax.rem(b, INNER)
    base = b - inner
    bits = (lax.rem(a, 2), a // 2)
    flip = ((b, m, a + 1 - 2 * bits[0]), (b, m, lax.rem(a + 2, 4)))
    early = outer == 1
    PSLOTS = spans["PS"][2] // C

    class Piece:
        def __init__(self, p, stack, lanes, first, n, R, F, full=False):
            self.p = p
            self.stack = stack
            self.lanes = pl.ds(*lanes)
            self.first = first
            self.n = n
            HALF, QUART = n // 2, n // 4
            self.SMALL = n // 16
            self.full = full
            self.steps = [0, 1, 2, 3, 5, 6] if full else [0, 1, 2, 3, 4, 5, 6]
            b1, b2 = bits[self.first], bits[1 - self.first]
            self.n1, self.n2 = flip[self.first], flip[1 - self.first]
            self.k1 = b1 * HALF
            self.s1 = (1 - b1) * HALF
            self.k2 = b1 * HALF + b2 * QUART
            self.s2 = b1 * HALF + (1 - b2) * QUART
            self.HALF, self.QUART = HALF, QUART
            self.R, self.F = R, F
            self.XB, self.YB, self.ZB = [spans[f"{x}{stack}"][1] for x in ("XB", "YB", "ZB")]

        def rows(self, start, at, n):
            return N.at[pl.ds(al(start + at, 16), n), self.lanes]

        def get(self, start, at, n):
            return N[pl.ds(al(start + at, 16), n), self.lanes].astype(F32)

        def put(self, start, at, n, v):
            N[pl.ds(al(start + at, 16), n), self.lanes] = v.astype(BF)

        def describe(self, make, i, dev):
            return lambda: remote(*make(), ps.at[self.p, i], pr.at[self.p, i], dev)

        def moves(self):
            F, R = self.F, self.R
            return {
                2: self.describe(lambda: (self.rows(R, self.s1, self.HALF), self.rows(self.XB, 0, self.HALF)), 2, self.n1),
                3: self.describe(lambda: (self.rows(R, self.s2, self.QUART), self.rows(self.YB, 0, self.QUART)), 3, self.n2),
                4: self.describe(lambda: (self.rows(F, self.k2, self.QUART),) * 2, 4, self.n2),
                5: self.describe(lambda: (self.rows(F, self.k1, self.HALF),) * 2, 5, self.n1),
            }

        def toward(self, which, i):
            j = lax.rem(inner + i, INNER)
            if self.full:
                src, dst = self.rows(self.R, self.k2, self.QUART), self.rows(self.ZB, inner * self.QUART, self.QUART)
            elif which == 0:
                src, dst = self.rows(self.R, self.k2 + j * self.SMALL, self.SMALL), self.rows(self.ZB, inner * self.SMALL, self.SMALL)
            else:
                src = dst = self.rows(self.F, self.k2 + inner * self.SMALL, self.SMALL)
            return remote(src, dst, zs.at[self.p, which, j], zr.at[self.p, which, inner], (base + j, m, a))

        def gather(self, which):
            for i in range(1, INNER):
                j = lax.rem(inner + i, INNER)
                if self.full:
                    ref = self.rows(self.ZB, j * self.QUART, self.QUART)
                else:
                    ref = self.rows(self.ZB, j * self.SMALL, self.SMALL) if which == 0 else self.rows(self.F, self.k2 + j * self.SMALL, self.SMALL)
                remote(ref, ref, zs.at[self.p, which, j], zr.at[self.p, which, j], (base + j, m, a)).wait_recv()

        def drain(self):
            for i in (2, 3, 4, 5):
                self.moves()[i]().wait_send()
            for which in range(1 if self.full else 2):
                for i in range(1, INNER):
                    self.toward(which, i).wait_send()
            if outer > 1:
                for i in range(1, outer):
                    self.outward(i).wait_send()
            self.out().wait()

        def outward(self, i):
            mine = b // INNER
            q = lax.rem(mine + i, outer)
            ref = r.F.at[self.slot(mine), self.lanes]
            return remote(ref, ref, r.os_.at[self.p, q], r.or_.at[self.p, mine], (q * INNER + inner, m, a))

        def slot(self, q):
            return pl.ds(al(spans[f"OB{self.stack}"][1] + q * self.SMALL, 8), self.SMALL)

        def out(self):
            k = self.stack
            to = r.oR.at[ORDER[k], :, self.lanes] if k < TAPS else r.oDP.at[pl.ds(self.F - dp_at, self.n), self.lanes]
            return local(self.rows(self.F, 0, self.n), to, 15 + self.p)

        def step(self, ph):
            p, moves = self.p, self.moves()
            HALF, QUART, SMALL = self.HALF, self.QUART, self.SMALL
            if ph == 0:
                moves[2]().start()
            elif ph == 1:
                moves[2]().wait_recv()
                self.put(self.R, self.k1, HALF, self.get(self.R, self.k1, HALF) + self.get(self.XB, 0, HALF))
                moves[3]().start()
            elif ph == 2:
                moves[3]().wait_recv()
                self.put(self.R, self.k2, QUART, self.get(self.R, self.k2, QUART) + self.get(self.YB, 0, QUART))
                for i in range(1, INNER):
                    self.toward(0, i).start()
            elif ph == 3:
                self.gather(0)
                n = QUART if self.full else SMALL
                at = self.k2 if self.full else self.k2 + inner * SMALL
                v = self.get(self.R, at, n)
                for i in range(1, INNER):
                    v += self.get(self.ZB, lax.rem(inner + i, INNER) * n, n)
                if outer > 1:
                    mine = b // INNER
                    r.F[self.slot(mine), self.lanes] = v
                    for i in range(1, outer):
                        self.outward(i).start()
                    for i in range(1, outer):
                        q = lax.rem(mine + i, outer)
                        ref = r.F.at[self.slot(q), self.lanes]
                        remote(ref, ref, r.os_.at[p, q], r.or_.at[p, q], (q * INNER + inner, m, a)).wait_recv()
                    v = r.F[self.slot(0), self.lanes]
                    for j in range(1, outer):
                        v += r.F[self.slot(j), self.lanes]
                self.put(self.F, at, n, v)
                if self.full:
                    moves[4]().start()
                else:
                    for i in range(1, INNER):
                        self.toward(1, i).start()
            elif ph == 4:
                self.gather(1)
                moves[4]().start()
            elif ph == 5:
                moves[4]().wait_recv()
                moves[5]().start()
            elif ph == 6:
                moves[5]().wait_recv()
                self.out().start()

    ORDER = (2, 1, 3, 0, 4)
    r_at, dp_at = spans["R"][1], spans["FD"][1]
    dps_at, dpr_at = spans["DPS"][1], r_at + TAPS * C
    thirds = [(q * CH // 3, CH // 3) for q in range(3)]
    pieces = []
    for k in range(TAPS + 1):
        for q in range(3):
            R, F = r_at + k * C, spans[f"F{k}"][1] if k < TAPS else dp_at
            pieces.append(Piece(len(pieces), k, thirds[q], (k + q) % 2, C, R, F))
    late = len(pieces)
    if early:
        pieces.append(Piece(late, 6, (0, CH), 0, CH, r_at + 6 * C, dp_at + C, True))
        pieces.append(Piece(late + 1, 7, (0, CH), 1, CH, r_at + 6 * C + CH, dp_at + C + CH, True))
    else:
        pieces.append(Piece(late, 6, (0, CH), 0, C, r_at + 6 * C, dp_at + C))

    class Share:
        def __init__(self, sem, src, dst, own, to, n):
            self.sem, self.src, self.dst, self.own, self.to, self.n = sem, src, dst, own, to, n

        def copy(self):
            at = lambda start: N.at[pl.ds(al(start, 16), self.n)]
            return remote(at(self.src), at(self.dst), r.shs.at[self.sem], r.shr.at[self.sem], place.partner)

        def sum(self):
            self.copy().wait_recv()
            v = self.own() + N[pl.ds(al(self.dst, 16), self.n), :].astype(F32)
            N[pl.ds(al(self.to, 16), self.n), :] = v.astype(BF)

    def dil_share(sem, at, n):
        own = lambda: N[pl.ds(dpr_at + at, n), :].astype(F32)
        return Share(sem, dps_at + at, dp_at + at, own, dpr_at + at, n)

    share_rest, share_pw, share_mid = dil_share(10, 0, C), dil_share(11, C, CH), dil_share(12, C + CH, CH)

    left = [list(pc.steps) for pc in pieces]
    plan = {}
    for name, which in PLAN:
        if not early:
            which = [p for p in which if p < len(pieces) and not (p == late and name in ("bh", "center", "center2"))]
        plan[name] = [(p, left[p].pop(0)) for p in which if left[p]]
    while any(left):
        first = max(len(x) for x in left)
        plan["end1"] += [(p, x.pop(0)) for p, x in enumerate(left) if len(x) == first]

    def pump(where):
        for p, ph in plan[where]:
            pieces[p].step(ph)

    ld_sto.wait()
    ld_raw.wait()
    CHK = 128
    raw_at = spans["RAW"][1] + m * HR

    def own_raw(i):
        return r.N[pl.ds(al(raw_at + i * CHK, 16), CHK), :].astype(F32).reshape(CHK // 8, 8, CH)

    def sto(i):
        return STO[pl.ds(al(i * CHK, CHK), CHK), :].astype(F32).reshape(CHK // 8, 8, CH)

    def s1(i, acc):
        return acc + jnp.sum(own_raw(i), axis=0) + jnp.sum(sto(i), axis=0)

    acc = lax.fori_loop(0, HR // CHK, s1, jnp.zeros((8, CH), F32))
    mean = row_sum(acc) / float(2 * HR)

    def s2(i, acc):
        u = own_raw(i) - mean
        v = sto(i) - mean
        return acc + jnp.sum(u * u, axis=0) + jnp.sum(v * v, axis=0)

    acc = lax.fori_loop(0, HR // CHK, s2, jnp.zeros((8, CH), F32))
    ex_in[0].start(jnp.concatenate([mean, row_sum(acc)], axis=0))

    ld_seg.wait()
    blocks = SEG.shape[1] // 128

    def make_segs(i, _):
        at = b * (T // 128) - 1 + i
        v = SEG[pl.ds(al(m * ROWS, ROWS), ROWS), pl.ds(al(jnp.clip(at, 0, blocks - 1) * 128, 128), 128)].astype(F32)
        v = jnp.where(jnp.logical_and(at >= 0, at < blocks), v, -1.0)
        for j in range(128):
            SEGX[pl.ds(al(i * 1024 + j * 8, 8), 8), :] = jnp.broadcast_to(v[:, j : j + 1], (8, 128))
        return 0

    lax.fori_loop(0, T // 128 + 2, make_segs, 0)
    BIN0 = 128 * 8

    def make_masks(i, _):
        mid = SEGX[pl.ds(al(i * 128 + BIN0, 128), 128), :]
        for j, o in enumerate((-2, -1, 1, 2)):
            off = SEGX[pl.ds(al(i * 128 + BIN0 + o * 8, 8), 128), :]
            MASK[j, pl.ds(al(i * 128, 128), 128), :] = jnp.where(off == mid, 1.0, 0.0).astype(BF)
        return 0

    lax.fori_loop(0, HR // 128, make_masks, 0)
    x_sig.wait_recv()
    BB = RT // ROWS

    def turn(src, dst, i):
        for h in range(2):
            for row in range(ROWS):
                v = src(h, row).astype(F32)
                for j in range(CH // 128):
                    LANES[pl.ds((h * (CH // 128) + j) * RT + row, BB, stride=ROWS), :] = v[:, j * 128 : (j + 1) * 128]
        for j in range(C // 128):
            dst[pl.ds(al(i * RT, RT), RT), j * 128 : (j + 1) * 128] = LANES[j * RT : (j + 1) * RT, :].astype(BF)

    def turn_x(i, _):
        turn(lambda h, row: RAW[pl.ds(al(h * HR + row * T + i * BB, BB), BB), :], X, i)
        return 0

    lax.fori_loop(0, T // BB, turn_x, 0)
    keep_x = local(X, r.oX, 13)
    keep_x.start()
    x_par.wait_recv()

    def vec(i):
        return jnp.concatenate([PAR[0, i : i + 1, :], PAR[1, i : i + 1, :]], axis=1)

    def hvec(i):
        return jnp.concatenate([PAR[0, i : i + 1, 0:HH], PAR[1, i : i + 1, 0:HH]], axis=1)

    la = ex_in[0].wait()
    n_own = float(2 * HR)
    lo = merged(la[0:na], n_own)
    hi = merged(la[na : 2 * na], n_own)
    ex_in[1].start(
        jnp.concatenate([jnp.concatenate([lo[0], hi[0]], axis=1), jnp.concatenate([lo[1], hi[1]], axis=1)], axis=0)
    )
    mu_in, sq = merged(ex_in[1].wait(), n_own * na)
    inv_in = lax.rsqrt(sq / total_in + EPSILON)
    gain_in, shift_in = vec(0), vec(1)
    scale_in = gain_in * inv_in
    ST[0:1, :] = mu_in
    ST[1:2, :] = inv_in
    ST[2:3, :] = gain_in
    HB = 256

    def make_hidden(i, last):
        at = al(i * HB, HB)
        pre = (X[pl.ds(at, HB), :].astype(F32) - mu_in) * scale_in + shift_in
        h = gelu_up(pre)
        H0[pl.ds(al(at + 16, 16), HB), :] = h.astype(BF)
        H1[pl.ds(at, HB), :] = jnp.concatenate([last, h[: HB - 8]], axis=0).astype(BF)
        return h[HB - 8 :]

    lax.fori_loop(0, HR // HB, make_hidden, jnp.zeros((8, C), F32))
    hs, hr = r.hs, r.hr
    down = (jnp.maximum(b - 1, 0), m, a)
    up = (jnp.minimum(b + 1, nb - 1), m, a)
    has_down, has_up = b > 0, b < nb - 1

    def when_down(f):
        pl.when(has_down)(f)

    def when_up(f):
        pl.when(has_up)(f)

    class Rims:
        def __init__(self, to_down, from_up, to_up, from_down, i):
            self.down = remote(to_down, from_up, hs.at[i], hr.at[i], down)
            self.up = remote(to_up, from_down, hs.at[i + 1], hr.at[i + 1], up)

        def start_down(self):
            when_down(self.down.start)

        def start_up(self):
            when_up(self.up.start)

        def wait_from_up(self):
            when_up(self.down.wait_recv)

        def wait_from_down(self):
            when_down(self.up.wait_recv)

        def drain(self):
            when_down(self.down.wait_send)
            when_up(self.up.wait_send)

    def clear_halo(ref):
        @pl.when(jnp.logical_not(has_down))
        def _():
            ref[0:16, :] = jnp.zeros((16, C), BF)

        @pl.when(jnp.logical_not(has_up))
        def _():
            ref[pl.ds(HR + 16, 16), :] = jnp.zeros((16, C), BF)

    def halos(ref, i):
        return Rims(ref.at[pl.ds(16, 16)], ref.at[pl.ds(HR + 16, 16)], ref.at[pl.ds(HR, 16)], ref.at[pl.ds(0, 16)], i)

    h_halo = halos(H0, 0)
    h_halo.start_down()
    h_halo.start_up()
    clear_halo(H0)

    def by_one_bin(even, odd):
        v = even[0:32, :].astype(F32)
        odd[0:16, :] = v[8:24].astype(BF)
        v = even[pl.ds(HR, 32), :].astype(F32)
        odd[pl.ds(HR, 16), :] = v[8:24].astype(BF)

    MJ = {-2: 0, -1: 1, 1: 2, 2: 3}

    def shifted(even, odd, o, at, n):
        if o % 2 == 0:
            v = even[pl.ds(al(at + (o + 2) * 8, 16), n), :]
        else:
            v = odd[pl.ds(al(at + (o + 1) * 8, 16), n), :]
        if o != 0:
            v = v * wide(MASK[MJ[o], pl.ds(al(at, 16), n), :], C // 128)
        return v

    def w(k):
        return W[k * C : (k + 1) * C, :]

    def put_lanes(v, n):
        for j in range(C // 128):
            LANES[j * RT : j * RT + n, :] = v[:, j * 128 : (j + 1) * 128]

    def get_lanes(at, n):
        return jnp.concatenate([LANES[pl.ds(al(j * RT + at, 8), n), :] for j in range(C // 128)], axis=1)

    for c in (*ld_w,):
        c.wait()
    for c in x_w:
        c.wait_recv()
    POOL, DIFF, SUM = r.POOL, r.DIFF, r.SUM
    SUM[...] = jnp.zeros_like(SUM)

    def conv_tile(i):
        at = al(i * RT, RT)
        acc = None
        for k in range(TAPS):
            d = dot(shifted(H0, H1, k - 2, at, RT), w(k), 1, 0)
            acc = d if acc is None else acc + d
        put_lanes(acc, RT)

        def pool(j, s):
            v = get_lanes(j * 128, 128).reshape(8, 2, 8, C)
            c0, c1 = v[:, 0], v[:, 1]
            d = c0 - c1
            p = jnp.maximum(c0, c1) + jnp.log(1.0 + jnp.exp(-jnp.abs(d)))
            to = pl.ds(al(i * (RT // 2) + j * 64, 64), 64)
            POOL[to, :] = p.reshape(64, C)
            DIFF[to, :] = d.reshape(64, C)
            return s + jnp.sum(p, axis=0)

        SUM[...] += lax.fori_loop(0, RT // 128, pool, jnp.zeros((8, C), F32))

    NT = HR // RT

    def conv_loop(i, _):
        conv_tile(i)
        return 0

    lax.fori_loop(1, NT - 1, conv_loop, 0)
    h_halo.wait_from_up()
    h_halo.wait_from_down()
    by_one_bin(H0, H1)
    lax.fori_loop(0, 2, lambda i, _: (conv_tile(i * (NT - 1)), 0)[1], 0)

    mean = row_sum(SUM[...]) / float(PR)

    def m2_mid(i, acc):
        v = POOL[pl.ds(al(i * 128, 128), 128), :].reshape(16, 8, C) - mean
        return acc + jnp.sum(v * v, axis=0)

    acc = lax.fori_loop(0, PR // 128, m2_mid, jnp.zeros((8, C), F32))
    ex_mid[0].start(jnp.concatenate([mean, row_sum(acc)], axis=0))

    ld_cot.wait()
    x_cot.wait_recv()

    def turn_ct(i, _):
        turn(lambda h, row: COT[h][pl.ds(al(row * S + i * BB, BB), BB), :], CT, i)
        return 0

    lax.fori_loop(0, S // BB, turn_ct, 0)
    ld_pw.wait()
    x_pw.wait_recv()
    GT, DO, E0 = part("GT"), part("DO"), part("E0")
    E1, GML = part("GM"), [part("GM", 0, PR), part("GM", PR, PR)]

    def make_gt(i, _):
        at = pl.ds(al(i * 256, 256), 256)
        GT[at, :] = dot(CT[at, :], PW[...], 1, 1)
        return 0

    lax.fori_loop(0, PR // 256, make_gt, 0)
    for c in ld_d:
        c.wait()
    for c in x_d:
        c.wait_recv()

    def dt(k):
        return DT[k * HC : (k + 1) * HC, :]

    mu_mid, sq = finish_stats(ex_mid, float(PR))
    inv_mid = lax.rsqrt(sq / total_mid + EPSILON)
    gain_mid, shift_mid = vec(2), vec(3)
    scale_mid = gain_mid * inv_mid

    def make_mid(i, _):
        at = pl.ds(al(i * 128, 128), 128)
        HM[at, :] = gelu_up((POOL[at, :] - mu_mid) * scale_mid + shift_mid).astype(BF)
        return 0

    lax.fori_loop(0, PR // 128, make_mid, 0)

    RS = [part("RS", 0, rim), part("RS", rim, rim)]
    RR = [part("RR", 0, rim), part("RR", rim, rim)]
    p_rims = Rims(RS[1], RR[1], RS[0], RR[0], 2)
    QR = PR // 4
    e0_at, e1_at, do_at, hm_at = spans["E0"][1], spans["GM"][1], spans["DO"][1], spans["HM"][1]

    def pick(i, table):
        v = jnp.int32(table[-1])
        for n in range(len(table) - 2, -1, -1):
            v = jnp.where(i == n, table[n], v)
        return v

    quarter = (3, 2, 0, 1, 0, 1, 2, 3, 0, 1, 2, 3)
    taps_of = (0, 0, 2, 2, 0, 0, 2, 2, 1, 1, 1, 1)
    starts = [{0: e0_at + rim, 1: do_at, 2: e1_at}[k] + q * QR for k, q in zip(taps_of, quarter)]

    def product(i, _):
        v = dot(
            r.M[pl.ds(al(hm_at + pick(i, quarter) * QR, 16), QR), :],
            r.M[pl.ds(al(dt0 + pick(i, taps_of) * HC, 16), HC), :],
            1, 1,
        )
        r.F[pl.ds(al(pick(i, starts), 8), QR), :] = v

        @pl.when(i == 1)
        def _():
            RS[0][...] = E0[PR : PR + rim, :].astype(BF)
            p_rims.start_up()

        @pl.when(i == 3)
        def _():
            RS[1][...] = E1[0:rim, :].astype(BF)
            p_rims.start_down()

        return 0

    lax.fori_loop(0, len(quarter), product, 0)

    def take_rims(rims, low, high):
        rims.wait_from_down()
        rims.wait_from_up()

        @pl.when(has_down)
        def _():
            low[...] = RR[0][...].astype(F32)

        @pl.when(jnp.logical_not(has_down))
        def _():
            low[...] = jnp.zeros((rim, HC), F32)

        @pl.when(has_up)
        def _():
            high[...] = RR[1][...].astype(F32)

        @pl.when(jnp.logical_not(has_up))
        def _():
            high[...] = jnp.zeros((rim, HC), F32)

    take_rims(p_rims, part("E0", 0, rim), part("GM", PR, rim))

    def same(i, by):
        def pick(off):
            return SEGX[pl.ds(al(i * 256 + BIN0 + off * 16, 16), 256), :].reshape(16, 2, 8, 128)[:, 0]

        return wide(jnp.where(pick(0) == pick(by), 1.0, 0.0).reshape(128, 128), HC // 128)

    def add_dil(i, s):
        at = pl.ds(al(i * 128, 128), 128)
        v = DO[at, :]
        v += same(i, -DIL) * E0[pl.ds(al(i * 128 + 8, 8), 128), :]
        v += same(i, DIL) * E1[pl.ds(al(i * 128 + DIL * 8, 8), 128), :]
        DO[at, :] = v
        return s + jnp.sum(v.reshape(16, 8, HC), axis=0)

    acc = lax.fori_loop(0, PR // 128, add_dil, jnp.zeros((8, HC), F32))
    mean = row_sum(acc) / float(PR)

    def m2_hid(i, acc):
        v = DO[pl.ds(al(i * 128, 128), 128), :].reshape(16, 8, HC) - mean
        return acc + jnp.sum(v * v, axis=0)

    acc = lax.fori_loop(0, PR // 128, m2_hid, jnp.zeros((8, HC), F32))
    ex_hid[0].start(jnp.concatenate([mean, row_sum(acc)], axis=0))
    mu_hid, sq = finish_stats(ex_hid, float(PR))
    inv_hid = lax.rsqrt(sq / total_mid + EPSILON)
    gain_hid, shift_hid = hvec(4), hvec(5)
    HT = part("HT")

    def make_top(i, s):
        at = pl.ds(al(i * 128, 128), 128)
        xhat = (DO[at, :] - mu_hid) * inv_hid
        h, slope = gelu_both(xhat * gain_hid + shift_hid)
        HT[at, :] = h.astype(BF)
        da = slope * GT[at, :]
        GT[at, :] = da
        DO[at, :] = xhat
        return (
            s[0] + jnp.sum((da * xhat).reshape(16, 8, HC), axis=0),
            s[1] + jnp.sum(da.reshape(16, 8, HC), axis=0),
        )

    zero = jnp.zeros((8, HC), F32)
    sg, sb = lax.fori_loop(0, PR // 128, make_top, (zero, zero))
    ex_bh[0].start(jnp.concatenate([row_sum(sg), row_sum(sb)], axis=0))

    OB = 256

    def make_out(i, _):
        at = pl.ds(al(i * OB, OB), OB)
        v = (POOL[at, :] + dot(HT[at, :], PW[...], 1, 0)).astype(BF)
        COT[0][at, :] = v[:, :CH]
        COT[1][at, :] = v[:, CH:]
        return 0

    lax.fori_loop(0, PR // OB, make_out, 0)
    cot_other = r.N.at[pl.ds(al(spans["COTR"][1] + other * PR, 16), PR)]
    o_own = local(cot_mine, r.oOUT.at[m], 14)
    o_own.start()
    o_cross = cross(cot_other, r.oOUT.at[m], 12)
    o_cross.start()
    gp = dot(HT[...], CT[...], 0, 0)
    N[dpr_at + C : dpr_at + C + HC, :] = jnp.where(m == 0, gp[:, :CH], gp[:, CH:]).astype(BF)
    N[dps_at + C : dps_at + C + HC, :] = jnp.where(m == 0, gp[:, CH:], gp[:, :CH]).astype(BF)
    share_pw.copy().start()

    v = finish_sums(ex_bh, lambda: (share_pw.sum(), pump("bh")))
    ST[8:10, 0:HC] = v
    ST[8:10, HC:] = jnp.zeros((2, C - HC), F32)
    scale = gain_hid * inv_hid
    mg, mb = v[0:1] / total_mid, v[1:2] / total_mid
    GD = [part("GD", k * PR, PR) for k in range(3)]

    def make_gd(i, _):
        at = pl.ds(al(i * 128, 128), 128)
        g = (scale * (GT[at, :] - mb - DO[at, :] * mg)).astype(BF)
        GD[1][at, :] = g
        E0[pl.ds(al(i * 128 + rim, 16), 128), :] = g.astype(F32)
        return 0

    lax.fori_loop(0, PR // 128, make_gd, 0)
    p_rims.drain()
    g_rims = Rims(part("GD", PR, rim), RR[1], part("GD", 2 * PR - rim, rim), RR[0], 4)
    g_rims.start_up()
    g_rims.start_down()


    def to_gm(make, add):
        def body(i, _):
            at = pl.ds(al(i * QR, QR), QR)
            v = make(at)
            for h in range(2):
                u = v[:, h * CH : (h + 1) * CH]
                GML[h][at, :] = GML[h][at, :] + u if add else u
            return 0

        lax.fori_loop(0, 4, body, 0)

    to_gm(lambda at: dot(GD[1][at, :], dt(1), 1, 0), False)
    gd_at = spans["GD"][1]

    def dil_grad(k, to):
        g = dot(N[pl.ds(al(gd_at + k * PR, 16), PR), :], HM[...], 0, 0)
        own = jnp.where(m == 0, g[:HH], g[HH:]).astype(BF)
        for_partner = jnp.where(m == 0, g[HH:], g[:HH]).astype(BF)
        for h in range(2):
            at = to + h * HH
            N[pl.ds(al(dpr_at + at, 16), HH), :] = own[:, h * CH : (h + 1) * CH]
            N[pl.ds(al(dps_at + at, 16), HH), :] = for_partner[:, h * CH : (h + 1) * CH]

    dil_grad(1, C + CH)
    share_mid.copy().start()
    pump("center")
    share_mid.sum()
    pump("center2")
    take_rims(g_rims, part("E0", 0, rim), part("E0", PR + rim, rim))
    pump("rims")

    def mask_gd(i, _):
        at = pl.ds(al(i * 128, 128), 128)
        GD[0][at, :] = (same(i, DIL) * E0[pl.ds(al(i * 128 + rim + DIL * 8, 8), 128), :]).astype(BF)
        GD[2][at, :] = (same(i, -DIL) * E0[pl.ds(al(i * 128 + rim - DIL * 8, 8), 128), :]).astype(BF)
        return 0

    lax.fori_loop(0, PR // 128, mask_gd, 0)
    to_gm(lambda at: dot(GD[0][at, :], dt(0), 1, 0) + dot(GD[2][at, :], dt(2), 1, 0), True)

    def gm(at):
        return jnp.concatenate([GML[0][at, :], GML[1][at, :]], axis=1)

    def make_dmid(i, s):
        at = pl.ds(al(i * 64, 64), 64)
        xhat = (POOL[at, :] - mu_mid) * inv_mid
        _, slope = gelu_both(xhat * gain_mid + shift_mid)
        da = slope * gm(at)
        GML[0][at, :] = da[:, :CH]
        GML[1][at, :] = da[:, CH:]
        return (
            s[0] + jnp.sum((da * xhat).reshape(8, 8, C), axis=0),
            s[1] + jnp.sum(da.reshape(8, 8, C), axis=0),
        )

    zero = jnp.zeros((8, C), F32)
    sg, sb = lax.fori_loop(0, PR // 64, make_dmid, (zero, zero))
    g_rims.drain()
    o_own.wait()
    o_cross.wait_send()
    keep_x.wait()
    ex_bm[0].start(jnp.concatenate([row_sum(sg), row_sum(sb)], axis=0))

    lax.fori_loop(0, 2, lambda i, _: (dil_grad(2 * i, i * CH), 0)[1], 0)
    share_rest.copy().start()
    v = finish_sums(ex_bm, lambda: (share_rest.sum(), pump("bm")))
    ST[6:8, :] = v
    mg, mb = v[0:1] / total_mid, v[1:2] / total_mid
    pump("bm2")
    GC0, GC1 = part("GC0"), H1

    def make_gc(i, last):
        at = pl.ds(al(i * 64, 64), 64)
        xhat = (POOL[at, :] - mu_mid) * inv_mid
        g = CT[at, :].astype(F32) + scale_mid * (gm(at) - mb - xhat * mg)
        d = DIFF[at, :]
        e = jnp.exp(-jnp.abs(d))
        big = 1.0 / (1.0 + e)
        small = e * big
        g0 = g * jnp.where(d >= 0, big, small)
        g1 = g * jnp.where(d >= 0, small, big)
        v = jnp.stack([g0.reshape(8, 8, C), g1.reshape(8, 8, C)], axis=1).reshape(128, C)
        GC0[pl.ds(al(i * 128 + 16, 16), 128), :] = v.astype(BF)
        GC1[pl.ds(al(i * 128, 128), 128), :] = jnp.concatenate([last, v[:120]], axis=0).astype(BF)
        return v[120:]

    lax.fori_loop(0, PR // 64, make_gc, jnp.zeros((8, C), F32))
    g_halo = halos(GC0, 6)
    g_halo.start_down()
    g_halo.start_up()
    clear_halo(GC0)
    XX = part("XX")
    back_x = local(r.oX, XX, 13)

    own_at = spans["GM"][1]
    h0_at = spans["H0"][1] + 16
    ps_at = spans["PS"][1]
    HALF = C // 2
    first_half = (1 - bits[0]) * HALF

    def tap_share(i, j):
        at = first_half if j == 0 else HALF - first_half
        own = lambda: r.F[pl.ds(al(own_at + i % 2 * PR + at, 8), HALF), :]
        return Share(2 * i + j, ps_at + i % PSLOTS * C + at, spans[f"F{i}"][1] + at, own, r_at + i * C + at, HALF)

    shares = [tap_share(i, j) for i in range(TAPS) for j in range(2)]

    def masked(k):
        def body(j, _):
            XX[pl.ds(al(j * 256, 256), 256), :] = shifted(GC0, GC1, 2 - k, j * 256, 256)
            return 0

        lax.fori_loop(0, HR // 256, body, 0)

    def half_tap(it, _):
        i, j = it // 2, lax.rem(it, 2)
        for n in range(TAPS):

            @pl.when(it == 2 * n)
            def _(n=n):
                if n == 1:
                    g_halo.wait_from_up()
                    g_halo.wait_from_down()
                    by_one_bin(GC0, GC1)
                if n >= PSLOTS:
                    for c in shares[2 * (n - PSLOTS) : 2 * (n - PSLOTS) + 2]:
                        c.copy().wait_send()
                masked(ORDER[n])

        odd = lax.rem(i, 2)
        at = jnp.where(j == 0, first_half, HALF - first_half)
        v = dot(r.M[h0_at : h0_at + HR, pl.ds(al(at, 128), HALF)], XX[...], 0, 0)
        r.F[pl.ds(al(own_at + odd * PR + at, 8), HALF), :] = jnp.where(m == 0, v[:, :CH], v[:, CH:])
        N[pl.ds(al(ps_at + lax.rem(i, PSLOTS) * C + at, 16), HALF), :] = jnp.where(m == 0, v[:, CH:], v[:, :CH]).astype(BF)
        for n in range(2 * TAPS):

            @pl.when(it == n)
            def _(n=n):
                shares[n].copy().start()
                if n:
                    shares[n - 1].sum()
                pump(f"tap{n}")

        return 0

    lax.fori_loop(0, 2 * TAPS, half_tap, 0)
    shares[-1].sum()
    pump("taps")

    back_x.start()
    for c in shares[2 * (TAPS - PSLOTS) :]:
        c.copy().wait_send()
    mu, inv, gain, shift = ST[0:1, :], ST[1:2, :], gain_in, shift_in
    RB = 256
    DA = [part("RAW", 0, HR), part("RAW", HR, HR)]

    def tile(i, s):
        at = i * RB
        acc = None
        for k in range(TAPS):
            d = dot(shifted(GC0, GC1, 2 - k, at, RB), w(k), 1, 1)
            acc = d if acc is None else acc + d
        put_lanes(acc, RB)
        for n in range(HR // RB):

            @pl.when(i == n)
            def _(n=n):
                pump(f"tile{2 * n}")
                if n == 0:
                    back_x.wait()


        def back(j, s):
            to = pl.ds(al(at + j * 64, 64), 64)
            xhat = (XX[to, :].astype(F32) - mu) * inv
            _, slope = gelu_both(xhat * gain + shift)
            da = slope * get_lanes(j * 64, 64)
            DA[0][to, :] = da[:, :CH].astype(BF)
            DA[1][to, :] = da[:, CH:].astype(BF)
            return (
                s[0] + jnp.sum((da * xhat).reshape(8, 8, C), axis=0),
                s[1] + jnp.sum(da.reshape(8, 8, C), axis=0),
            )

        s = lax.fori_loop(0, RB // 64, back, s)
        for n in range(HR // RB):

            @pl.when(i == n)
            def _(n=n):
                pump(f"tile{2 * n + 1}")

        return s

    s = lax.fori_loop(0, HR // RB, tile, (zero, zero))
    ex_bi[0].start(jnp.concatenate([row_sum(s[0]), row_sum(s[1])], axis=0))
    d_own = local(raw_mine, r.oDA.at[m], 12)
    d_own.start()
    d_cross = cross(r.N.at[pl.ds(al(spans["RAW"][1] + other * HR, 16), HR)], r.oDA.at[m], 13)
    d_cross.start()
    pump("end0")
    ex_bi[1].start(functools.reduce(jnp.add, ex_bi[0].wait()))
    pump("end1")
    ST[4:6, :] = functools.reduce(jnp.add, ex_bi[1].wait())
    ST[3:4, :] = jnp.zeros((1, C), F32)
    ST[10:16, :] = jnp.zeros((6, C), F32)
    o_st = local(ST, r.oST, 14)
    o_st.start()
    for pc in pieces:
        pc.drain()
    for c in (share_rest, share_pw, share_mid):
        c.copy().wait_send()
    d_own.wait()
    o_st.wait()
    d_cross.wait()
    o_cross.wait_recv()
    for c in crosses:
        c.wait_send()
    for e in exchanges:
        e[0].drain()
        e[1].drain()
    h_halo.drain()
    g_halo.drain()


def call_main(axes, sig, seg, cot, wide_taps, taps, pw, vectors):
    nb, nm, na = axes
    CH = sig.shape[1]
    C = 2 * CH
    HC = pw.shape[0]
    assert HC == CH
    HR = sig.shape[0] // 2
    PR = cot.shape[0] // 2
    T, S = HR // ROWS, PR // ROWS
    rim = (DIL + 1) * ROWS
    RT = 512
    NA = nm * na
    early = nb == 4
    NP = 3 * (TAPS + 1) + (2 if early else 1)
    inputs = dict(sig=sig, seg=seg, cot=cot, wide=wide_taps, taps=taps, pw=pw)
    inputs.update({f"v{i}": v for i, v in enumerate(vectors)})
    sd = jax.ShapeDtypeStruct
    outs = dict(
        oX=sd((HR, C), BF),
        oDA=sd((2, HR, CH), BF),
        oOUT=sd((2, PR, CH), BF),
        oR=sd((TAPS, C, CH), BF),
        oDP=sd((2 * C, CH), BF),
        oST=sd((16, C), F32),
    )
    spans = {}

    def lay(pool, start, items):
        for name, n in items:
            spans[name] = (pool, start, n)
            start += n
        return start

    end = lay("N", 0, [("RAW", 2 * HR), ("STO", HR), ("COTR", 2 * PR), ("HT", PR), ("RS", 2 * rim), ("RR", 2 * rim)])
    lay("N", spans["STO"][1], [("DPS", 2 * C)])
    lay("N", spans["COTR"][1], [(f"XB{p}", C // 2) for p in range(TAPS)])
    lay("N", spans["HT"][1], [(f"YB{p}", C // 4) for p in range(TAPS)])
    lay("N", spans["RS"][1], [(f"F{p}", C) for p in range(2)])
    end = lay("N", end, [("GD", 3 * PR)])
    lay("N", spans["GD"][1], [("R", (TAPS + 2) * C)])
    end = max(end, spans["R"][1] + (TAPS + 2) * C)
    end = lay("N", end, [(f"F{p}", C) for p in range(2, TAPS)] + [("FD", 2 * C)])
    lay("N", spans["RAW"][1] + HR, [("PS", 2 * C)])
    sizes = {p: C for p in range(TAPS + 1)} | ({6: CH, 7: CH} if early else {6: C})
    rest = range(TAPS, len(sizes))
    end = lay("N", end, [(f"XB{p}", sizes[p] // 2) for p in rest] + [(f"YB{p}", sizes[p] // 4) for p in rest])
    n_rows = lay("N", end, [(f"ZB{p}", C // 2 if p > 5 and early else C // 4) for p in range(len(sizes))])
    end = lay("M", 0, [("X", HR), ("gap", 32), ("HM", PR), ("CT", PR), ("H0", HR + 32), ("H1", HR + 32)])
    lay("M", 0, [("GC0", HR + 32)])
    lay("M", spans["HM"][1], [("XX", HR)])
    m_rows = lay("M", end, [("W", TAPS * C), ("PW", HC), ("DT", 3 * HC)])
    f_rows = lay("F", 0, [("E0", PR + 2 * rim), ("GM", 2 * PR), ("DO", PR), ("GT", PR)])
    V = pltpu.VMEM
    DMA = pltpu.SemaphoreType.DMA
    scratch = dict(
        N=V((n_rows, CH), BF),
        M=V((m_rows, C), BF),
        F=V((f_rows, CH), F32),
        LANES=V((C // 128 * RT, 128), F32),
        MASK=V((4, HR, 128), BF),
        SEG=V(seg.shape, jnp.int32),
        SEGX=V(((T + 256) * ROWS, 128), F32),
        PAR=V((2, 8, CH), F32),
        ST=V((16, C), F32),
        SUM=V((8, C), F32),
        POOL=V((PR, C), F32),
        DIFF=V((PR, C), F32),
        XIA=V((NA, 2, CH), F32), XIB=V((nb, 2, C), F32),
        XMA=V((NA, 2, C), F32), XMB=V((nb, 2, C), F32),
        XHA=V((NA, 2, HC), F32), XHB=V((nb, 2, HC), F32),
        XGA=V((NA, 2, HC), F32), XGB=V((nb, 2, HC), F32),
        XDA=V((NA, 2, C), F32), XDB=V((nb, 2, C), F32),
        XSA=V((NA, 2, C), F32), XSB=V((nb, 2, C), F32),
        lsem=DMA((15 + NP,)),
        shs=DMA((13,)), shr=DMA((13,)),
        csem_s=DMA((14,)), csem_r=DMA((14,)),
        as_=DMA((6, NA)), ar_=DMA((6, NA)),
        bs_=DMA((6, nb)), br_=DMA((6, nb)),
        hs=DMA((8,)), hr=DMA((8,)),
        ps=DMA((NP, 6)), pr=DMA((NP, 6)),
        zs=DMA((NP, 2, 4)), zr=DMA((NP, 2, 4)),
    )
    outer = nb // 4
    if outer > 1:
        scratch.update(os_=DMA((NP, outer)), or_=DMA((NP, outer)))
        n = outer * (C // 16)
        assert lay("F", spans["E0"][1], [(f"OB{p}", n) for p in range(TAPS)]) <= spans["GM"][1]
        assert lay("F", spans["DO"][1], [(f"OB{p}", n) for p in range(TAPS, TAPS + 2)]) <= f_rows
    names = list(inputs) + list(outs) + list(scratch)
    anyspec = pl.BlockSpec(memory_space=pl.ANY)
    vmem = pl.BlockSpec(memory_space=pltpu.VMEM)
    res = pl.pallas_call(
        functools.partial(main_body, (nb, nm, na, T, S, CH, HC), names, spans),
        out_shape=list(outs.values()),
        in_specs=[vmem if n.startswith("v") else anyspec for n in inputs],
        out_specs=[anyspec] * len(outs),
        scratch_shapes=list(scratch.values()),
        compiler_params=pltpu.CompilerParams(
            collective_id=0, has_side_effects=True, vmem_limit_bytes=VMEM_BYTES
        ),
        cost_estimate=pl.CostEstimate(flops=44_000_000_000, bytes_accessed=40_000_000, transcendentals=8_000_000),
        name="forward_and_backward",
    )(*inputs.values())
    return dict(zip(outs, res, strict=True))


def last_body(dims, sig, da, out, rr, dk0, dk1, pw, stats, gs_ref, out_ref, gw_ref, dk_ref, pw_ref,
              g0, g1, g2, g3, g4, g5, lanes, lanes2):
    CH, total_in = dims
    m = lax.axis_index("mp")
    step = pl.program_id(0)
    n = da.shape[1]
    BB = n // ROWS
    v = da[0].astype(F32)
    u = out[0].astype(F32)
    n2 = out.shape[1]
    B2 = n2 // ROWS
    for j in range(CH // 128):
        lanes[j * n : (j + 1) * n, :] = v[:, j * 128 : (j + 1) * 128]
        lanes2[j * n2 : (j + 1) * n2, :] = u[:, j * 128 : (j + 1) * 128]
    st = stats[:, pl.ds(al(m * CH, CH), CH)]
    mu, inv, gain, gg, gb = [st[i : i + 1] for i in (0, 1, 2, 4, 5)]
    scale = gain * inv
    mg, mb = gg / total_in, gb / total_in
    for row in range(ROWS):
        for j in range(CH // 128):
            c = slice(j * 128, (j + 1) * 128)
            d = lanes[pl.ds(j * n + row, BB, stride=ROWS), :]
            xhat = (sig[row, :, c].astype(F32) - mu[:, c]) * inv[:, c]
            gs_ref[row, :, c] = scale[:, c] * (d - mb[:, c] - xhat * mg[:, c])
            out_ref[row, :, c] = lanes2[pl.ds(j * n2 + row, B2, stride=ROWS), :].astype(BF)
    gw_ref[...] = rr[...].astype(F32)
    dk_ref[...] = jnp.concatenate([dk0[...].astype(F32), dk1[...].astype(F32)], axis=1)
    pw_ref[...] = pw[...].astype(F32)

    @pl.when(step == 0)
    def _():
        for ref, i in ((g0, 4), (g1, 5), (g2, 6), (g3, 7)):
            ref[...] = st[i : i + 1].reshape(CH)
        HH = g4.shape[0]
        hid = stats[8:10, : 2 * HH]
        hid = jnp.where(m == 0, hid[:, :HH], hid[:, HH:])
        g4[...] = hid[0:1].reshape(HH)
        g5[...] = hid[1:2].reshape(HH)


def call_last(axes, sig, o):
    nb, nm, na = axes
    rows, T, CH = sig.shape
    S = T // 2
    C = 2 * CH
    HC = CH
    HH = HC // 2
    NC = 4
    steps = 2 * NC
    sd = jax.ShapeDtypeStruct
    total_in = float(rows * T * nb * na)
    rr = o["oR"].reshape(-1, CH)
    dp = o["oDP"]
    flat = lambda n, w: pl.BlockSpec((n, w), lambda i: (i, 0))
    whole1 = pl.BlockSpec(memory_space=pltpu.VMEM)
    nr, npw, nd = rr.shape[0] // steps, HC // steps, HH
    tap_of = lambda i: jnp.minimum(i // 2, 2)
    base = lambda i: jnp.where(tap_of(i) == 1, 6, tap_of(i))
    return pl.pallas_call(
        functools.partial(last_body, (CH, total_in)),
        grid=(steps,),
        out_shape=[
            sd((rows, T, CH), F32),
            sd((rows, S, CH), BF),
            sd(rr.shape, F32),
            sd((3 * HH, C), F32),
            sd((HC, CH), F32),
            *[sd((CH,), F32)] * 4,
            *[sd((HH,), F32)] * 2,
        ],
        in_specs=[
            pl.BlockSpec((ROWS, T // NC, CH), lambda i: (i // NC, i % NC, 0)),
            pl.BlockSpec((1, T * ROWS // NC, CH), lambda i: (i // NC, i % NC, 0)),
            pl.BlockSpec((1, S * ROWS // NC, CH), lambda i: (i // NC, i % NC, 0)),
            flat(nr, CH),
            pl.BlockSpec((nd, CH), lambda i: (base(i), 0)),
            pl.BlockSpec((nd, CH), lambda i: (base(i) + 1, 0)),
            pl.BlockSpec((npw, CH), lambda i: (4 * HH // npw + i, 0)),
            pl.BlockSpec((16, C), lambda i: (0, 0)),
        ],
        out_specs=[
            pl.BlockSpec((ROWS, T // NC, CH), lambda i: (i // NC, i % NC, 0)),
            pl.BlockSpec((ROWS, S // NC, CH), lambda i: (i // NC, i % NC, 0)),
            flat(nr, CH),
            pl.BlockSpec((nd, C), lambda i: (tap_of(i), 0)),
            flat(npw, CH),
            *[pl.BlockSpec((CH,), lambda i: (0,))] * 4,
            *[pl.BlockSpec((HH,), lambda i: (0,))] * 2,
        ],
        scratch_shapes=[
            pltpu.VMEM((CH // 128 * T * ROWS // NC, 128), F32),
            pltpu.VMEM((CH // 128 * S * ROWS // NC, 128), F32),
        ],
        compiler_params=pltpu.CompilerParams(vmem_limit_bytes=VMEM_BYTES),
        name="last_pass",
    )(sig, o["oDA"], o["oOUT"], rr, dp, dp, dp, o["oST"])


def on_device(axes, signal, seg, cotangent, conv_wide, taps, pointwise, *vectors):
    CH = signal.shape[2]
    o = call_main(
        axes, signal.reshape(-1, CH), seg, cotangent.reshape(-1, CH), conv_wide, jnp.swapaxes(taps, 1, 2), pointwise, vectors
    )
    gs, out, gw, dk, pw, *small = call_last(axes, signal, o)
    K, C, HH = taps.shape
    return (out, gs, gw.reshape(conv_wide.shape), jnp.swapaxes(dk.reshape(K, HH, C), 1, 2), pw, *small)


def solution(mesh):
    axes = (mesh.shape["bins"], mesh.shape["mp"], mesh.shape["batch"])
    cut = P("batch", "bins", "mp")
    tap = P(None, None, "mp")
    return jax.shard_map(
        functools.partial(on_device, axes),
        mesh=mesh,
        in_specs=(cut, P("batch", None), cut, tap, tap, P(None, "mp")) + (P("mp"),) * 6,
        out_specs=(cut, cut, tap, tap, P(None, "mp")) + (P("mp"),) * 6,
        check_vma=False,
    )
```

```python
import functools
import types

import jax
import jax.numpy as jnp
from jax import lax
from jax.experimental import pallas as pl
from jax.experimental.pallas import tpu as pltpu
from jax.sharding import PartitionSpec as P

DIL = 57
EPSILON = 1e-05
TAPS = 5
BF = jnp.bfloat16
F32 = jnp.float32
MESH = pl.DeviceIdType.MESH
K0 = 0.7978845608028654
K3 = 0.044715
ROWS = 8
VMEM_BYTES = 63 * 2**20


def gelu_up(x):
    t = jnp.tanh(x * (K0 + (K0 * K3) * (x * x)))
    h = 0.5 * x
    return h + h * t


def gelu_both(x):
    x2 = x * x
    t = jnp.tanh(x * (K0 + (K0 * K3) * x2))
    h = 0.5 * x
    return h + h * t, 0.5 + 0.5 * t + h * (1.0 - t * t) * (K0 + (3.0 * K0 * K3) * x2)


def dot(a, b, ca, cb):
    return lax.dot_general(a, b, (((ca,), (cb,)), ((), ())), preferred_element_type=F32)


def wide(mask, times):
    return jnp.concatenate([mask] * times, axis=1)


def al(x, n):
    return pl.multiple_of(x, n)


class Place:
    def __init__(self, nb, nm, na):
        self.nb, self.nm, self.na = nb, nm, na
        self.b = lax.axis_index("bins")
        self.m = lax.axis_index("mp")
        self.a = lax.axis_index("batch")
        self.layer = nm * na
        self.q = self.m * na + self.a

    def in_layer(self, q):
        return (self.b, q // self.na, lax.rem(q, self.na))

    def in_bins(self, b):
        return (b, self.m, self.a)

    @property
    def partner(self):
        return (self.b, 1 - self.m, self.a)

    def others(self, me, n):
        return [lax.rem(me + i, n) for i in range(1, n)]


def remote(src, dst, ss, rs, dev):
    return pltpu.make_async_remote_copy(
        src_ref=src, dst_ref=dst, send_sem=ss, recv_sem=rs, device_id=dev, device_id_type=MESH
    )


class Exchange:
    def __init__(self, buf, me, n, dev_of, ss, rs, others):
        self.buf, self.me, self.n, self.dev_of, self.ss, self.rs, self.others = (
            buf, me, n, dev_of, ss, rs, others,
        )

    def start(self, value):
        self.buf[self.me] = value
        for q in self.others:
            remote(self.buf.at[self.me], self.buf.at[self.me], self.ss.at[q], self.rs.at[self.me], self.dev_of(q)).start()

    def wait(self):
        for q in self.others:
            remote(self.buf.at[q], self.buf.at[q], self.ss.at[q], self.rs.at[q], self.dev_of(q)).wait_recv()
        return [self.buf[i] for i in range(self.n)]

    def drain(self):
        for q in self.others:
            remote(self.buf.at[self.me], self.buf.at[self.me], self.ss.at[q], self.rs.at[q], self.dev_of(q)).wait_send()


def merged(parts, count):
    means = [p[0:1] for p in parts]
    total = functools.reduce(jnp.add, means)
    mean = total / len(parts)
    squares = functools.reduce(jnp.add, [p[1:2] for p in parts])
    apart = functools.reduce(jnp.add, [(x - mean) * (x - mean) for x in means])
    return mean, squares + count * apart


def row_sum(x):
    return jnp.sum(x, axis=0, keepdims=True)


def greet(place):
    barrier = pltpu.get_barrier_semaphore()
    devices = [place.in_layer(q) for q in place.others(place.q, place.layer)]
    devices += [place.in_bins(b) for b in place.others(place.b, place.nb)]
    for d in devices:
        pl.semaphore_signal(barrier, inc=1, device_id=d, device_id_type=MESH)
    pl.semaphore_wait(barrier, len(devices))


PLAN = (
    ("bh", [18]),
    ("center", [18]),
    ("center2", [19]),
    ("rims", [18]),
    ("bm", [19, 15, 16, 17]),
    ("bm2", [18]),
    ("tap0", [19, 15, 16, 17]),
    ("tap1", [18, 0, 2]),
    ("tap2", [1]),
    ("tap3", [15, 16, 17, 4]),
    ("tap4", [3, 5]),
    ("tap5", [18, 1, 6, 8]),
    ("tap6", [19, 0, 15, 7]),
    ("tap7", [16, 2, 3, 10]),
    ("tap8", [17, 4, 5, 9, 11]),
    ("tap9", [1, 0, 15, 12, 14]),
    ("taps", [6, 7, 16, 13]),
    ("tile0", [2, 8, 4, 17]),
    ("tile1", [19]),
    ("tile2", [1, 9, 3, 0]),
    ("tile3", [11]),
    ("tile4", [10, 6, 2, 5]),
    ("tile5", [16, 4, 15]),
    ("tile6", [1, 13, 12]),
    ("tile7", [3, 8]),
    ("tile8", [0, 14, 6]),
    ("tile9", [7, 2, 19]),
    ("tile10", [17, 5, 10, 9, 4]),
    ("tile11", [11]),
    ("tile12", [3, 15, 8, 12, 16]),
    ("tile13", [6, 0]),
    ("tile14", [1, 7, 14, 13, 5, 2]),
    ("tile15", [10, 3]),
    ("end0", [9, 17, 11, 4, 0, 8, 6, 5, 12, 7, 1, 2, 14]),
    ("end1", [13, 3, 4, 10, 8, 9, 6, 11, 5, 7, 12, 10, 14, 8, 13, 9, 11, 7, 12, 10, 14, 13, 9, 12, 11, 14, 13]),
)


def main_body(dims, names, spans, *refs):
    nb, nm, na, T, S, CH, HC = dims
    C = 2 * CH
    HR = T * ROWS
    PR = S * ROWS
    rim = (DIL + 1) * ROWS
    r = types.SimpleNamespace(**dict(zip(names, refs, strict=True)))
    place = Place(nb, nm, na)
    b, m, a = place.b, place.m, place.a
    other = 1 - m
    total_in = float(HR * nb * nm * na)
    total_mid = float(PR * nb * nm * na)
    LANES = r.LANES
    RT = LANES.shape[0] // (C // 128)

    def part(name, at=0, n=None):
        pool, start, rows = spans[name]
        return getattr(r, pool).at[pl.ds(start + at, rows if n is None else n)]

    def local(src, dst, i):
        return pltpu.make_async_copy(src, dst, r.lsem.at[i])

    def cross(src, dst, i):
        return remote(src, dst, r.csem_s.at[i], r.csem_r.at[i], place.partner)

    RAW, STO, X, CT, HM = part("RAW"), part("STO"), part("X"), part("CT"), part("HM")
    H0, H1, W, PW, DT = part("H0"), part("H1"), part("W"), part("PW"), part("DT")
    COT = [part("COTR", 0, PR), part("COTR", PR, PR)]
    vectors = [r.v0, r.v1, r.v2, r.v3, r.v4, r.v5]
    PAR, SEG, SEGX, MASK, ST = r.PAR, r.SEG, r.SEGX, r.MASK, r.ST
    half = lambda at, n: pl.ds(al(at + m * n, n), n)

    sig, cot = r.sig, r.cot
    mine, theirs = pl.ds(al(m * HR, HR), HR), pl.ds(al(other * HR, HR), HR)
    raw_mine = r.N.at[pl.ds(al(spans["RAW"][1] + m * HR, 16), HR)]
    cot_mine = r.N.at[pl.ds(al(spans["COTR"][1] + m * PR, 16), PR)]
    lanes = pl.ds(al(m * CH, CH), CH)
    w0, pw0, dt0 = spans["W"][1], spans["PW"][1], spans["DT"][1]
    HH = HC // 2

    def weight(k):
        return r.M.at[pl.ds(w0 + k * C, C), lanes]

    def tap_rows(k):
        return r.M.at[pl.ds(al(dt0 + k * HC + m * HH, 16), HH)]

    pw_mine = r.M.at[pl.ds(pw0, HC), lanes]
    ld_sto = local(sig.at[theirs], STO, 0)
    ld_raw = local(sig.at[mine], raw_mine, 1)
    ld_seg = local(r.seg, SEG, 2)
    ld_w = [local(r.wide.at[k], weight(k), 3 + k) for k in range(TAPS)]
    ld_d = [local(r.taps.at[k], tap_rows(k), 8 + k) for k in range(3)]
    ld_pw = local(r.pw, pw_mine, 11)
    ld_cot = local(cot.at[pl.ds(al(m * PR, PR), PR)], cot_mine, 12)
    for c in [ld_sto, ld_raw, ld_seg, *ld_w, *ld_d, ld_pw, ld_cot]:
        c.start()
    for i in range(4):
        PAR[m, i : i + 1, :] = vectors[i][...].reshape(1, CH)
    for i in range(4, 6):
        PAR[m, i : i + 1, 0:HH] = vectors[i][...].reshape(1, HH)
    greet(place)
    x_sig = cross(sig.at[theirs], raw_mine, 0)
    x_par = cross(PAR.at[m], PAR.at[m], 1)
    x_w = [cross(r.wide.at[k], weight(k), 2 + k) for k in range(TAPS)]
    x_d = [cross(r.taps.at[k], tap_rows(k), 7 + k) for k in range(3)]
    x_pw = cross(r.pw, pw_mine, 10)
    x_cot = cross(cot.at[pl.ds(al(other * PR, PR), PR)], cot_mine, 11)
    crosses = [x_sig, x_par, *x_w, x_cot, x_pw, *x_d]
    for c in crosses:
        c.start()

    def exchange(i, name):
        return (
            Exchange(getattr(r, name + "A"), place.q, place.layer, place.in_layer, r.as_.at[i], r.ar_.at[i], place.others(place.q, place.layer)),
            Exchange(getattr(r, name + "B"), b, nb, place.in_bins, r.bs_.at[i], r.br_.at[i], place.others(b, nb)),
        )

    def finish_stats(ex, count):
        mean, squares = merged(ex[0].wait(), count)
        ex[1].start(jnp.concatenate([mean, squares], axis=0))
        return merged(ex[1].wait(), count * place.layer)

    def finish_sums(ex, between=lambda: None):
        ex[1].start(functools.reduce(jnp.add, ex[0].wait()))
        between()
        return functools.reduce(jnp.add, ex[1].wait())

    ex_in, ex_mid, ex_hid, ex_bh, ex_bm, ex_bi = exchanges = [
        exchange(i, n) for i, n in enumerate(["XI", "XM", "XH", "XG", "XD", "XS"])
    ]

    ps, pr, zs, zr = r.ps, r.pr, r.zs, r.zr
    N = r.N
    INNER = 4
    outer = nb // INNER
    inner = lax.rem(b, INNER)
    base = b - inner
    bits = (lax.rem(a, 2), a // 2)
    flip = ((b, m, a + 1 - 2 * bits[0]), (b, m, lax.rem(a + 2, 4)))
    early = outer == 1
    PSLOTS = spans["PS"][2] // C

    class Piece:
        def __init__(self, p, stack, lanes, first, n, R, F, full=False):
            self.p = p
            self.stack = stack
            self.lanes = pl.ds(*lanes)
            self.first = first
            self.n = n
            HALF, QUART = n // 2, n // 4
            self.SMALL = n // 16
            self.full = full
            self.steps = [0, 1, 2, 3, 5, 6] if full else [0, 1, 2, 3, 4, 5, 6]
            b1, b2 = bits[self.first], bits[1 - self.first]
            self.n1, self.n2 = flip[self.first], flip[1 - self.first]
            self.k1 = b1 * HALF
            self.s1 = (1 - b1) * HALF
            self.k2 = b1 * HALF + b2 * QUART
            self.s2 = b1 * HALF + (1 - b2) * QUART
            self.HALF, self.QUART = HALF, QUART
            self.R, self.F = R, F
            self.XB, self.YB, self.ZB = [spans[f"{x}{stack}"][1] for x in ("XB", "YB", "ZB")]

        def rows(self, start, at, n):
            return N.at[pl.ds(al(start + at, 16), n), self.lanes]

        def get(self, start, at, n):
            return N[pl.ds(al(start + at, 16), n), self.lanes].astype(F32)

        def put(self, start, at, n, v):
            N[pl.ds(al(start + at, 16), n), self.lanes] = v.astype(BF)

        def describe(self, make, i, dev):
            return lambda: remote(*make(), ps.at[self.p, i], pr.at[self.p, i], dev)

        def moves(self):
            F, R = self.F, self.R
            return {
                2: self.describe(lambda: (self.rows(R, self.s1, self.HALF), self.rows(self.XB, 0, self.HALF)), 2, self.n1),
                3: self.describe(lambda: (self.rows(R, self.s2, self.QUART), self.rows(self.YB, 0, self.QUART)), 3, self.n2),
                4: self.describe(lambda: (self.rows(F, self.k2, self.QUART),) * 2, 4, self.n2),
                5: self.describe(lambda: (self.rows(F, self.k1, self.HALF),) * 2, 5, self.n1),
            }

        def toward(self, which, i):
            j = lax.rem(inner + i, INNER)
            if self.full:
                src, dst = self.rows(self.R, self.k2, self.QUART), self.rows(self.ZB, inner * self.QUART, self.QUART)
            elif which == 0:
                src, dst = self.rows(self.R, self.k2 + j * self.SMALL, self.SMALL), self.rows(self.ZB, inner * self.SMALL, self.SMALL)
            else:
                src = dst = self.rows(self.F, self.k2 + inner * self.SMALL, self.SMALL)
            return remote(src, dst, zs.at[self.p, which, j], zr.at[self.p, which, inner], (base + j, m, a))

        def gather(self, which):
            for i in range(1, INNER):
                j = lax.rem(inner + i, INNER)
                if self.full:
                    ref = self.rows(self.ZB, j * self.QUART, self.QUART)
                else:
                    ref = self.rows(self.ZB, j * self.SMALL, self.SMALL) if which == 0 else self.rows(self.F, self.k2 + j * self.SMALL, self.SMALL)
                remote(ref, ref, zs.at[self.p, which, j], zr.at[self.p, which, j], (base + j, m, a)).wait_recv()

        def drain(self):
            for i in (2, 3, 4, 5):
                self.moves()[i]().wait_send()
            for which in range(1 if self.full else 2):
                for i in range(1, INNER):
                    self.toward(which, i).wait_send()
            if outer > 1:
                for i in range(1, outer):
                    self.outward(i).wait_send()
            self.out().wait()

        def outward(self, i):
            mine = b // INNER
            q = lax.rem(mine + i, outer)
            ref = r.F.at[self.slot(mine), self.lanes]
            return remote(ref, ref, r.os_.at[self.p, q], r.or_.at[self.p, mine], (q * INNER + inner, m, a))

        def slot(self, q):
            return pl.ds(al(spans[f"OB{self.stack}"][1] + q * self.SMALL, 8), self.SMALL)

        def out(self):
            k = self.stack
            to = r.oR.at[ORDER[k], :, self.lanes] if k < TAPS else r.oDP.at[pl.ds(self.F - dp_at, self.n), self.lanes]
            return local(self.rows(self.F, 0, self.n), to, 15 + self.p)

        def step(self, ph):
            p, moves = self.p, self.moves()
            HALF, QUART, SMALL = self.HALF, self.QUART, self.SMALL
            if ph == 0:
                moves[2]().start()
            elif ph == 1:
                moves[2]().wait_recv()
                self.put(self.R, self.k1, HALF, self.get(self.R, self.k1, HALF) + self.get(self.XB, 0, HALF))
                moves[3]().start()
            elif ph == 2:
                moves[3]().wait_recv()
                self.put(self.R, self.k2, QUART, self.get(self.R, self.k2, QUART) + self.get(self.YB, 0, QUART))
                for i in range(1, INNER):
                    self.toward(0, i).start()
            elif ph == 3:
                self.gather(0)
                n = QUART if self.full else SMALL
                at = self.k2 if self.full else self.k2 + inner * SMALL
                v = self.get(self.R, at, n)
                for i in range(1, INNER):
                    v += self.get(self.ZB, lax.rem(inner + i, INNER) * n, n)
                if outer > 1:
                    mine = b // INNER
                    r.F[self.slot(mine), self.lanes] = v
                    for i in range(1, outer):
                        self.outward(i).start()
                    for i in range(1, outer):
                        q = lax.rem(mine + i, outer)
                        ref = r.F.at[self.slot(q), self.lanes]
                        remote(ref, ref, r.os_.at[p, q], r.or_.at[p, q], (q * INNER + inner, m, a)).wait_recv()
                    v = r.F[self.slot(0), self.lanes]
                    for j in range(1, outer):
                        v += r.F[self.slot(j), self.lanes]
                self.put(self.F, at, n, v)
                if self.full:
                    moves[4]().start()
                else:
                    for i in range(1, INNER):
                        self.toward(1, i).start()
            elif ph == 4:
                self.gather(1)
                moves[4]().start()
            elif ph == 5:
                moves[4]().wait_recv()
                moves[5]().start()
            elif ph == 6:
                moves[5]().wait_recv()
                self.out().start()

    ORDER = (2, 1, 3, 0, 4)
    r_at, dp_at = spans["R"][1], spans["FD"][1]
    dps_at, dpr_at = spans["DPS"][1], r_at + TAPS * C
    thirds = [(q * CH // 3, CH // 3) for q in range(3)]
    pieces = []
    for k in range(TAPS + 1):
        for q in range(3):
            R, F = r_at + k * C, spans[f"F{k}"][1] if k < TAPS else dp_at
            pieces.append(Piece(len(pieces), k, thirds[q], (k + q) % 2, C, R, F))
    late = len(pieces)
    if early:
        pieces.append(Piece(late, 6, (0, CH), 0, CH, r_at + 6 * C, dp_at + C, True))
        pieces.append(Piece(late + 1, 7, (0, CH), 1, CH, r_at + 6 * C + CH, dp_at + C + CH, True))
    else:
        pieces.append(Piece(late, 6, (0, CH), 0, C, r_at + 6 * C, dp_at + C))

    class Share:
        def __init__(self, sem, src, dst, own, to, n):
            self.sem, self.src, self.dst, self.own, self.to, self.n = sem, src, dst, own, to, n

        def copy(self):
            at = lambda start: N.at[pl.ds(al(start, 16), self.n)]
            return remote(at(self.src), at(self.dst), r.shs.at[self.sem], r.shr.at[self.sem], place.partner)

        def sum(self):
            self.copy().wait_recv()
            v = self.own() + N[pl.ds(al(self.dst, 16), self.n), :].astype(F32)
            N[pl.ds(al(self.to, 16), self.n), :] = v.astype(BF)

    def dil_share(sem, at, n):
        own = lambda: N[pl.ds(dpr_at + at, n), :].astype(F32)
        return Share(sem, dps_at + at, dp_at + at, own, dpr_at + at, n)

    share_rest, share_pw, share_mid = dil_share(10, 0, C), dil_share(11, C, CH), dil_share(12, C + CH, CH)

    left = [list(pc.steps) for pc in pieces]
    plan = {}
    for name, which in PLAN:
        if not early:
            which = [p for p in which if p < len(pieces) and not (p == late and name in ("bh", "center", "center2"))]
        plan[name] = [(p, left[p].pop(0)) for p in which if left[p]]
    while any(left):
        first = max(len(x) for x in left)
        plan["end1"] += [(p, x.pop(0)) for p, x in enumerate(left) if len(x) == first]

    def pump(where):
        for p, ph in plan[where]:
            pieces[p].step(ph)

    ld_sto.wait()
    ld_raw.wait()
    CHK = 128
    raw_at = spans["RAW"][1] + m * HR

    def own_raw(i):
        return r.N[pl.ds(al(raw_at + i * CHK, 16), CHK), :].astype(F32).reshape(CHK // 8, 8, CH)

    def sto(i):
        return STO[pl.ds(al(i * CHK, CHK), CHK), :].astype(F32).reshape(CHK // 8, 8, CH)

    def s1(i, acc):
        return acc + jnp.sum(own_raw(i), axis=0) + jnp.sum(sto(i), axis=0)

    acc = lax.fori_loop(0, HR // CHK, s1, jnp.zeros((8, CH), F32))
    mean = row_sum(acc) / float(2 * HR)

    def s2(i, acc):
        u = own_raw(i) - mean
        v = sto(i) - mean
        return acc + jnp.sum(u * u, axis=0) + jnp.sum(v * v, axis=0)

    acc = lax.fori_loop(0, HR // CHK, s2, jnp.zeros((8, CH), F32))
    ex_in[0].start(jnp.concatenate([mean, row_sum(acc)], axis=0))

    ld_seg.wait()
    blocks = SEG.shape[1] // 128

    def make_segs(i, _):
        at = b * (T // 128) - 1 + i
        v = SEG[pl.ds(al(m * ROWS, ROWS), ROWS), pl.ds(al(jnp.clip(at, 0, blocks - 1) * 128, 128), 128)].astype(F32)
        v = jnp.where(jnp.logical_and(at >= 0, at < blocks), v, -1.0)
        for j in range(128):
            SEGX[pl.ds(al(i * 1024 + j * 8, 8), 8), :] = jnp.broadcast_to(v[:, j : j + 1], (8, 128))
        return 0

    lax.fori_loop(0, T // 128 + 2, make_segs, 0)
    BIN0 = 128 * 8

    def make_masks(i, _):
        mid = SEGX[pl.ds(al(i * 128 + BIN0, 128), 128), :]
        for j, o in enumerate((-2, -1, 1, 2)):
            off = SEGX[pl.ds(al(i * 128 + BIN0 + o * 8, 8), 128), :]
            MASK[j, pl.ds(al(i * 128, 128), 128), :] = jnp.where(off == mid, 1.0, 0.0).astype(BF)
        return 0

    lax.fori_loop(0, HR // 128, make_masks, 0)
    x_sig.wait_recv()
    BB = RT // ROWS

    def turn(src, dst, i):
        for h in range(2):
            for row in range(ROWS):
                v = src(h, row).astype(F32)
                for j in range(CH // 128):
                    LANES[pl.ds((h * (CH // 128) + j) * RT + row, BB, stride=ROWS), :] = v[:, j * 128 : (j + 1) * 128]
        for j in range(C // 128):
            dst[pl.ds(al(i * RT, RT), RT), j * 128 : (j + 1) * 128] = LANES[j * RT : (j + 1) * RT, :].astype(BF)

    def turn_x(i, _):
        turn(lambda h, row: RAW[pl.ds(al(h * HR + row * T + i * BB, BB), BB), :], X, i)
        return 0

    lax.fori_loop(0, T // BB, turn_x, 0)
    keep_x = local(X, r.oX, 13)
    keep_x.start()
    x_par.wait_recv()

    def vec(i):
        return jnp.concatenate([PAR[0, i : i + 1, :], PAR[1, i : i + 1, :]], axis=1)

    def hvec(i):
        return jnp.concatenate([PAR[0, i : i + 1, 0:HH], PAR[1, i : i + 1, 0:HH]], axis=1)

    la = ex_in[0].wait()
    n_own = float(2 * HR)
    lo = merged(la[0:na], n_own)
    hi = merged(la[na : 2 * na], n_own)
    ex_in[1].start(
        jnp.concatenate([jnp.concatenate([lo[0], hi[0]], axis=1), jnp.concatenate([lo[1], hi[1]], axis=1)], axis=0)
    )
    mu_in, sq = merged(ex_in[1].wait(), n_own * na)
    inv_in = lax.rsqrt(sq / total_in + EPSILON)
    gain_in, shift_in = vec(0), vec(1)
    scale_in = gain_in * inv_in
    ST[0:1, :] = mu_in
    ST[1:2, :] = inv_in
    ST[2:3, :] = gain_in
    HB = 256

    def make_hidden(i, last):
        at = al(i * HB, HB)
        pre = (X[pl.ds(at, HB), :].astype(F32) - mu_in) * scale_in + shift_in
        h = gelu_up(pre)
        H0[pl.ds(al(at + 16, 16), HB), :] = h.astype(BF)
        H1[pl.ds(at, HB), :] = jnp.concatenate([last, h[: HB - 8]], axis=0).astype(BF)
        return h[HB - 8 :]

    lax.fori_loop(0, HR // HB, make_hidden, jnp.zeros((8, C), F32))
    hs, hr = r.hs, r.hr
    down = (jnp.maximum(b - 1, 0), m, a)
    up = (jnp.minimum(b + 1, nb - 1), m, a)
    has_down, has_up = b > 0, b < nb - 1

    def when_down(f):
        pl.when(has_down)(f)

    def when_up(f):
        pl.when(has_up)(f)

    class Rims:
        def __init__(self, to_down, from_up, to_up, from_down, i):
            self.down = remote(to_down, from_up, hs.at[i], hr.at[i], down)
            self.up = remote(to_up, from_down, hs.at[i + 1], hr.at[i + 1], up)

        def start_down(self):
            when_down(self.down.start)

        def start_up(self):
            when_up(self.up.start)

        def wait_from_up(self):
            when_up(self.down.wait_recv)

        def wait_from_down(self):
            when_down(self.up.wait_recv)

        def drain(self):
            when_down(self.down.wait_send)
            when_up(self.up.wait_send)

    def clear_halo(ref):
        @pl.when(jnp.logical_not(has_down))
        def _():
            ref[0:16, :] = jnp.zeros((16, C), BF)

        @pl.when(jnp.logical_not(has_up))
        def _():
            ref[pl.ds(HR + 16, 16), :] = jnp.zeros((16, C), BF)

    def halos(ref, i):
        return Rims(ref.at[pl.ds(16, 16)], ref.at[pl.ds(HR + 16, 16)], ref.at[pl.ds(HR, 16)], ref.at[pl.ds(0, 16)], i)

    h_halo = halos(H0, 0)
    h_halo.start_down()
    h_halo.start_up()
    clear_halo(H0)

    def by_one_bin(even, odd):
        v = even[0:32, :].astype(F32)
        odd[0:16, :] = v[8:24].astype(BF)
        v = even[pl.ds(HR, 32), :].astype(F32)
        odd[pl.ds(HR, 16), :] = v[8:24].astype(BF)

    MJ = {-2: 0, -1: 1, 1: 2, 2: 3}

    def shifted(even, odd, o, at, n):
        if o % 2 == 0:
            v = even[pl.ds(al(at + (o + 2) * 8, 16), n), :]
        else:
            v = odd[pl.ds(al(at + (o + 1) * 8, 16), n), :]
        if o != 0:
            v = v * wide(MASK[MJ[o], pl.ds(al(at, 16), n), :], C // 128)
        return v

    def w(k):
        return W[k * C : (k + 1) * C, :]

    def put_lanes(v, n):
        for j in range(C // 128):
            LANES[j * RT : j * RT + n, :] = v[:, j * 128 : (j + 1) * 128]

    def get_lanes(at, n):
        return jnp.concatenate([LANES[pl.ds(al(j * RT + at, 8), n), :] for j in range(C // 128)], axis=1)

    for c in (*ld_w,):
        c.wait()
    for c in x_w:
        c.wait_recv()
    POOL, DIFF, SUM = r.POOL, r.DIFF, r.SUM
    SUM[...] = jnp.zeros_like(SUM)

    def conv_tile(i):
        at = al(i * RT, RT)
        acc = None
        for k in range(TAPS):
            d = dot(shifted(H0, H1, k - 2, at, RT), w(k), 1, 0)
            acc = d if acc is None else acc + d
        put_lanes(acc, RT)

        def pool(j, s):
            v = get_lanes(j * 128, 128).reshape(8, 2, 8, C)
            c0, c1 = v[:, 0], v[:, 1]
            d = c0 - c1
            p = jnp.maximum(c0, c1) + jnp.log(1.0 + jnp.exp(-jnp.abs(d)))
            to = pl.ds(al(i * (RT // 2) + j * 64, 64), 64)
            POOL[to, :] = p.reshape(64, C)
            DIFF[to, :] = d.reshape(64, C)
            return s + jnp.sum(p, axis=0)

        SUM[...] += lax.fori_loop(0, RT // 128, pool, jnp.zeros((8, C), F32))

    NT = HR // RT

    def conv_loop(i, _):
        conv_tile(i)
        return 0

    lax.fori_loop(1, NT - 1, conv_loop, 0)
    h_halo.wait_from_up()
    h_halo.wait_from_down()
    by_one_bin(H0, H1)
    lax.fori_loop(0, 2, lambda i, _: (conv_tile(i * (NT - 1)), 0)[1], 0)

    mean = row_sum(SUM[...]) / float(PR)

    def m2_mid(i, acc):
        v = POOL[pl.ds(al(i * 128, 128), 128), :].reshape(16, 8, C) - mean
        return acc + jnp.sum(v * v, axis=0)

    acc = lax.fori_loop(0, PR // 128, m2_mid, jnp.zeros((8, C), F32))
    ex_mid[0].start(jnp.concatenate([mean, row_sum(acc)], axis=0))

    ld_cot.wait()
    x_cot.wait_recv()

    def turn_ct(i, _):
        turn(lambda h, row: COT[h][pl.ds(al(row * S + i * BB, BB), BB), :], CT, i)
        return 0

    lax.fori_loop(0, S // BB, turn_ct, 0)
    ld_pw.wait()
    x_pw.wait_recv()
    GT, DO, E0 = part("GT"), part("DO"), part("E0")
    E1, GML = part("GM"), [part("GM", 0, PR), part("GM", PR, PR)]

    def make_gt(i, _):
        at = pl.ds(al(i * 256, 256), 256)
        GT[at, :] = dot(CT[at, :], PW[...], 1, 1)
        return 0

    lax.fori_loop(0, PR // 256, make_gt, 0)
    for c in ld_d:
        c.wait()
    for c in x_d:
        c.wait_recv()

    def dt(k):
        return DT[k * HC : (k + 1) * HC, :]

    mu_mid, sq = finish_stats(ex_mid, float(PR))
    inv_mid = lax.rsqrt(sq / total_mid + EPSILON)
    gain_mid, shift_mid = vec(2), vec(3)
    scale_mid = gain_mid * inv_mid

    def make_mid(i, _):
        at = pl.ds(al(i * 128, 128), 128)
        HM[at, :] = gelu_up((POOL[at, :] - mu_mid) * scale_mid + shift_mid).astype(BF)
        return 0

    lax.fori_loop(0, PR // 128, make_mid, 0)

    packed = early
    WIN = 32 * ROWS
    nrim = WIN if packed else rim
    RS = [part("RS", 0, nrim), part("RS", rim, nrim)]
    RR = [part("RR", 0, nrim), part("RR", rim, nrim)]

    def ended(s):
        before = SEGX[pl.ds(al(BIN0 + (s - 33) * 16, 8), 8), :]
        after = SEGX[pl.ds(al(BIN0 + s * 16, 8), 8), :]
        return wide(jnp.where(before != after, 1.0, 0.0), HC // 128).reshape(1, ROWS, HC)

    ended_up, ended_down = ended(S), ended(0)

    def choose(flag, x, y):
        three = (WIN // ROWS, ROWS, HC)
        return jnp.where(flag > 0.5, x.reshape(three), y.reshape(three)).reshape(WIN, HC)

    def pack_up(start):
        at = lambda s: r.F[pl.ds(start + s * ROWS, WIN), :]
        return choose(ended_up, at(S - 32), at(S - DIL)).astype(BF)

    def pack_down(start):
        at = lambda s: r.F[pl.ds(start + s * ROWS, WIN), :]
        return choose(ended_down, at(DIL - 32), at(0)).astype(BF)

    def unpack(flag, ref, v, first):
        ref[...] = jnp.zeros((rim, HC), F32)
        a, c = first * ROWS, (first + DIL - 32) * ROWS
        ref[a : a + WIN, :] = choose(flag, jnp.zeros((WIN, HC), F32), v)
        ref[c : c + WIN, :] = choose(flag, v, ref[c : c + WIN, :])

    p_rims = Rims(RS[1], RR[1], RS[0], RR[0], 2)
    QR = PR // 4
    e0_at, e1_at, do_at, hm_at = spans["E0"][1], spans["GM"][1], spans["DO"][1], spans["HM"][1]

    def pick(i, table):
        v = jnp.int32(table[-1])
        for n in range(len(table) - 2, -1, -1):
            v = jnp.where(i == n, table[n], v)
        return v

    quarter = (3, 2, 0, 1, 0, 1, 2, 3, 0, 1, 2, 3)
    taps_of = (0, 0, 2, 2, 0, 0, 2, 2, 1, 1, 1, 1)
    starts = [{0: e0_at + rim, 1: do_at, 2: e1_at}[k] + q * QR for k, q in zip(taps_of, quarter)]

    def product(i, _):
        v = dot(
            r.M[pl.ds(al(hm_at + pick(i, quarter) * QR, 16), QR), :],
            r.M[pl.ds(al(dt0 + pick(i, taps_of) * HC, 16), HC), :],
            1, 1,
        )
        r.F[pl.ds(al(pick(i, starts), 8), QR), :] = v

        @pl.when(i == 1)
        def _():
            RS[0][...] = pack_up(e0_at + rim) if packed else E0[PR : PR + rim, :].astype(BF)
            p_rims.start_up()

        @pl.when(i == 3)
        def _():
            RS[1][...] = pack_down(e1_at) if packed else E1[0:rim, :].astype(BF)
            p_rims.start_down()

        return 0

    lax.fori_loop(0, len(quarter), product, 0)

    def take_rims(rims, low, high):
        rims.wait_from_down()
        rims.wait_from_up()

        @pl.when(has_down)
        def _():
            v = RR[0][...].astype(F32)
            if packed:
                unpack(ended_down, low, v, 1)
            else:
                low[...] = v

        @pl.when(jnp.logical_not(has_down))
        def _():
            low[...] = jnp.zeros((rim, HC), F32)

        @pl.when(has_up)
        def _():
            v = RR[1][...].astype(F32)
            if packed:
                unpack(ended_up, high, v, 0)
            else:
                high[...] = v

        @pl.when(jnp.logical_not(has_up))
        def _():
            high[...] = jnp.zeros((rim, HC), F32)

    take_rims(p_rims, part("E0", 0, rim), part("GM", PR, rim))

    def same(i, by):
        def pick(off):
            return SEGX[pl.ds(al(i * 256 + BIN0 + off * 16, 16), 256), :].reshape(16, 2, 8, 128)[:, 0]

        return wide(jnp.where(pick(0) == pick(by), 1.0, 0.0).reshape(128, 128), HC // 128)

    def add_dil(i, s):
        at = pl.ds(al(i * 128, 128), 128)
        v = DO[at, :]
        v += same(i, -DIL) * E0[pl.ds(al(i * 128 + 8, 8), 128), :]
        v += same(i, DIL) * E1[pl.ds(al(i * 128 + DIL * 8, 8), 128), :]
        DO[at, :] = v
        return s + jnp.sum(v.reshape(16, 8, HC), axis=0)

    acc = lax.fori_loop(0, PR // 128, add_dil, jnp.zeros((8, HC), F32))
    mean = row_sum(acc) / float(PR)

    def m2_hid(i, acc):
        v = DO[pl.ds(al(i * 128, 128), 128), :].reshape(16, 8, HC) - mean
        return acc + jnp.sum(v * v, axis=0)

    acc = lax.fori_loop(0, PR // 128, m2_hid, jnp.zeros((8, HC), F32))
    ex_hid[0].start(jnp.concatenate([mean, row_sum(acc)], axis=0))
    mu_hid, sq = finish_stats(ex_hid, float(PR))
    inv_hid = lax.rsqrt(sq / total_mid + EPSILON)
    gain_hid, shift_hid = hvec(4), hvec(5)
    HT = part("HT")

    def make_top(i, s):
        at = pl.ds(al(i * 128, 128), 128)
        xhat = (DO[at, :] - mu_hid) * inv_hid
        h, slope = gelu_both(xhat * gain_hid + shift_hid)
        HT[at, :] = h.astype(BF)
        da = slope * GT[at, :]
        GT[at, :] = da
        DO[at, :] = xhat
        return (
            s[0] + jnp.sum((da * xhat).reshape(16, 8, HC), axis=0),
            s[1] + jnp.sum(da.reshape(16, 8, HC), axis=0),
        )

    zero = jnp.zeros((8, HC), F32)
    sg, sb = lax.fori_loop(0, PR // 128, make_top, (zero, zero))
    ex_bh[0].start(jnp.concatenate([row_sum(sg), row_sum(sb)], axis=0))

    OB = 256

    def make_out(i, _):
        at = pl.ds(al(i * OB, OB), OB)
        v = (POOL[at, :] + dot(HT[at, :], PW[...], 1, 0)).astype(BF)
        COT[0][at, :] = v[:, :CH]
        COT[1][at, :] = v[:, CH:]
        return 0

    lax.fori_loop(0, PR // OB, make_out, 0)
    cot_other = r.N.at[pl.ds(al(spans["COTR"][1] + other * PR, 16), PR)]
    o_own = local(cot_mine, r.oOUT.at[m], 14)
    o_own.start()
    o_cross = cross(cot_other, r.oOUT.at[m], 12)
    o_cross.start()
    gp = dot(HT[...], CT[...], 0, 0)
    N[dpr_at + C : dpr_at + C + HC, :] = jnp.where(m == 0, gp[:, :CH], gp[:, CH:]).astype(BF)
    N[dps_at + C : dps_at + C + HC, :] = jnp.where(m == 0, gp[:, CH:], gp[:, :CH]).astype(BF)
    share_pw.copy().start()

    v = finish_sums(ex_bh, lambda: (share_pw.sum(), pump("bh")))
    ST[8:10, 0:HC] = v
    ST[8:10, HC:] = jnp.zeros((2, C - HC), F32)
    scale = gain_hid * inv_hid
    mg, mb = v[0:1] / total_mid, v[1:2] / total_mid
    GD = [part("GD", k * PR, PR) for k in range(3)]

    def make_gd(i, _):
        at = pl.ds(al(i * 128, 128), 128)
        g = (scale * (GT[at, :] - mb - DO[at, :] * mg)).astype(BF)
        GD[1][at, :] = g
        E0[pl.ds(al(i * 128 + rim, 16), 128), :] = g.astype(F32)
        return 0

    lax.fori_loop(0, PR // 128, make_gd, 0)
    p_rims.drain()
    if packed:
        RS[0][...] = pack_up(e0_at + rim)
        RS[1][...] = pack_down(e0_at + rim)
        g_rims = Rims(RS[1], RR[1], RS[0], RR[0], 4)
    else:
        g_rims = Rims(part("GD", PR, rim), RR[1], part("GD", 2 * PR - rim, rim), RR[0], 4)
    g_rims.start_up()
    g_rims.start_down()


    def to_gm(make, add):
        def body(i, _):
            at = pl.ds(al(i * QR, QR), QR)
            v = make(at)
            for h in range(2):
                u = v[:, h * CH : (h + 1) * CH]
                GML[h][at, :] = GML[h][at, :] + u if add else u
            return 0

        lax.fori_loop(0, 4, body, 0)

    to_gm(lambda at: dot(GD[1][at, :], dt(1), 1, 0), False)
    gd_at = spans["GD"][1]

    def dil_grad(k, to):
        g = dot(N[pl.ds(al(gd_at + k * PR, 16), PR), :], HM[...], 0, 0)
        own = jnp.where(m == 0, g[:HH], g[HH:]).astype(BF)
        for_partner = jnp.where(m == 0, g[HH:], g[:HH]).astype(BF)
        for h in range(2):
            at = to + h * HH
            N[pl.ds(al(dpr_at + at, 16), HH), :] = own[:, h * CH : (h + 1) * CH]
            N[pl.ds(al(dps_at + at, 16), HH), :] = for_partner[:, h * CH : (h + 1) * CH]

    dil_grad(1, C + CH)
    share_mid.copy().start()
    pump("center")
    share_mid.sum()
    pump("center2")
    take_rims(g_rims, part("E0", 0, rim), part("E0", PR + rim, rim))
    pump("rims")

    def mask_gd(i, _):
        at = pl.ds(al(i * 128, 128), 128)
        GD[0][at, :] = (same(i, DIL) * E0[pl.ds(al(i * 128 + rim + DIL * 8, 8), 128), :]).astype(BF)
        GD[2][at, :] = (same(i, -DIL) * E0[pl.ds(al(i * 128 + rim - DIL * 8, 8), 128), :]).astype(BF)
        return 0

    lax.fori_loop(0, PR // 128, mask_gd, 0)
    to_gm(lambda at: dot(GD[0][at, :], dt(0), 1, 0) + dot(GD[2][at, :], dt(2), 1, 0), True)

    def gm(at):
        return jnp.concatenate([GML[0][at, :], GML[1][at, :]], axis=1)

    def make_dmid(i, s):
        at = pl.ds(al(i * 64, 64), 64)
        xhat = (POOL[at, :] - mu_mid) * inv_mid
        _, slope = gelu_both(xhat * gain_mid + shift_mid)
        da = slope * gm(at)
        GML[0][at, :] = da[:, :CH]
        GML[1][at, :] = da[:, CH:]
        return (
            s[0] + jnp.sum((da * xhat).reshape(8, 8, C), axis=0),
            s[1] + jnp.sum(da.reshape(8, 8, C), axis=0),
        )

    zero = jnp.zeros((8, C), F32)
    sg, sb = lax.fori_loop(0, PR // 64, make_dmid, (zero, zero))
    g_rims.drain()
    o_own.wait()
    o_cross.wait_send()
    keep_x.wait()
    ex_bm[0].start(jnp.concatenate([row_sum(sg), row_sum(sb)], axis=0))

    lax.fori_loop(0, 2, lambda i, _: (dil_grad(2 * i, i * CH), 0)[1], 0)
    share_rest.copy().start()
    v = finish_sums(ex_bm, lambda: (share_rest.sum(), pump("bm")))
    ST[6:8, :] = v
    mg, mb = v[0:1] / total_mid, v[1:2] / total_mid
    pump("bm2")
    GC0, GC1 = part("GC0"), H1

    def make_gc(i, last):
        at = pl.ds(al(i * 64, 64), 64)
        xhat = (POOL[at, :] - mu_mid) * inv_mid
        g = CT[at, :].astype(F32) + scale_mid * (gm(at) - mb - xhat * mg)
        d = DIFF[at, :]
        e = jnp.exp(-jnp.abs(d))
        big = 1.0 / (1.0 + e)
        small = e * big
        g0 = g * jnp.where(d >= 0, big, small)
        g1 = g * jnp.where(d >= 0, small, big)
        v = jnp.stack([g0.reshape(8, 8, C), g1.reshape(8, 8, C)], axis=1).reshape(128, C)
        GC0[pl.ds(al(i * 128 + 16, 16), 128), :] = v.astype(BF)
        GC1[pl.ds(al(i * 128, 128), 128), :] = jnp.concatenate([last, v[:120]], axis=0).astype(BF)
        return v[120:]

    lax.fori_loop(0, PR // 64, make_gc, jnp.zeros((8, C), F32))
    g_halo = halos(GC0, 6)
    g_halo.start_down()
    g_halo.start_up()
    clear_halo(GC0)
    XX = part("XX")
    back_x = local(r.oX, XX, 13)

    own_at = spans["GM"][1]
    h0_at = spans["H0"][1] + 16
    ps_at = spans["PS"][1]
    HALF = C // 2
    first_half = (1 - bits[0]) * HALF

    def tap_share(i, j):
        at = first_half if j == 0 else HALF - first_half
        own = lambda: r.F[pl.ds(al(own_at + i % 2 * PR + at, 8), HALF), :]
        return Share(2 * i + j, ps_at + i % PSLOTS * C + at, spans[f"F{i}"][1] + at, own, r_at + i * C + at, HALF)

    shares = [tap_share(i, j) for i in range(TAPS) for j in range(2)]

    def masked(k):
        def body(j, _):
            XX[pl.ds(al(j * 256, 256), 256), :] = shifted(GC0, GC1, 2 - k, j * 256, 256)
            return 0

        lax.fori_loop(0, HR // 256, body, 0)

    def half_tap(it, _):
        i, j = it // 2, lax.rem(it, 2)
        for n in range(TAPS):

            @pl.when(it == 2 * n)
            def _(n=n):
                if n == 1:
                    g_halo.wait_from_up()
                    g_halo.wait_from_down()
                    by_one_bin(GC0, GC1)
                if n >= PSLOTS:
                    for c in shares[2 * (n - PSLOTS) : 2 * (n - PSLOTS) + 2]:
                        c.copy().wait_send()
                masked(ORDER[n])

        odd = lax.rem(i, 2)
        at = jnp.where(j == 0, first_half, HALF - first_half)
        v = dot(r.M[h0_at : h0_at + HR, pl.ds(al(at, 128), HALF)], XX[...], 0, 0)
        r.F[pl.ds(al(own_at + odd * PR + at, 8), HALF), :] = jnp.where(m == 0, v[:, :CH], v[:, CH:])
        N[pl.ds(al(ps_at + lax.rem(i, PSLOTS) * C + at, 16), HALF), :] = jnp.where(m == 0, v[:, CH:], v[:, :CH]).astype(BF)
        for n in range(2 * TAPS):

            @pl.when(it == n)
            def _(n=n):
                shares[n].copy().start()
                if n:
                    shares[n - 1].sum()
                pump(f"tap{n}")

        return 0

    lax.fori_loop(0, 2 * TAPS, half_tap, 0)
    shares[-1].sum()
    pump("taps")

    back_x.start()
    for c in shares[2 * (TAPS - PSLOTS) :]:
        c.copy().wait_send()
    mu, inv, gain, shift = ST[0:1, :], ST[1:2, :], gain_in, shift_in
    RB = 256
    DA = [part("RAW", 0, HR), part("RAW", HR, HR)]

    def tile(i, s):
        at = i * RB
        acc = None
        for k in range(TAPS):
            d = dot(shifted(GC0, GC1, 2 - k, at, RB), w(k), 1, 1)
            acc = d if acc is None else acc + d
        put_lanes(acc, RB)
        for n in range(HR // RB):

            @pl.when(i == n)
            def _(n=n):
                pump(f"tile{2 * n}")
                if n == 0:
                    back_x.wait()


        def back(j, s):
            to = pl.ds(al(at + j * 64, 64), 64)
            xhat = (XX[to, :].astype(F32) - mu) * inv
            _, slope = gelu_both(xhat * gain + shift)
            da = slope * get_lanes(j * 64, 64)
            DA[0][to, :] = da[:, :CH].astype(BF)
            DA[1][to, :] = da[:, CH:].astype(BF)
            return (
                s[0] + jnp.sum((da * xhat).reshape(8, 8, C), axis=0),
                s[1] + jnp.sum(da.reshape(8, 8, C), axis=0),
            )

        s = lax.fori_loop(0, RB // 64, back, s)
        for n in range(HR // RB):

            @pl.when(i == n)
            def _(n=n):
                pump(f"tile{2 * n + 1}")

        return s

    s = lax.fori_loop(0, HR // RB, tile, (zero, zero))
    ex_bi[0].start(jnp.concatenate([row_sum(s[0]), row_sum(s[1])], axis=0))
    d_own = local(raw_mine, r.oDA.at[m], 12)
    d_own.start()
    d_cross = cross(r.N.at[pl.ds(al(spans["RAW"][1] + other * HR, 16), HR)], r.oDA.at[m], 13)
    d_cross.start()
    pump("end0")
    ex_bi[1].start(functools.reduce(jnp.add, ex_bi[0].wait()))
    pump("end1")
    ST[4:6, :] = functools.reduce(jnp.add, ex_bi[1].wait())
    ST[3:4, :] = jnp.zeros((1, C), F32)
    ST[10:16, :] = jnp.zeros((6, C), F32)
    o_st = local(ST, r.oST, 14)
    o_st.start()
    for pc in pieces:
        pc.drain()
    for c in (share_rest, share_pw, share_mid):
        c.copy().wait_send()
    d_own.wait()
    o_st.wait()
    d_cross.wait()
    o_cross.wait_recv()
    for c in crosses:
        c.wait_send()
    for e in exchanges:
        e[0].drain()
        e[1].drain()
    h_halo.drain()
    g_halo.drain()


def call_main(axes, sig, seg, cot, wide_taps, taps, pw, vectors):
    nb, nm, na = axes
    CH = sig.shape[1]
    C = 2 * CH
    HC = pw.shape[0]
    assert HC == CH
    HR = sig.shape[0] // 2
    PR = cot.shape[0] // 2
    T, S = HR // ROWS, PR // ROWS
    rim = (DIL + 1) * ROWS
    RT = 512
    NA = nm * na
    early = nb == 4
    NP = 3 * (TAPS + 1) + (2 if early else 1)
    inputs = dict(sig=sig, seg=seg, cot=cot, wide=wide_taps, taps=taps, pw=pw)
    inputs.update({f"v{i}": v for i, v in enumerate(vectors)})
    sd = jax.ShapeDtypeStruct
    outs = dict(
        oX=sd((HR, C), BF),
        oDA=sd((2, HR, CH), BF),
        oOUT=sd((2, PR, CH), BF),
        oR=sd((TAPS, C, CH), BF),
        oDP=sd((2 * C, CH), BF),
        oST=sd((16, C), F32),
    )
    spans = {}

    def lay(pool, start, items):
        for name, n in items:
            spans[name] = (pool, start, n)
            start += n
        return start

    end = lay("N", 0, [("RAW", 2 * HR), ("STO", HR), ("COTR", 2 * PR), ("HT", PR), ("RS", 2 * rim), ("RR", 2 * rim)])
    lay("N", spans["STO"][1], [("DPS", 2 * C)])
    lay("N", spans["COTR"][1], [(f"XB{p}", C // 2) for p in range(TAPS)])
    lay("N", spans["HT"][1], [(f"YB{p}", C // 4) for p in range(TAPS)])
    lay("N", spans["RS"][1], [(f"F{p}", C) for p in range(2)])
    end = lay("N", end, [("GD", 3 * PR)])
    lay("N", spans["GD"][1], [("R", (TAPS + 2) * C)])
    end = max(end, spans["R"][1] + (TAPS + 2) * C)
    end = lay("N", end, [(f"F{p}", C) for p in range(2, TAPS)] + [("FD", 2 * C)])
    lay("N", spans["RAW"][1] + HR, [("PS", 2 * C)])
    sizes = {p: C for p in range(TAPS + 1)} | ({6: CH, 7: CH} if early else {6: C})
    rest = range(TAPS, len(sizes))
    end = lay("N", end, [(f"XB{p}", sizes[p] // 2) for p in rest] + [(f"YB{p}", sizes[p] // 4) for p in rest])
    n_rows = lay("N", end, [(f"ZB{p}", C // 2 if p > 5 and early else C // 4) for p in range(len(sizes))])
    end = lay("M", 0, [("X", HR), ("gap", 32), ("HM", PR), ("CT", PR), ("H0", HR + 32), ("H1", HR + 32)])
    lay("M", 0, [("GC0", HR + 32)])
    lay("M", spans["HM"][1], [("XX", HR)])
    m_rows = lay("M", end, [("W", TAPS * C), ("PW", HC), ("DT", 3 * HC)])
    f_rows = lay("F", 0, [("E0", PR + 2 * rim), ("GM", 2 * PR), ("DO", PR), ("GT", PR)])
    V = pltpu.VMEM
    DMA = pltpu.SemaphoreType.DMA
    scratch = dict(
        N=V((n_rows, CH), BF),
        M=V((m_rows, C), BF),
        F=V((f_rows, CH), F32),
        LANES=V((C // 128 * RT, 128), F32),
        MASK=V((4, HR, 128), BF),
        SEG=V(seg.shape, jnp.int32),
        SEGX=V(((T + 256) * ROWS, 128), F32),
        PAR=V((2, 8, CH), F32),
        ST=V((16, C), F32),
        SUM=V((8, C), F32),
        POOL=V((PR, C), F32),
        DIFF=V((PR, C), F32),
        XIA=V((NA, 2, CH), F32), XIB=V((nb, 2, C), F32),
        XMA=V((NA, 2, C), F32), XMB=V((nb, 2, C), F32),
        XHA=V((NA, 2, HC), F32), XHB=V((nb, 2, HC), F32),
        XGA=V((NA, 2, HC), F32), XGB=V((nb, 2, HC), F32),
        XDA=V((NA, 2, C), F32), XDB=V((nb, 2, C), F32),
        XSA=V((NA, 2, C), F32), XSB=V((nb, 2, C), F32),
        lsem=DMA((15 + NP,)),
        shs=DMA((13,)), shr=DMA((13,)),
        csem_s=DMA((14,)), csem_r=DMA((14,)),
        as_=DMA((6, NA)), ar_=DMA((6, NA)),
        bs_=DMA((6, nb)), br_=DMA((6, nb)),
        hs=DMA((8,)), hr=DMA((8,)),
        ps=DMA((NP, 6)), pr=DMA((NP, 6)),
        zs=DMA((NP, 2, 4)), zr=DMA((NP, 2, 4)),
    )
    outer = nb // 4
    if outer > 1:
        scratch.update(os_=DMA((NP, outer)), or_=DMA((NP, outer)))
        n = outer * (C // 16)
        assert lay("F", spans["E0"][1], [(f"OB{p}", n) for p in range(TAPS)]) <= spans["GM"][1]
        assert lay("F", spans["DO"][1], [(f"OB{p}", n) for p in range(TAPS, TAPS + 2)]) <= f_rows
    names = list(inputs) + list(outs) + list(scratch)
    anyspec = pl.BlockSpec(memory_space=pl.ANY)
    vmem = pl.BlockSpec(memory_space=pltpu.VMEM)
    res = pl.pallas_call(
        functools.partial(main_body, (nb, nm, na, T, S, CH, HC), names, spans),
        out_shape=list(outs.values()),
        in_specs=[vmem if n.startswith("v") else anyspec for n in inputs],
        out_specs=[anyspec] * len(outs),
        scratch_shapes=list(scratch.values()),
        compiler_params=pltpu.CompilerParams(
            collective_id=0, has_side_effects=True, vmem_limit_bytes=VMEM_BYTES
        ),
        cost_estimate=pl.CostEstimate(flops=44_000_000_000, bytes_accessed=40_000_000, transcendentals=8_000_000),
        name="forward_and_backward",
    )(*inputs.values())
    return dict(zip(outs, res, strict=True))


def last_body(dims, sig, da, out, rr, dp, stats, gs, oo, gw, dk, pw, g0, g1, g2, g3, g4, g5,
              sig_v, da_v, out_v, rr_v, dp_v, st_v, gs_v, oo_v, gw_v, dk_v, pw_v, lanes, ls, ss):
    CH, total_in = dims
    m = lax.axis_index("mp")
    taps = rr.shape[0]
    T, S = sig.shape[1], oo.shape[1]
    HH = g4.shape[0]
    copy = pltpu.make_async_copy

    def load(src, dst, i):
        return copy(src, dst, ls.at[i])

    def load_tap(k):
        return load(rr.at[k], rr_v.at[k], k)

    def load_half(h):
        rows = pl.ds(h * ROWS, ROWS)
        return [
            load(da.at[h], da_v.at[h], taps + 3 * h),
            load(sig.at[rows], sig_v.at[rows], taps + 3 * h + 1),
            load(out.at[h], out_v.at[h], taps + 3 * h + 2),
        ]

    ld_st = load(stats, st_v, taps + 6)
    ld_dp = load(dp, dp_v, taps + 7)
    ld_st.start()
    for k in range(taps):
        load_tap(k).start()
    for h in range(2):
        for c in load_half(h):
            c.start()
    ld_dp.start()

    def store_tap(k):
        return copy(gw_v.at[k], gw.at[k], ss.at[k])

    def tap(k, _):
        load_tap(k).wait()

        def part(i, _):
            at = pl.ds(al(i * 96, 96), 96)
            gw_v[k, at, :] = rr_v[k, at, :].astype(F32)
            return 0

        lax.fori_loop(0, rr.shape[1] // 96, part, 0)
        store_tap(k).start()
        return 0

    lax.fori_loop(0, taps, tap, 0)
    ld_st.wait()
    st = st_v[:, pl.ds(al(m * CH, CH), CH)]
    mu, inv, gain, gg, gb = [st[i : i + 1] for i in (0, 1, 2, 4, 5)]
    scale = gain * inv
    mg, mb = gg / total_in, gb / total_in
    BB = 64
    n = BB * ROWS

    def store_gs(h, c):
        at = (pl.ds(h * ROWS, ROWS), pl.ds(al(c * BB, BB), BB))
        return copy(gs_v.at[at], gs.at[at], ss.at[taps + h * (T // BB) + c])

    def store_oo(h):
        at = pl.ds(h * ROWS, ROWS)
        return copy(oo_v.at[at], oo.at[at], ss.at[taps + 2 * (T // BB) + h])

    def fill(v):
        for j in range(CH // 128):
            lanes[j * n : (j + 1) * n, :] = v[:, j * 128 : (j + 1) * 128].astype(F32)

    def half(h, _):
        for c in load_half(h):
            c.wait()

        def block(c, _):
            fill(da_v[h, pl.ds(al(c * n, n), n), :])
            bins = pl.ds(al(c * BB, BB), BB)
            for row in range(ROWS):
                for j in range(CH // 128):
                    l = slice(j * 128, (j + 1) * 128)
                    d = lanes[pl.ds(j * n + row, BB, stride=ROWS), :]
                    xhat = (sig_v[h * ROWS + row, bins, l].astype(F32) - mu[:, l]) * inv[:, l]
                    gs_v[h * ROWS + row, bins, l] = scale[:, l] * (d - mb[:, l] - xhat * mg[:, l])
            store_gs(h, c).start()
            return 0

        lax.fori_loop(0, T // BB, block, 0)

        def block2(c, _):
            fill(out_v[h, pl.ds(al(c * n, n), n), :])
            bins = pl.ds(al(c * BB, BB), BB)
            for row in range(ROWS):
                for j in range(CH // 128):
                    oo_v[h * ROWS + row, bins, j * 128 : (j + 1) * 128] = lanes[pl.ds(j * n + row, BB, stride=ROWS), :].astype(BF)
            return 0

        lax.fori_loop(0, S // BB, block2, 0)
        store_oo(h).start()
        return 0

    lax.fori_loop(0, 2, half, 0)
    ld_dp.wait()
    for k, at in enumerate((0, 6, 2)):
        for h in range(2):
            dk_v[k * HH : (k + 1) * HH, h * CH : (h + 1) * CH] = dp_v[(at + h) * HH : (at + h + 1) * HH, :].astype(F32)
    pw_v[...] = dp_v[4 * HH : 6 * HH, :].astype(F32)
    st_dk = copy(dk_v, dk, ss.at[taps + 2 * (T // BB) + 2])
    st_pw = copy(pw_v, pw, ss.at[taps + 2 * (T // BB) + 3])
    st_dk.start()
    st_pw.start()
    for ref, i in ((g0, 4), (g1, 5), (g2, 6), (g3, 7)):
        ref[...] = st[i : i + 1].reshape(CH)
    hid = st_v[8:10, : 2 * HH]
    hid = jnp.where(m == 0, hid[:, :HH], hid[:, HH:])
    g4[...] = hid[0:1].reshape(HH)
    g5[...] = hid[1:2].reshape(HH)
    for k in range(taps):
        store_tap(k).wait()
    for h in range(2):
        for c in range(T // BB):
            store_gs(h, c).wait()
        store_oo(h).wait()
    st_dk.wait()
    st_pw.wait()


def call_last(axes, sig, o):
    nb, nm, na = axes
    rows, T, CH = sig.shape
    S = T // 2
    C = 2 * CH
    HC = CH
    HH = HC // 2
    rr = o["oR"]
    total_in = float(rows * T * nb * na)
    sd = jax.ShapeDtypeStruct
    V = pltpu.VMEM
    anyspec = pl.BlockSpec(memory_space=pl.ANY)
    vmem = pl.BlockSpec(memory_space=pltpu.VMEM)
    inputs = (sig, o["oDA"], o["oOUT"], rr, o["oDP"], o["oST"])
    big = [sd((rows, T, CH), F32), sd((rows, S, CH), BF), sd(rr.shape, F32), sd((3 * HH, C), F32), sd((HC, CH), F32)]
    return pl.pallas_call(
        functools.partial(last_body, (CH, total_in)),
        out_shape=big + [sd((CH,), F32)] * 4 + [sd((HH,), F32)] * 2,
        in_specs=[anyspec] * len(inputs),
        out_specs=[anyspec] * len(big) + [vmem] * 6,
        scratch_shapes=[V(x.shape, x.dtype) for x in inputs]
        + [V(x.shape, x.dtype) for x in big]
        + [V((CH // 128 * 64 * ROWS, 128), F32), pltpu.SemaphoreType.DMA((rr.shape[0] + 8,)), pltpu.SemaphoreType.DMA((rr.shape[0] + T // 32 + 4,))],
        compiler_params=pltpu.CompilerParams(vmem_limit_bytes=VMEM_BYTES),
        name="last_pass",
    )(*inputs)


def on_device(axes, signal, seg, cotangent, conv_wide, taps, pointwise, *vectors):
    CH = signal.shape[2]
    o = call_main(
        axes, signal.reshape(-1, CH), seg, cotangent.reshape(-1, CH), conv_wide, jnp.swapaxes(taps, 1, 2), pointwise, vectors
    )
    gs, out, gw, dk, pw, *small = call_last(axes, signal, o)
    K, C, HH = taps.shape
    return (out, gs, gw.reshape(conv_wide.shape), jnp.swapaxes(dk.reshape(K, HH, C), 1, 2), pw, *small)


def solution(mesh):
    axes = (mesh.shape["bins"], mesh.shape["mp"], mesh.shape["batch"])
    cut = P("batch", "bins", "mp")
    tap = P(None, None, "mp")
    return jax.shard_map(
        functools.partial(on_device, axes),
        mesh=mesh,
        in_specs=(cut, P("batch", None), cut, tap, tap, P(None, "mp")) + (P("mp"),) * 6,
        out_specs=(cut, cut, tap, tap, P(None, "mp")) + (P("mp"),) * 6,
        check_vma=False,
    )
```

```python
import functools
import types

import jax
import jax.numpy as jnp
from jax import lax
from jax.experimental import pallas as pl
from jax.experimental.pallas import tpu as pltpu
from jax.sharding import PartitionSpec as P

DIL = 57
EPSILON = 1e-05
TAPS = 5
BF = jnp.bfloat16
F32 = jnp.float32
MESH = pl.DeviceIdType.MESH
K0 = 0.7978845608028654
K3 = 0.044715
ROWS = 8
VMEM_BYTES = 63 * 2**20


def gelu_up(x):
    t = jnp.tanh(x * (K0 + (K0 * K3) * (x * x)))
    h = 0.5 * x
    return h + h * t


def gelu_both(x):
    x2 = x * x
    t = jnp.tanh(x * (K0 + (K0 * K3) * x2))
    h = 0.5 * x
    return h + h * t, 0.5 + 0.5 * t + h * (1.0 - t * t) * (K0 + (3.0 * K0 * K3) * x2)


def dot(a, b, ca, cb):
    return lax.dot_general(a, b, (((ca,), (cb,)), ((), ())), preferred_element_type=F32)


def wide(mask, times):
    return jnp.concatenate([mask] * times, axis=1)


def al(x, n):
    return pl.multiple_of(x, n)


class Place:
    def __init__(self, nb, nm, na):
        self.nb, self.nm, self.na = nb, nm, na
        self.b = lax.axis_index("bins")
        self.m = lax.axis_index("mp")
        self.a = lax.axis_index("batch")
        self.layer = nm * na
        self.q = self.m * na + self.a

    def in_layer(self, q):
        return (self.b, q // self.na, lax.rem(q, self.na))

    def in_bins(self, b):
        return (b, self.m, self.a)

    @property
    def partner(self):
        return (self.b, 1 - self.m, self.a)

    def others(self, me, n):
        return [lax.rem(me + i, n) for i in range(1, n)]


def remote(src, dst, ss, rs, dev):
    return pltpu.make_async_remote_copy(
        src_ref=src, dst_ref=dst, send_sem=ss, recv_sem=rs, device_id=dev, device_id_type=MESH
    )


class Exchange:
    def __init__(self, buf, me, n, dev_of, ss, rs, others):
        self.buf, self.me, self.n, self.dev_of, self.ss, self.rs, self.others = (
            buf, me, n, dev_of, ss, rs, others,
        )

    def start(self, value):
        self.buf[self.me] = value
        own = self.buf.at[self.me]
        for q in self.others:
            remote(own, own, self.ss, self.rs, self.dev_of(q)).start()

    def all_others(self):
        ref = self.buf.at[pl.ds(0, self.n - 1)]
        return remote(ref, ref, self.ss, self.rs, self.dev_of(self.others[0]))

    def wait(self):
        self.all_others().wait_recv()
        return [self.buf[i] for i in range(self.n)]

    def drain(self):
        self.all_others().wait_send()


def merged(parts, count):
    means = [p[0:1] for p in parts]
    total = functools.reduce(jnp.add, means)
    mean = total / len(parts)
    squares = functools.reduce(jnp.add, [p[1:2] for p in parts])
    apart = functools.reduce(jnp.add, [(x - mean) * (x - mean) for x in means])
    return mean, squares + count * apart


def row_sum(x):
    return jnp.sum(x, axis=0, keepdims=True)


def greet(devices):
    barrier = pltpu.get_barrier_semaphore()
    for d in devices:
        pl.semaphore_signal(barrier, inc=1, device_id=d, device_id_type=MESH)
    pl.semaphore_wait(barrier, len(devices))


PLAN = (
    ("bh", [18]),
    ("center", [18]),
    ("center2", [19]),
    ("rims", [18]),
    ("bm", [19, 15, 16, 17]),
    ("bm2", [18]),
    ("tap0", [19, 15, 16, 17]),
    ("tap1", [18, 0, 2]),
    ("tap2", [1, 15, 16]),
    ("tap3", [17, 4]),
    ("tap4", [3, 5]),
    ("tap5", [18, 1, 6, 8]),
    ("tap6", [19, 0, 15, 7]),
    ("tap7", [16, 2, 3, 17, 10]),
    ("tap8", [4, 5, 1, 9, 11, 0]),
    ("tap9", [15, 6, 12, 14, 7]),
    ("taps", [16, 2, 13, 17]),
    ("tile0", [8, 4, 1, 19]),
    ("tile1", [0, 9, 3]),
    ("tile2", [2, 11]),
    ("tile3", [10]),
    ("tile4", [6, 5, 4, 16, 15, 1]),
    ("tile5", []),
    ("tile6", [0, 13, 12, 3, 8]),
    ("tile7", [2, 14]),
    ("tile8", [7, 6, 19, 17, 5]),
    ("tile9", [10, 9, 4]),
    ("tile10", [11, 3, 15, 8]),
    ("tile11", [0]),
    ("tile12", [16, 7, 12, 1, 6, 2, 13]),
    ("tile13", [5, 14]),
    ("tile14", [3, 10, 9]),
    ("tile15", [17, 0]),
    ("end0", [11, 4, 8, 2, 7, 1, 5, 12, 6, 13, 4, 14]),
    ("end1", [3, 7, 10, 8, 9, 6, 11, 5, 12, 13, 7, 8, 14, 10, 9, 12, 11, 13, 14, 10, 9, 12, 11, 14, 13]),
)


def main_body(dims, names, spans, *refs):
    nb, nm, na, T, S, CH, HC = dims
    C = 2 * CH
    HR = T * ROWS
    PR = S * ROWS
    rim = (DIL + 1) * ROWS
    r = types.SimpleNamespace(**dict(zip(names, refs, strict=True)))
    place = Place(nb, nm, na)
    b, m, a = place.b, place.m, place.a
    other = 1 - m
    total_in = float(HR * nb * nm * na)
    total_mid = float(PR * nb * nm * na)
    LANES = r.LANES
    RT = LANES.shape[0] // (C // 128)
    early = nb == 4

    def part(name, at=0, n=None):
        pool, start, rows = spans[name]
        return getattr(r, pool).at[pl.ds(start + at, rows if n is None else n)]

    def local(src, dst, i):
        return pltpu.make_async_copy(src, dst, r.lsem.at[i])

    def cross(src, dst, i):
        return remote(src, dst, r.csem_s.at[i], r.csem_r.at[i], place.partner)

    RAW, STO, X, CT, HM = part("RAW"), part("STO"), part("X"), part("CT"), part("HM")
    H0, H1, W, PW, DT = part("H0"), part("H1"), part("W"), part("PW"), part("DT")
    COT = [part("COTR", 0, PR), part("COTR", PR, PR)]
    vectors = [r.v0, r.v1, r.v2, r.v3, r.v4, r.v5]
    PAR, SEG, SEGX, MASK, ST = r.PAR, r.SEG, r.SEGX, r.MASK, r.ST
    half = lambda at, n: pl.ds(al(at + m * n, n), n)

    sig, cot = r.sig, r.cot
    mine, theirs = pl.ds(al(m * HR, HR), HR), pl.ds(al(other * HR, HR), HR)
    raw_mine = r.N.at[pl.ds(al(spans["RAW"][1] + m * HR, 16), HR)]
    cot_mine = r.N.at[pl.ds(al(spans["COTR"][1] + m * PR, 16), PR)]
    lanes = pl.ds(al(m * CH, CH), CH)
    w0, pw0, dt0 = spans["W"][1], spans["PW"][1], spans["DT"][1]
    HH = HC // 2

    def weight(k):
        return r.M.at[pl.ds(w0 + k * C, C), lanes]

    def tap_rows(k):
        return r.M.at[pl.ds(al(dt0 + k * HC + m * HH, 16), HH)]

    pw_mine = r.M.at[pl.ds(pw0, HC), lanes]
    ld_sto = local(sig.at[theirs], STO, 0)
    ld_raw = local(sig.at[mine], raw_mine, 1)
    ld_seg = local(r.seg, SEG, 2)
    ld_w = [local(r.wide.at[k], weight(k), 3 + k) for k in range(TAPS)]
    ld_d = [local(r.taps.at[k], tap_rows(k), 8 + k) for k in range(3)]
    ld_pw = local(r.pw, pw_mine, 11)
    ld_cot = local(cot.at[pl.ds(al(m * PR, PR), PR)], cot_mine, 12)
    for c in [ld_sto, ld_raw, ld_seg, *ld_w, *ld_d, ld_pw, ld_cot]:
        c.start()
    for i in range(4):
        PAR[m, i : i + 1, :] = vectors[i][...].reshape(1, CH)
    for i in range(4, 6):
        PAR[m, i : i + 1, 0:HH] = vectors[i][...].reshape(1, HH)
    if early:
        chips, chip = nb * na, b * na + a
        first = (m, nm, lambda q: (b, q, a))
        second = (chip, chips, lambda q: (q // na, m, lax.rem(q, na)))
    else:
        first = (place.q, place.layer, place.in_layer)
        second = (b, nb, place.in_bins)
    greet([g[2](q) for g in (first, second) for q in place.others(*g[:2])])
    x_sig = cross(sig.at[theirs], raw_mine, 0)
    x_par = cross(PAR.at[m], PAR.at[m], 1)
    x_w = [cross(r.wide.at[k], weight(k), 2 + k) for k in range(TAPS)]
    x_d = [cross(r.taps.at[k], tap_rows(k), 7 + k) for k in range(3)]
    x_pw = cross(r.pw, pw_mine, 10)
    x_cot = cross(cot.at[pl.ds(al(other * PR, PR), PR)], cot_mine, 11)
    crosses = [x_sig, x_par, *x_w, x_cot, x_pw, *x_d]
    for c in crosses:
        c.start()

    def exchange(i, name):
        one, two = (second, first) if early and i == 0 else (first, second)
        return (
            Exchange(getattr(r, name + "A"), *one, r.as_.at[i], r.ar_.at[i], place.others(*one[:2])),
            Exchange(getattr(r, name + "B"), *two, r.bs_.at[i], r.br_.at[i], place.others(*two[:2])),
        )

    def begin_stats(ex, mean, squares, count):
        ex[0].start(jnp.concatenate([mean, squares], axis=0))
        ex[1].start(jnp.concatenate(merged(ex[0].wait(), count), axis=0))

    def finish_stats(ex, count):
        return merged(ex[1].wait(), count * first[1])

    def begin_sums(ex, one, two):
        ex[0].start(jnp.concatenate([one, two], axis=0))
        ex[1].start(functools.reduce(jnp.add, ex[0].wait()))

    def finish_sums(ex):
        return functools.reduce(jnp.add, ex[1].wait())

    ex_in, ex_mid, ex_hid, ex_bh, ex_bm, ex_bi = exchanges = [
        exchange(i, n) for i, n in enumerate(["XI", "XM", "XH", "XG", "XD", "XS"])
    ]

    ps, pr, zr = r.ps, r.pr, r.zr
    N = r.N
    INNER = 4
    outer = nb // INNER
    inner = lax.rem(b, INNER)
    base = b - inner
    bits = (lax.rem(a, 2), a // 2)
    flip = ((b, m, a + 1 - 2 * bits[0]), (b, m, lax.rem(a + 2, 4)))
    PSLOTS = spans["PS"][2] // C

    class Piece:
        def __init__(self, p, stack, lanes, first, n, R, F, full=False):
            self.p = p
            self.stack = stack
            self.lanes = pl.ds(*lanes)
            self.first = first
            self.n = n
            HALF, QUART = n // 2, n // 4
            self.SMALL = n // 16
            self.full = full
            self.steps = [0, 1, 2, 3, 5, 6] if full else [0, 1, 2, 3, 4, 5, 6]
            b1, b2 = bits[self.first], bits[1 - self.first]
            self.n1, self.n2 = flip[self.first], flip[1 - self.first]
            self.k1 = b1 * HALF
            self.s1 = (1 - b1) * HALF
            self.k2 = b1 * HALF + b2 * QUART
            self.s2 = b1 * HALF + (1 - b2) * QUART
            self.HALF, self.QUART = HALF, QUART
            self.R, self.F = R, F
            self.XB, self.YB, self.ZB = [spans[f"{x}{stack}"][1] for x in ("XB", "YB", "ZB")]

        def rows(self, start, at, n):
            return N.at[pl.ds(al(start + at, 16), n), self.lanes]

        def get(self, start, at, n):
            return N[pl.ds(al(start + at, 16), n), self.lanes].astype(F32)

        def put(self, start, at, n, v):
            N[pl.ds(al(start + at, 16), n), self.lanes] = v.astype(BF)

        def describe(self, make, i, dev):
            return lambda: remote(*make(), ps.at[self.p], pr.at[self.p, i - 2], dev)

        def moves(self):
            F, R = self.F, self.R
            return {
                2: self.describe(lambda: (self.rows(R, self.s1, self.HALF), self.rows(self.XB, 0, self.HALF)), 2, self.n1),
                3: self.describe(lambda: (self.rows(R, self.s2, self.QUART), self.rows(self.YB, 0, self.QUART)), 3, self.n2),
                4: self.describe(lambda: (self.rows(F, self.k2, self.QUART),) * 2, 4, self.n2),
                5: self.describe(lambda: (self.rows(F, self.k1, self.HALF),) * 2, 5, self.n1),
            }

        def toward(self, which, i):
            j = lax.rem(inner + i, INNER)
            if self.full:
                src, dst = self.rows(self.R, self.k2, self.QUART), self.rows(self.ZB, inner * self.QUART, self.QUART)
            elif which == 0:
                src, dst = self.rows(self.R, self.k2 + j * self.SMALL, self.SMALL), self.rows(self.ZB, inner * self.SMALL, self.SMALL)
            else:
                src = dst = self.rows(self.F, self.k2 + inner * self.SMALL, self.SMALL)
            return remote(src, dst, ps.at[self.p], zr.at[self.p, which], (base + j, m, a))

        def gather(self, which):
            n = (INNER - 1) * (self.QUART if self.full else self.SMALL)
            ref = self.rows(self.ZB, 0, n) if which == 0 else self.rows(self.F, self.k2, n)
            remote(ref, ref, ps.at[self.p], zr.at[self.p, which], (base + lax.rem(inner + 1, INNER), m, a)).wait_recv()

        def drain(self):
            n = self.n + self.n // 2 + (INNER - 1) * (self.QUART if self.full else 2 * self.SMALL)
            ref = N.at[pl.ds(0, n), self.lanes]
            remote(ref, ref, ps.at[self.p], pr.at[self.p, 0], self.n1).wait_send()
            if outer > 1:
                for i in range(1, outer):
                    self.outward(i).wait_send()
            self.out().wait()

        def outward(self, i):
            mine = b // INNER
            q = lax.rem(mine + i, outer)
            ref = r.F.at[self.slot(mine), self.lanes]
            return remote(ref, ref, r.os_.at[self.p, q], r.or_.at[self.p, mine], (q * INNER + inner, m, a))

        def slot(self, q):
            return pl.ds(al(spans[f"OB{self.stack}"][1] + q * self.SMALL, 8), self.SMALL)

        def out(self):
            k = self.stack
            to = r.oR.at[ORDER[k], :, self.lanes] if k < TAPS else r.oDP.at[pl.ds(self.F - dp_at, self.n), self.lanes]
            return local(self.rows(self.F, 0, self.n), to, 15 + self.p)

        def step(self, ph):
            p, moves = self.p, self.moves()
            HALF, QUART, SMALL = self.HALF, self.QUART, self.SMALL
            if ph == 0:
                moves[2]().start()
            elif ph == 1:
                moves[2]().wait_recv()
                self.put(self.R, self.k1, HALF, self.get(self.R, self.k1, HALF) + self.get(self.XB, 0, HALF))
                moves[3]().start()
            elif ph == 2:
                moves[3]().wait_recv()
                self.put(self.R, self.k2, QUART, self.get(self.R, self.k2, QUART) + self.get(self.YB, 0, QUART))
                for i in range(1, INNER):
                    self.toward(0, i).start()
            elif ph == 3:
                self.gather(0)
                n = QUART if self.full else SMALL
                at = self.k2 if self.full else self.k2 + inner * SMALL
                v = self.get(self.R, at, n)
                for i in range(1, INNER):
                    v += self.get(self.ZB, lax.rem(inner + i, INNER) * n, n)
                if outer > 1:
                    mine = b // INNER
                    r.F[self.slot(mine), self.lanes] = v
                    for i in range(1, outer):
                        self.outward(i).start()
                    for i in range(1, outer):
                        q = lax.rem(mine + i, outer)
                        ref = r.F.at[self.slot(q), self.lanes]
                        remote(ref, ref, r.os_.at[p, q], r.or_.at[p, q], (q * INNER + inner, m, a)).wait_recv()
                    v = r.F[self.slot(0), self.lanes]
                    for j in range(1, outer):
                        v += r.F[self.slot(j), self.lanes]
                self.put(self.F, at, n, v)
                if self.full:
                    moves[4]().start()
                else:
                    for i in range(1, INNER):
                        self.toward(1, i).start()
            elif ph == 4:
                self.gather(1)
                moves[4]().start()
            elif ph == 5:
                moves[4]().wait_recv()
                moves[5]().start()
            elif ph == 6:
                moves[5]().wait_recv()
                self.out().start()

    ORDER = (2, 1, 3, 0, 4)
    r_at, dp_at = spans["R"][1], spans["FD"][1]
    dps_at, dpr_at = spans["DPS"][1], r_at + TAPS * C
    thirds = [(q * CH // 3, CH // 3) for q in range(3)]
    pieces = []
    for k in range(TAPS + 1):
        for q in range(3):
            R, F = r_at + k * C, spans[f"F{k}"][1] if k < TAPS else dp_at
            pieces.append(Piece(len(pieces), k, thirds[q], (k + q) % 2, C, R, F))
    late = len(pieces)
    if early:
        pieces.append(Piece(late, 6, (0, CH), 0, CH, r_at + 6 * C, dp_at + C, True))
        pieces.append(Piece(late + 1, 7, (0, CH), 1, CH, r_at + 6 * C + CH, dp_at + C + CH, True))
    else:
        pieces.append(Piece(late, 6, (0, CH), 0, C, r_at + 6 * C, dp_at + C))

    class Share:
        def __init__(self, sem, src, dst, own, to, n):
            self.sem, self.src, self.dst, self.own, self.to, self.n = sem, src, dst, own, to, n

        def copy(self):
            at = lambda start: N.at[pl.ds(al(start, 16), self.n)]
            return remote(at(self.src), at(self.dst), r.shs.at[self.sem], r.shr.at[self.sem], place.partner)

        def sum(self):
            self.copy().wait_recv()
            v = self.own() + N[pl.ds(al(self.dst, 16), self.n), :].astype(F32)
            N[pl.ds(al(self.to, 16), self.n), :] = v.astype(BF)

    def dil_share(sem, at, n):
        own = lambda: N[pl.ds(dpr_at + at, n), :].astype(F32)
        return Share(sem, dps_at + at, dp_at + at, own, dpr_at + at, n)

    share_rest, share_pw, share_mid = dil_share(10, 0, C), dil_share(11, C, CH), dil_share(12, C + CH, CH)

    left = [list(pc.steps) for pc in pieces]
    plan = {}
    for name, which in PLAN:
        if not early:
            which = [p for p in which if p < len(pieces) and not (p == late and name in ("bh", "center", "center2"))]
        plan[name] = [(p, left[p].pop(0)) for p in which if left[p]]
    while any(left):
        most = max(len(x) for x in left)
        plan["end1"] += [(p, x.pop(0)) for p, x in enumerate(left) if len(x) == most]

    def pump(where):
        for p, ph in plan[where]:
            pieces[p].step(ph)

    ld_sto.wait()
    ld_raw.wait()
    CHK = 128
    raw_at = spans["RAW"][1] + m * HR

    def own_raw(i):
        return r.N[pl.ds(al(raw_at + i * CHK, 16), CHK), :].astype(F32).reshape(CHK // 8, 8, CH)

    def sto(i):
        return STO[pl.ds(al(i * CHK, CHK), CHK), :].astype(F32).reshape(CHK // 8, 8, CH)

    def s1(i, acc):
        return acc + jnp.sum(own_raw(i), axis=0) + jnp.sum(sto(i), axis=0)

    acc = lax.fori_loop(0, HR // CHK, s1, jnp.zeros((8, CH), F32))
    mean = row_sum(acc) / float(2 * HR)

    def s2(i, acc):
        u = own_raw(i) - mean
        v = sto(i) - mean
        return acc + jnp.sum(u * u, axis=0) + jnp.sum(v * v, axis=0)

    acc = lax.fori_loop(0, HR // CHK, s2, jnp.zeros((8, CH), F32))
    ex_in[0].start(jnp.concatenate([mean, row_sum(acc)], axis=0))

    ld_seg.wait()
    blocks = SEG.shape[1] // 128

    def make_segs(i, _):
        at = b * (T // 128) - 1 + i
        v = SEG[pl.ds(al(m * ROWS, ROWS), ROWS), pl.ds(al(jnp.clip(at, 0, blocks - 1) * 128, 128), 128)].astype(F32)
        v = jnp.where(jnp.logical_and(at >= 0, at < blocks), v, -1.0)
        for j in range(128):
            SEGX[pl.ds(al(i * 1024 + j * 8, 8), 8), :] = jnp.broadcast_to(v[:, j : j + 1], (8, 128))
        return 0

    lax.fori_loop(0, T // 128 + 2, make_segs, 0)
    BIN0 = 128 * 8

    def make_masks(i, _):
        mid = SEGX[pl.ds(al(i * 128 + BIN0, 128), 128), :]
        for j, o in enumerate((-2, -1, 1, 2)):
            off = SEGX[pl.ds(al(i * 128 + BIN0 + o * 8, 8), 128), :]
            MASK[j, pl.ds(al(i * 128, 128), 128), :] = jnp.where(off == mid, 1.0, 0.0).astype(BF)
        return 0

    lax.fori_loop(0, HR // 128, make_masks, 0)
    x_sig.wait_recv()
    BB = RT // ROWS

    def turn(src, dst, i):
        for h in range(2):
            for row in range(ROWS):
                v = src(h, row).astype(F32)
                for j in range(CH // 128):
                    LANES[pl.ds((h * (CH // 128) + j) * RT + row, BB, stride=ROWS), :] = v[:, j * 128 : (j + 1) * 128]
        for j in range(C // 128):
            dst[pl.ds(al(i * RT, RT), RT), j * 128 : (j + 1) * 128] = LANES[j * RT : (j + 1) * RT, :].astype(BF)

    def turn_x(i, _):
        turn(lambda h, row: RAW[pl.ds(al(h * HR + row * T + i * BB, BB), BB), :], X, i)
        return 0

    lax.fori_loop(0, T // BB, turn_x, 0)
    keep_x = local(X, r.oX, 13)
    keep_x.start()
    x_par.wait_recv()

    def vec(i):
        return jnp.concatenate([PAR[0, i : i + 1, :], PAR[1, i : i + 1, :]], axis=1)

    def hvec(i):
        return jnp.concatenate([PAR[0, i : i + 1, 0:HH], PAR[1, i : i + 1, 0:HH]], axis=1)

    la = ex_in[0].wait()
    n_own = float(2 * HR)
    both = lambda x, y: jnp.concatenate([jnp.concatenate([x[i], y[i]], axis=1) for i in range(2)], axis=0)
    if early:
        ex_in[1].start(jnp.concatenate(merged(la, n_own), axis=0))
        lb = ex_in[1].wait()
        v = both((lb[0][0:1], lb[0][1:2]), (lb[1][0:1], lb[1][1:2]))
        mu_in, sq = v[0:1], v[1:2]
    else:
        ex_in[1].start(both(merged(la[0:na], n_own), merged(la[na : 2 * na], n_own)))
        mu_in, sq = merged(ex_in[1].wait(), n_own * na)
    inv_in = lax.rsqrt(sq / total_in + EPSILON)
    gain_in, shift_in = vec(0), vec(1)
    scale_in = gain_in * inv_in
    ST[0:1, :] = mu_in
    ST[1:2, :] = inv_in
    ST[2:3, :] = gain_in
    HB = 256

    def make_hidden(i, last):
        at = al(i * HB, HB)
        pre = (X[pl.ds(at, HB), :].astype(F32) - mu_in) * scale_in + shift_in
        h = gelu_up(pre)
        H0[pl.ds(al(at + 16, 16), HB), :] = h.astype(BF)
        H1[pl.ds(at, HB), :] = jnp.concatenate([last, h[: HB - 8]], axis=0).astype(BF)
        return h[HB - 8 :]

    lax.fori_loop(0, HR // HB, make_hidden, jnp.zeros((8, C), F32))
    hs, hr = r.hs, r.hr
    down = (jnp.maximum(b - 1, 0), m, a)
    up = (jnp.minimum(b + 1, nb - 1), m, a)
    has_down, has_up = b > 0, b < nb - 1

    def when_down(f):
        pl.when(has_down)(f)

    def when_up(f):
        pl.when(has_up)(f)

    class Rims:
        def __init__(self, to_down, from_up, to_up, from_down, i):
            self.down = remote(to_down, from_up, hs.at[i], hr.at[i], down)
            self.up = remote(to_up, from_down, hs.at[i + 1], hr.at[i + 1], up)

        def start_down(self):
            when_down(self.down.start)

        def start_up(self):
            when_up(self.up.start)

        def wait_from_up(self):
            when_up(self.down.wait_recv)

        def wait_from_down(self):
            when_down(self.up.wait_recv)

        def drain(self):
            when_down(self.down.wait_send)
            when_up(self.up.wait_send)

    def clear_halo(ref):
        @pl.when(jnp.logical_not(has_down))
        def _():
            ref[0:16, :] = jnp.zeros((16, C), BF)

        @pl.when(jnp.logical_not(has_up))
        def _():
            ref[pl.ds(HR + 16, 16), :] = jnp.zeros((16, C), BF)

    def halos(ref, i):
        return Rims(ref.at[pl.ds(16, 16)], ref.at[pl.ds(HR + 16, 16)], ref.at[pl.ds(HR, 16)], ref.at[pl.ds(0, 16)], i)

    h_halo = halos(H0, 0)
    h_halo.start_down()
    h_halo.start_up()
    clear_halo(H0)

    def by_one_bin(even, odd):
        v = even[0:32, :].astype(F32)
        odd[0:16, :] = v[8:24].astype(BF)
        v = even[pl.ds(HR, 32), :].astype(F32)
        odd[pl.ds(HR, 16), :] = v[8:24].astype(BF)

    MJ = {-2: 0, -1: 1, 1: 2, 2: 3}

    def shifted(even, odd, o, at, n):
        if o % 2 == 0:
            v = even[pl.ds(al(at + (o + 2) * 8, 16), n), :]
        else:
            v = odd[pl.ds(al(at + (o + 1) * 8, 16), n), :]
        if o != 0:
            v = v * wide(MASK[MJ[o], pl.ds(al(at, 16), n), :], C // 128)
        return v

    def w(k):
        return W[k * C : (k + 1) * C, :]

    def put_lanes(v, n):
        for j in range(C // 128):
            LANES[j * RT : j * RT + n, :] = v[:, j * 128 : (j + 1) * 128]

    def get_lanes(at, n):
        return jnp.concatenate([LANES[pl.ds(al(j * RT + at, 8), n), :] for j in range(C // 128)], axis=1)

    for c in (*ld_w,):
        c.wait()
    for c in x_w:
        c.wait_recv()
    POOL, DIFF, SUM = r.POOL, r.DIFF, r.SUM
    SUM[...] = jnp.zeros_like(SUM)

    def conv_tile(i):
        at = al(i * RT, RT)
        acc = None
        for k in range(TAPS):
            d = dot(shifted(H0, H1, k - 2, at, RT), w(k), 1, 0)
            acc = d if acc is None else acc + d
        put_lanes(acc, RT)

        def pool(j, s):
            v = get_lanes(j * 128, 128).reshape(8, 2, 8, C)
            c0, c1 = v[:, 0], v[:, 1]
            d = c0 - c1
            p = jnp.maximum(c0, c1) + jnp.log(1.0 + jnp.exp(-jnp.abs(d)))
            to = pl.ds(al(i * (RT // 2) + j * 64, 64), 64)
            POOL[to, :] = p.reshape(64, C)
            DIFF[to, :] = d.reshape(64, C)
            return s + jnp.sum(p, axis=0)

        SUM[...] += lax.fori_loop(0, RT // 128, pool, jnp.zeros((8, C), F32))

    NT = HR // RT

    def conv_loop(i, _):
        conv_tile(i)
        return 0

    lax.fori_loop(1, NT - 1, conv_loop, 0)
    h_halo.wait_from_up()
    h_halo.wait_from_down()
    by_one_bin(H0, H1)
    lax.fori_loop(0, 2, lambda i, _: (conv_tile(i * (NT - 1)), 0)[1], 0)

    mean = row_sum(SUM[...]) / float(PR)

    def m2_mid(i, acc):
        v = POOL[pl.ds(al(i * 128, 128), 128), :].reshape(16, 8, C) - mean
        return acc + jnp.sum(v * v, axis=0)

    acc = lax.fori_loop(0, PR // 128, m2_mid, jnp.zeros((8, C), F32))
    begin_stats(ex_mid, mean, row_sum(acc), float(PR))

    ld_cot.wait()
    x_cot.wait_recv()

    def turn_ct(i, _):
        turn(lambda h, row: COT[h][pl.ds(al(row * S + i * BB, BB), BB), :], CT, i)
        return 0

    lax.fori_loop(0, S // BB, turn_ct, 0)
    ld_pw.wait()
    x_pw.wait_recv()
    GT, DO, E0 = part("GT"), part("DO"), part("E0")
    E1, GML = part("GM"), [part("GM", 0, PR), part("GM", PR, PR)]

    def make_gt(i, _):
        at = pl.ds(al(i * 256, 256), 256)
        GT[at, :] = dot(CT[at, :], PW[...], 1, 1)
        return 0

    lax.fori_loop(0, PR // 256, make_gt, 0)
    for c in ld_d:
        c.wait()
    for c in x_d:
        c.wait_recv()

    def dt(k):
        return DT[k * HC : (k + 1) * HC, :]

    mu_mid, sq = finish_stats(ex_mid, float(PR))
    inv_mid = lax.rsqrt(sq / total_mid + EPSILON)
    gain_mid, shift_mid = vec(2), vec(3)
    scale_mid = gain_mid * inv_mid

    def make_mid(i, _):
        at = pl.ds(al(i * 128, 128), 128)
        HM[at, :] = gelu_up((POOL[at, :] - mu_mid) * scale_mid + shift_mid).astype(BF)
        return 0

    lax.fori_loop(0, PR // 128, make_mid, 0)

    packed = early
    WIN = 32 * ROWS
    nrim = WIN if packed else rim
    RS = [part("RS", 0, nrim), part("RS", rim, nrim)]
    RR = [part("RR", 0, nrim), part("RR", rim, nrim)]

    def ended(s):
        before = SEGX[pl.ds(al(BIN0 + (s - 33) * 16, 8), 8), :]
        after = SEGX[pl.ds(al(BIN0 + s * 16, 8), 8), :]
        return wide(jnp.where(before != after, 1.0, 0.0), HC // 128).reshape(1, ROWS, HC)

    ended_up, ended_down = ended(S), ended(0)

    def choose(flag, x, y):
        three = (WIN // ROWS, ROWS, HC)
        return jnp.where(flag > 0.5, x.reshape(three), y.reshape(three)).reshape(WIN, HC)

    def pack_up(start):
        at = lambda s: r.F[pl.ds(start + s * ROWS, WIN), :]
        return choose(ended_up, at(S - 32), at(S - DIL)).astype(BF)

    def pack_down(start):
        at = lambda s: r.F[pl.ds(start + s * ROWS, WIN), :]
        return choose(ended_down, at(DIL - 32), at(0)).astype(BF)

    def unpack(flag, ref, v, first):
        ref[...] = jnp.zeros((rim, HC), F32)
        a, c = first * ROWS, (first + DIL - 32) * ROWS
        ref[a : a + WIN, :] = choose(flag, jnp.zeros((WIN, HC), F32), v)
        ref[c : c + WIN, :] = choose(flag, v, ref[c : c + WIN, :])

    p_rims = Rims(RS[1], RR[1], RS[0], RR[0], 2)
    QR = PR // 2
    e0_at, e1_at, do_at, hm_at = spans["E0"][1], spans["GM"][1], spans["DO"][1], spans["HM"][1]

    def pick(i, table):
        v = jnp.int32(table[-1])
        for n in range(len(table) - 2, -1, -1):
            v = jnp.where(i == n, table[n], v)
        return v

    halves_of = (1, 0, 0, 1, 0, 1)
    taps_of = (0, 2, 0, 2, 1, 1)
    starts = [{0: e0_at + rim, 1: do_at, 2: e1_at}[k] + q * QR for k, q in zip(taps_of, halves_of)]

    def product(i, _):
        v = dot(
            r.M[pl.ds(al(hm_at + pick(i, halves_of) * QR, 16), QR), :],
            r.M[pl.ds(al(dt0 + pick(i, taps_of) * HC, 16), HC), :],
            1, 1,
        )
        r.F[pl.ds(al(pick(i, starts), 8), QR), :] = v

        @pl.when(i == 0)
        def _():
            RS[0][...] = pack_up(e0_at + rim) if packed else E0[PR : PR + rim, :].astype(BF)
            p_rims.start_up()

        @pl.when(i == 1)
        def _():
            RS[1][...] = pack_down(e1_at) if packed else E1[0:rim, :].astype(BF)
            p_rims.start_down()

        return 0

    lax.fori_loop(0, len(halves_of), product, 0)

    def take_rims(rims, low, high):
        rims.wait_from_down()
        rims.wait_from_up()

        @pl.when(has_down)
        def _():
            v = RR[0][...].astype(F32)
            if packed:
                unpack(ended_down, low, v, 1)
            else:
                low[...] = v

        @pl.when(jnp.logical_not(has_down))
        def _():
            low[...] = jnp.zeros((rim, HC), F32)

        @pl.when(has_up)
        def _():
            v = RR[1][...].astype(F32)
            if packed:
                unpack(ended_up, high, v, 0)
            else:
                high[...] = v

        @pl.when(jnp.logical_not(has_up))
        def _():
            high[...] = jnp.zeros((rim, HC), F32)

    take_rims(p_rims, part("E0", 0, rim), part("GM", PR, rim))

    def same(i, by):
        def pick(off):
            return SEGX[pl.ds(al(i * 256 + BIN0 + off * 16, 16), 256), :].reshape(16, 2, 8, 128)[:, 0]

        return wide(jnp.where(pick(0) == pick(by), 1.0, 0.0).reshape(128, 128), HC // 128)

    def add_dil(i, s):
        at = pl.ds(al(i * 128, 128), 128)
        v = DO[at, :]
        v += same(i, -DIL) * E0[pl.ds(al(i * 128 + 8, 8), 128), :]
        v += same(i, DIL) * E1[pl.ds(al(i * 128 + DIL * 8, 8), 128), :]
        DO[at, :] = v
        return s + jnp.sum(v.reshape(16, 8, HC), axis=0)

    acc = lax.fori_loop(0, PR // 128, add_dil, jnp.zeros((8, HC), F32))
    mean = row_sum(acc) / float(PR)

    def m2_hid(i, acc):
        v = DO[pl.ds(al(i * 128, 128), 128), :].reshape(16, 8, HC) - mean
        return acc + jnp.sum(v * v, axis=0)

    acc = lax.fori_loop(0, PR // 128, m2_hid, jnp.zeros((8, HC), F32))
    begin_stats(ex_hid, mean, row_sum(acc), float(PR))
    SL = [part("RAW", 0, PR), part("RAW", PR, PR)]

    def make_slope(i, _):
        at = pl.ds(al(i * 64, 64), 64)
        _, slope = gelu_both((POOL[at, :] - mu_mid) * scale_mid + shift_mid)
        SL[0][at, :] = slope[:, :CH].astype(BF)
        SL[1][at, :] = slope[:, CH:].astype(BF)
        return 0

    lax.fori_loop(0, PR // 64, make_slope, 0)


    def pool_weights(i, _):
        at = pl.ds(al(i * 64, 64), 64)
        DIFF[at, :] = 0.5 + 0.5 * jnp.tanh(0.5 * DIFF[at, :])
        return 0

    lax.fori_loop(0, PR // 64, pool_weights, 0)
    mu_hid, sq = finish_stats(ex_hid, float(PR))
    inv_hid = lax.rsqrt(sq / total_mid + EPSILON)
    gain_hid, shift_hid = hvec(4), hvec(5)
    HT = part("HT")

    def make_top(i, s):
        at = pl.ds(al(i * 128, 128), 128)
        xhat = (DO[at, :] - mu_hid) * inv_hid
        h, slope = gelu_both(xhat * gain_hid + shift_hid)
        HT[at, :] = h.astype(BF)
        da = slope * GT[at, :]
        GT[at, :] = da
        DO[at, :] = xhat
        return (
            s[0] + jnp.sum((da * xhat).reshape(16, 8, HC), axis=0),
            s[1] + jnp.sum(da.reshape(16, 8, HC), axis=0),
        )

    zero = jnp.zeros((8, HC), F32)
    sg, sb = lax.fori_loop(0, PR // 128, make_top, (zero, zero))
    begin_sums(ex_bh, row_sum(sg), row_sum(sb))

    OB = 256

    def make_out(i, _):
        at = pl.ds(al(i * OB, OB), OB)
        v = (POOL[at, :] + dot(HT[at, :], PW[...], 1, 0)).astype(BF)
        COT[0][at, :] = v[:, :CH]
        COT[1][at, :] = v[:, CH:]
        return 0

    lax.fori_loop(0, PR // OB, make_out, 0)
    cot_other = r.N.at[pl.ds(al(spans["COTR"][1] + other * PR, 16), PR)]
    o_own = local(cot_mine, r.oOUT.at[m], 14)
    o_own.start()
    o_cross = cross(cot_other, r.oOUT.at[m], 12)
    o_cross.start()
    gp = dot(HT[...], CT[...], 0, 0)
    N[dpr_at + C : dpr_at + C + HC, :] = jnp.where(m == 0, gp[:, :CH], gp[:, CH:]).astype(BF)
    N[dps_at + C : dps_at + C + HC, :] = jnp.where(m == 0, gp[:, CH:], gp[:, :CH]).astype(BF)
    share_pw.copy().start()

    share_pw.sum()
    pump("bh")
    v = finish_sums(ex_bh)
    ST[8:10, 0:HC] = v
    ST[8:10, HC:] = jnp.zeros((2, C - HC), F32)
    scale = gain_hid * inv_hid
    mg, mb = v[0:1] / total_mid, v[1:2] / total_mid
    GD = [part("GD", k * PR, PR) for k in range(3)]

    def make_gd(i, _):
        at = pl.ds(al(i * 128, 128), 128)
        g = (scale * (GT[at, :] - mb - DO[at, :] * mg)).astype(BF)
        GD[1][at, :] = g
        E0[pl.ds(al(i * 128 + rim, 16), 128), :] = g.astype(F32)
        return 0

    lax.fori_loop(0, PR // 128, make_gd, 0)
    p_rims.drain()
    if packed:
        RS[0][...] = pack_up(e0_at + rim)
        RS[1][...] = pack_down(e0_at + rim)
        g_rims = Rims(RS[1], RR[1], RS[0], RR[0], 4)
    else:
        g_rims = Rims(part("GD", PR, rim), RR[1], part("GD", 2 * PR - rim, rim), RR[0], 4)
    g_rims.start_up()
    g_rims.start_down()


    def to_gm(i, v, add):
        at = pl.ds(al(i * QR, QR), QR)
        for h in range(2):
            u = v[:, h * CH : (h + 1) * CH]
            GML[h][at, :] = GML[h][at, :] + u if add else u

    def mid_center(i, _):
        to_gm(i, dot(GD[1][pl.ds(al(i * QR, QR), QR), :], dt(1), 1, 0), False)
        return 0

    lax.fori_loop(0, 2, mid_center, 0)
    gd_at = spans["GD"][1]

    def dil_grad(k, to):
        g = dot(N[pl.ds(al(gd_at + k * PR, 16), PR), :], HM[...], 0, 0)
        own = jnp.where(m == 0, g[:HH], g[HH:]).astype(BF)
        for_partner = jnp.where(m == 0, g[HH:], g[:HH]).astype(BF)
        for h in range(2):
            at = to + h * HH
            N[pl.ds(al(dpr_at + at, 16), HH), :] = own[:, h * CH : (h + 1) * CH]
            N[pl.ds(al(dps_at + at, 16), HH), :] = for_partner[:, h * CH : (h + 1) * CH]

    dil_grad(1, C + CH)
    share_mid.copy().start()
    pump("center")
    share_mid.sum()
    pump("center2")
    gd_of = [spans["GD"][1], spans["GD"][1] + 2 * PR]

    def mid_side(by, i):
        g_at = gd_of[0 if by > 0 else 1]

        def body(j, _):
            n = i * (QR // 128) + j
            v = same(n, by) * E0[pl.ds(al(n * 128 + rim + by * 8, 8), 128), :]
            N[pl.ds(al(g_at + n * 128, 16), 128), :] = v.astype(BF)
            return 0

        lax.fori_loop(0, QR // 128, body, 0)
        g = N[pl.ds(al(g_at + i * QR, 16), QR), :]
        to_gm(i, dot(g, dt(0 if by > 0 else 2), 1, 0), True)

    mid_side(DIL, 0)
    mid_side(-DIL, 1)
    take_rims(g_rims, part("E0", 0, rim), part("E0", PR + rim, rim))
    pump("rims")
    mid_side(DIL, 1)
    mid_side(-DIL, 0)

    def gm(at):
        return jnp.concatenate([GML[0][at, :], GML[1][at, :]], axis=1)

    def make_dmid(i, s):
        at = pl.ds(al(i * 64, 64), 64)
        xhat = (POOL[at, :] - mu_mid) * inv_mid
        da = jnp.concatenate([SL[0][at, :], SL[1][at, :]], axis=1).astype(F32) * gm(at)
        GML[0][at, :] = da[:, :CH]
        GML[1][at, :] = da[:, CH:]
        return (
            s[0] + jnp.sum((da * xhat).reshape(8, 8, C), axis=0),
            s[1] + jnp.sum(da.reshape(8, 8, C), axis=0),
        )

    zero = jnp.zeros((8, C), F32)
    sg, sb = lax.fori_loop(0, PR // 64, make_dmid, (zero, zero))
    g_rims.drain()
    o_own.wait()
    o_cross.wait_send()
    keep_x.wait()
    begin_sums(ex_bm, row_sum(sg), row_sum(sb))

    lax.fori_loop(0, 2, lambda i, _: (dil_grad(2 * i, i * CH), 0)[1], 0)
    share_rest.copy().start()
    share_rest.sum()
    pump("bm")
    v = finish_sums(ex_bm)
    ST[6:8, :] = v
    mg, mb = v[0:1] / total_mid, v[1:2] / total_mid
    pump("bm2")
    GC0, GC1 = part("GC0"), H1

    def make_gc(i, last):
        at = pl.ds(al(i * 64, 64), 64)
        xhat = (POOL[at, :] - mu_mid) * inv_mid
        g = CT[at, :].astype(F32) + scale_mid * (gm(at) - mb - xhat * mg)
        g0 = g * DIFF[at, :]
        g1 = g - g0
        v = jnp.stack([g0.reshape(8, 8, C), g1.reshape(8, 8, C)], axis=1).reshape(128, C)
        GC0[pl.ds(al(i * 128 + 16, 16), 128), :] = v.astype(BF)
        GC1[pl.ds(al(i * 128, 128), 128), :] = jnp.concatenate([last, v[:120]], axis=0).astype(BF)
        return v[120:]

    lax.fori_loop(0, PR // 64, make_gc, jnp.zeros((8, C), F32))
    g_halo = halos(GC0, 6)
    g_halo.start_down()
    g_halo.start_up()
    clear_halo(GC0)
    XX = part("XX")
    back_x = local(r.oX, XX, 13)

    own_at = spans["GM"][1]
    h0_at = spans["H0"][1] + 16
    ps_at = spans["PS"][1]
    HALF = C // 2
    first_half = (1 - bits[0]) * HALF

    def tap_share(i, j):
        at = first_half if j == 0 else HALF - first_half
        own = lambda: r.F[pl.ds(al(own_at + i % 2 * PR + at, 8), HALF), :]
        return Share(2 * i + j, ps_at + i % PSLOTS * C + at, spans[f"F{i}"][1] + at, own, r_at + i * C + at, HALF)

    shares = [tap_share(i, j) for i in range(TAPS) for j in range(2)]

    def masked(k):
        def body(j, _):
            XX[pl.ds(al(j * 256, 256), 256), :] = shifted(GC0, GC1, 2 - k, j * 256, 256)
            return 0

        lax.fori_loop(0, HR // 256, body, 0)

    def half_tap(it, _):
        i, j = it // 2, lax.rem(it, 2)
        for n in range(TAPS):

            @pl.when(it == 2 * n)
            def _(n=n):
                if n == 1:
                    g_halo.wait_from_up()
                    g_halo.wait_from_down()
                    by_one_bin(GC0, GC1)
                if n >= PSLOTS:
                    for c in shares[2 * (n - PSLOTS) : 2 * (n - PSLOTS) + 2]:
                        c.copy().wait_send()
                masked(ORDER[n])

        odd = lax.rem(i, 2)
        at = jnp.where(j == 0, first_half, HALF - first_half)
        v = dot(r.M[h0_at : h0_at + HR, pl.ds(al(at, 128), HALF)], XX[...], 0, 0)
        r.F[pl.ds(al(own_at + odd * PR + at, 8), HALF), :] = jnp.where(m == 0, v[:, :CH], v[:, CH:])
        N[pl.ds(al(ps_at + lax.rem(i, PSLOTS) * C + at, 16), HALF), :] = jnp.where(m == 0, v[:, CH:], v[:, :CH]).astype(BF)
        for n in range(2 * TAPS):

            @pl.when(it == n)
            def _(n=n):
                shares[n].copy().start()
                if n:
                    shares[n - 1].sum()
                pump(f"tap{n}")

        return 0

    lax.fori_loop(0, 2 * TAPS, half_tap, 0)
    shares[-1].sum()
    pump("taps")

    back_x.start()
    for c in shares[2 * (TAPS - PSLOTS) :]:
        c.copy().wait_send()
    mu, inv, gain, shift = ST[0:1, :], ST[1:2, :], gain_in, shift_in
    RB = 256
    DA = [part("RAW", 0, HR), part("RAW", HR, HR)]

    def tile(i, s):
        at = i * RB
        acc = None
        for k in range(TAPS):
            d = dot(shifted(GC0, GC1, 2 - k, at, RB), w(k), 1, 1)
            acc = d if acc is None else acc + d
        put_lanes(acc, RB)
        for n in range(HR // RB):

            @pl.when(i == n)
            def _(n=n):
                pump(f"tile{2 * n}")
                if n == 0:
                    back_x.wait()


        def back(j, s):
            to = pl.ds(al(at + j * 64, 64), 64)
            xhat = (XX[to, :].astype(F32) - mu) * inv
            _, slope = gelu_both(xhat * gain + shift)
            da = slope * get_lanes(j * 64, 64)
            DA[0][to, :] = da[:, :CH].astype(BF)
            DA[1][to, :] = da[:, CH:].astype(BF)
            return (
                s[0] + jnp.sum((da * xhat).reshape(8, 8, C), axis=0),
                s[1] + jnp.sum(da.reshape(8, 8, C), axis=0),
            )

        s = lax.fori_loop(0, RB // 64, back, s)
        for n in range(HR // RB):

            @pl.when(i == n)
            def _(n=n):
                pump(f"tile{2 * n + 1}")

        return s

    s = lax.fori_loop(0, HR // RB, tile, (zero, zero))
    begin_sums(ex_bi, row_sum(s[0]), row_sum(s[1]))
    d_own = local(raw_mine, r.oDA.at[m], 12)
    d_own.start()
    d_cross = cross(r.N.at[pl.ds(al(spans["RAW"][1] + other * HR, 16), HR)], r.oDA.at[m], 13)
    d_cross.start()
    pump("end0")
    pump("end1")
    ST[4:6, :] = finish_sums(ex_bi)
    ST[3:4, :] = jnp.zeros((1, C), F32)
    ST[10:16, :] = jnp.zeros((6, C), F32)
    o_st = local(ST, r.oST, 14)
    o_st.start()
    for pc in pieces:
        pc.drain()
    for c in (share_rest, share_pw, share_mid):
        c.copy().wait_send()
    d_own.wait()
    o_st.wait()
    d_cross.wait()
    o_cross.wait_recv()
    for c in crosses:
        c.wait_send()
    for e in exchanges:
        e[0].drain()
        e[1].drain()
    h_halo.drain()
    g_halo.drain()


def call_main(axes, sig, seg, cot, wide_taps, taps, pw, vectors):
    nb, nm, na = axes
    CH = sig.shape[1]
    C = 2 * CH
    HC = pw.shape[0]
    assert HC == CH
    HR = sig.shape[0] // 2
    PR = cot.shape[0] // 2
    T, S = HR // ROWS, PR // ROWS
    rim = (DIL + 1) * ROWS
    RT = 512
    NA = nm * na
    early = nb == 4
    NP = 3 * (TAPS + 1) + (2 if early else 1)
    inputs = dict(sig=sig, seg=seg, cot=cot, wide=wide_taps, taps=taps, pw=pw)
    inputs.update({f"v{i}": v for i, v in enumerate(vectors)})
    sd = jax.ShapeDtypeStruct
    outs = dict(
        oX=sd((HR, C), BF),
        oDA=sd((2, HR, CH), BF),
        oOUT=sd((2, PR, CH), BF),
        oR=sd((TAPS, C, CH), BF),
        oDP=sd((2 * C, CH), BF),
        oST=sd((16, C), F32),
    )
    spans = {}

    def lay(pool, start, items):
        for name, n in items:
            spans[name] = (pool, start, n)
            start += n
        return start

    end = lay("N", 0, [("RAW", 2 * HR), ("STO", HR), ("COTR", 2 * PR), ("HT", PR), ("RS", 2 * rim), ("RR", 2 * rim)])
    lay("N", spans["STO"][1], [("DPS", 2 * C)])
    lay("N", spans["COTR"][1], [(f"XB{p}", C // 2) for p in range(TAPS)])
    lay("N", spans["HT"][1], [(f"YB{p}", C // 4) for p in range(TAPS)])
    lay("N", spans["RS"][1], [(f"F{p}", C) for p in range(2)])
    end = lay("N", end, [("GD", 3 * PR)])
    lay("N", spans["GD"][1], [("R", (TAPS + 2) * C)])
    end = max(end, spans["R"][1] + (TAPS + 2) * C)
    end = lay("N", end, [(f"F{p}", C) for p in range(2, TAPS)] + [("FD", 2 * C)])
    lay("N", spans["RAW"][1] + HR, [("PS", 2 * C)])
    sizes = {p: C for p in range(TAPS + 1)} | ({6: CH, 7: CH} if early else {6: C})
    rest = range(TAPS, len(sizes))
    end = lay("N", end, [(f"XB{p}", sizes[p] // 2) for p in rest] + [(f"YB{p}", sizes[p] // 4) for p in rest])
    n_rows = lay("N", end, [(f"ZB{p}", C // 2 if p > 5 and early else C // 4) for p in range(len(sizes))])
    end = lay("M", 0, [("X", HR), ("gap", 32), ("HM", PR), ("CT", PR), ("H0", HR + 32), ("H1", HR + 32)])
    lay("M", 0, [("GC0", HR + 32)])
    lay("M", spans["HM"][1], [("XX", HR)])
    m_rows = lay("M", end, [("W", TAPS * C), ("PW", HC), ("DT", 3 * HC)])
    f_rows = lay("F", 0, [("E0", PR + 2 * rim), ("GM", 2 * PR), ("DO", PR), ("GT", PR)])
    V = pltpu.VMEM
    DMA = pltpu.SemaphoreType.DMA
    scratch = dict(
        N=V((n_rows, CH), BF),
        M=V((m_rows, C), BF),
        F=V((f_rows, CH), F32),
        LANES=V((C // 128 * RT, 128), F32),
        MASK=V((4, HR, 128), BF),
        SEG=V(seg.shape, jnp.int32),
        SEGX=V(((T + 256) * ROWS, 128), F32),
        PAR=V((2, 8, CH), F32),
        ST=V((16, C), F32),
        SUM=V((8, C), F32),
        POOL=V((PR, C), F32),
        DIFF=V((PR, C), F32),
        lsem=DMA((15 + NP,)),
        shs=DMA((13,)), shr=DMA((13,)),
        csem_s=DMA((14,)), csem_r=DMA((14,)),
        as_=DMA((6,)), ar_=DMA((6,)),
        bs_=DMA((6,)), br_=DMA((6,)),
        hs=DMA((8,)), hr=DMA((8,)),
        ps=DMA((NP,)), pr=DMA((NP, 4)),
        zr=DMA((NP, 2)),
    )
    for i, (name, width) in enumerate([("XI", C), ("XM", C), ("XH", HC), ("XG", HC), ("XD", C), ("XS", C)]):
        if early:
            sizes_ab = (nb * na, nm) if i == 0 else (nm, nb * na)
            widths = (CH, CH) if i == 0 else (width, width)
        else:
            sizes_ab = (NA, nb)
            widths = (CH if i == 0 else width, width)
        for x, n, lanes in zip("AB", sizes_ab, widths):
            scratch[name + x] = V((n, 2, lanes), F32)
    outer = nb // 4
    if outer > 1:
        scratch.update(os_=DMA((NP, outer)), or_=DMA((NP, outer)))
        n = outer * (C // 16)
        assert lay("F", spans["E0"][1], [(f"OB{p}", n) for p in range(TAPS)]) <= spans["GM"][1]
        assert lay("F", spans["DO"][1], [(f"OB{p}", n) for p in range(TAPS, TAPS + 2)]) <= f_rows
    names = list(inputs) + list(outs) + list(scratch)
    anyspec = pl.BlockSpec(memory_space=pl.ANY)
    vmem = pl.BlockSpec(memory_space=pltpu.VMEM)
    res = pl.pallas_call(
        functools.partial(main_body, (nb, nm, na, T, S, CH, HC), names, spans),
        out_shape=list(outs.values()),
        in_specs=[vmem if n.startswith("v") else anyspec for n in inputs],
        out_specs=[anyspec] * len(outs),
        scratch_shapes=list(scratch.values()),
        compiler_params=pltpu.CompilerParams(
            collective_id=0, has_side_effects=True, vmem_limit_bytes=VMEM_BYTES
        ),
        cost_estimate=pl.CostEstimate(flops=44_000_000_000, bytes_accessed=40_000_000, transcendentals=8_000_000),
        name="forward_and_backward",
    )(*inputs.values())
    return dict(zip(outs, res, strict=True))


def last_body(dims, sig, da, out, rr, dp, stats, gs, oo, gw, dk, pw, g0, g1, g2, g3, g4, g5,
              sig_v, da_v, out_v, rr_v, dp_v, st_v, gs_v, oo_v, gw_v, dk_v, pw_v, lanes, ls, ss):
    CH, total_in = dims
    m = lax.axis_index("mp")
    taps = rr.shape[0]
    T, S = sig.shape[1], oo.shape[1]
    HH = g4.shape[0]
    copy = pltpu.make_async_copy

    def load(src, dst, i):
        return copy(src, dst, ls.at[i])

    def load_tap(k):
        return load(rr.at[k], rr_v.at[k], k)

    def load_half(h):
        rows = pl.ds(h * ROWS, ROWS)
        return [
            load(da.at[h], da_v.at[h], taps + 3 * h),
            load(sig.at[rows], sig_v.at[rows], taps + 3 * h + 1),
            load(out.at[h], out_v.at[h], taps + 3 * h + 2),
        ]

    ld_st = load(stats, st_v, taps + 6)
    ld_dp = load(dp, dp_v, taps + 7)
    ld_st.start()
    for k in range(taps):
        load_tap(k).start()
    for h in range(2):
        for c in load_half(h):
            c.start()
    ld_dp.start()

    def store_tap(k):
        return copy(gw_v.at[k], gw.at[k], ss.at[k])

    def tap(k, _):
        load_tap(k).wait()

        def part(i, _):
            at = pl.ds(al(i * 96, 96), 96)
            gw_v[k, at, :] = rr_v[k, at, :].astype(F32)
            return 0

        lax.fori_loop(0, rr.shape[1] // 96, part, 0)
        store_tap(k).start()
        return 0

    lax.fori_loop(0, taps, tap, 0)
    ld_st.wait()
    st = st_v[:, pl.ds(al(m * CH, CH), CH)]
    mu, inv, gain, gg, gb = [st[i : i + 1] for i in (0, 1, 2, 4, 5)]
    scale = gain * inv
    mg, mb = gg / total_in, gb / total_in
    BB = 64
    n = BB * ROWS

    def store_gs(h, c):
        at = (pl.ds(h * ROWS, ROWS), pl.ds(al(c * BB, BB), BB))
        return copy(gs_v.at[at], gs.at[at], ss.at[taps + h * (T // BB) + c])

    def store_oo(h):
        at = pl.ds(h * ROWS, ROWS)
        return copy(oo_v.at[at], oo.at[at], ss.at[taps + 2 * (T // BB) + h])

    def fill(v):
        for j in range(CH // 128):
            lanes[j * n : (j + 1) * n, :] = v[:, j * 128 : (j + 1) * 128].astype(F32)

    def half(h, _):
        for c in load_half(h):
            c.wait()

        def block(c, _):
            fill(da_v[h, pl.ds(al(c * n, n), n), :])
            bins = pl.ds(al(c * BB, BB), BB)
            for row in range(ROWS):
                for j in range(CH // 128):
                    l = slice(j * 128, (j + 1) * 128)
                    d = lanes[pl.ds(j * n + row, BB, stride=ROWS), :]
                    xhat = (sig_v[h * ROWS + row, bins, l].astype(F32) - mu[:, l]) * inv[:, l]
                    gs_v[h * ROWS + row, bins, l] = scale[:, l] * (d - mb[:, l] - xhat * mg[:, l])
            store_gs(h, c).start()
            return 0

        lax.fori_loop(0, T // BB, block, 0)

        def block2(c, _):
            fill(out_v[h, pl.ds(al(c * n, n), n), :])
            bins = pl.ds(al(c * BB, BB), BB)
            for row in range(ROWS):
                for j in range(CH // 128):
                    oo_v[h * ROWS + row, bins, j * 128 : (j + 1) * 128] = lanes[pl.ds(j * n + row, BB, stride=ROWS), :].astype(BF)
            return 0

        lax.fori_loop(0, S // BB, block2, 0)
        store_oo(h).start()
        return 0

    lax.fori_loop(0, 2, half, 0)
    ld_dp.wait()
    for k, at in enumerate((0, 6, 2)):
        for h in range(2):
            dk_v[k * HH : (k + 1) * HH, h * CH : (h + 1) * CH] = dp_v[(at + h) * HH : (at + h + 1) * HH, :].astype(F32)
    pw_v[...] = dp_v[4 * HH : 6 * HH, :].astype(F32)
    st_dk = copy(dk_v, dk, ss.at[taps + 2 * (T // BB) + 2])
    st_pw = copy(pw_v, pw, ss.at[taps + 2 * (T // BB) + 3])
    st_dk.start()
    st_pw.start()
    for ref, i in ((g0, 4), (g1, 5), (g2, 6), (g3, 7)):
        ref[...] = st[i : i + 1].reshape(CH)
    hid = st_v[8:10, : 2 * HH]
    hid = jnp.where(m == 0, hid[:, :HH], hid[:, HH:])
    g4[...] = hid[0:1].reshape(HH)
    g5[...] = hid[1:2].reshape(HH)
    for k in range(taps):
        store_tap(k).wait()
    for h in range(2):
        for c in range(T // BB):
            store_gs(h, c).wait()
        store_oo(h).wait()
    st_dk.wait()
    st_pw.wait()


def call_last(axes, sig, o):
    nb, nm, na = axes
    rows, T, CH = sig.shape
    S = T // 2
    C = 2 * CH
    HC = CH
    HH = HC // 2
    rr = o["oR"]
    total_in = float(rows * T * nb * na)
    sd = jax.ShapeDtypeStruct
    V = pltpu.VMEM
    anyspec = pl.BlockSpec(memory_space=pl.ANY)
    vmem = pl.BlockSpec(memory_space=pltpu.VMEM)
    inputs = (sig, o["oDA"], o["oOUT"], rr, o["oDP"], o["oST"])
    big = [sd((rows, T, CH), F32), sd((rows, S, CH), BF), sd(rr.shape, F32), sd((3 * HH, C), F32), sd((HC, CH), F32)]
    return pl.pallas_call(
        functools.partial(last_body, (CH, total_in)),
        out_shape=big + [sd((CH,), F32)] * 4 + [sd((HH,), F32)] * 2,
        in_specs=[anyspec] * len(inputs),
        out_specs=[anyspec] * len(big) + [vmem] * 6,
        scratch_shapes=[V(x.shape, x.dtype) for x in inputs]
        + [V(x.shape, x.dtype) for x in big]
        + [V((CH // 128 * 64 * ROWS, 128), F32), pltpu.SemaphoreType.DMA((rr.shape[0] + 8,)), pltpu.SemaphoreType.DMA((rr.shape[0] + T // 32 + 4,))],
        compiler_params=pltpu.CompilerParams(vmem_limit_bytes=VMEM_BYTES),
        name="last_pass",
    )(*inputs)


def on_device(axes, signal, seg, cotangent, conv_wide, taps, pointwise, *vectors):
    CH = signal.shape[2]
    o = call_main(
        axes, signal.reshape(-1, CH), seg, cotangent.reshape(-1, CH), conv_wide, jnp.swapaxes(taps, 1, 2), pointwise, vectors
    )
    gs, out, gw, dk, pw, *small = call_last(axes, signal, o)
    K, C, HH = taps.shape
    return (out, gs, gw.reshape(conv_wide.shape), jnp.swapaxes(dk.reshape(K, HH, C), 1, 2), pw, *small)


def solution(mesh):
    axes = (mesh.shape["bins"], mesh.shape["mp"], mesh.shape["batch"])
    cut = P("batch", "bins", "mp")
    tap = P(None, None, "mp")
    return jax.shard_map(
        functools.partial(on_device, axes),
        mesh=mesh,
        in_specs=(cut, P("batch", None), cut, tap, tap, P(None, "mp")) + (P("mp"),) * 6,
        out_specs=(cut, cut, tap, tap, P(None, "mp")) + (P("mp"),) * 6,
        check_vma=False,
    )
```

```python
import functools
import types

import jax
import jax.numpy as jnp
from jax import lax
from jax.experimental import pallas as pl
from jax.experimental.pallas import tpu as pltpu
from jax.sharding import PartitionSpec as P

DIL = 57
EPSILON = 1e-05
TAPS = 5
BF = jnp.bfloat16
F32 = jnp.float32
MESH = pl.DeviceIdType.MESH
K0 = 0.7978845608028654
K3 = 0.044715
ROWS = 8
VMEM_BYTES = 63 * 2**20


def gelu_up(x):
    t = jnp.tanh(x * (K0 + (K0 * K3) * (x * x)))
    h = 0.5 * x
    return h + h * t


def gelu_both(x):
    x2 = x * x
    t = jnp.tanh(x * (K0 + (K0 * K3) * x2))
    h = 0.5 * x
    return h + h * t, 0.5 + 0.5 * t + h * (1.0 - t * t) * (K0 + (3.0 * K0 * K3) * x2)


def dot(a, b, ca, cb):
    return lax.dot_general(a, b, (((ca,), (cb,)), ((), ())), preferred_element_type=F32)


def wide(mask, times):
    return jnp.concatenate([mask] * times, axis=1)


def al(x, n):
    return pl.multiple_of(x, n)


class Place:
    def __init__(self, nb, nm, na):
        self.nb, self.nm, self.na = nb, nm, na
        self.b = lax.axis_index("bins")
        self.m = lax.axis_index("mp")
        self.a = lax.axis_index("batch")
        self.layer = nm * na
        self.q = self.m * na + self.a

    def in_layer(self, q):
        return (self.b, q // self.na, lax.rem(q, self.na))

    def in_bins(self, b):
        return (b, self.m, self.a)

    @property
    def partner(self):
        return (self.b, 1 - self.m, self.a)

    def others(self, me, n):
        return [lax.rem(me + i, n) for i in range(1, n)]


def remote(src, dst, ss, rs, dev):
    return pltpu.make_async_remote_copy(
        src_ref=src, dst_ref=dst, send_sem=ss, recv_sem=rs, device_id=dev, device_id_type=MESH
    )


class Exchange:
    def __init__(self, buf, me, n, dev_of, ss, rs, others):
        self.buf, self.me, self.n, self.dev_of, self.ss, self.rs, self.others = (
            buf, me, n, dev_of, ss, rs, others,
        )

    def start(self, value):
        self.buf[self.me] = value
        own = self.buf.at[self.me]
        for q in self.others:
            remote(own, own, self.ss, self.rs, self.dev_of(q)).start()

    def all_others(self):
        ref = self.buf.at[pl.ds(0, self.n - 1)]
        return remote(ref, ref, self.ss, self.rs, self.dev_of(self.others[0]))

    def wait(self):
        self.all_others().wait_recv()
        return [self.buf[i] for i in range(self.n)]

    def drain(self):
        self.all_others().wait_send()


def merged(parts, count):
    means = [p[0:1] for p in parts]
    total = functools.reduce(jnp.add, means)
    mean = total / len(parts)
    squares = functools.reduce(jnp.add, [p[1:2] for p in parts])
    apart = functools.reduce(jnp.add, [(x - mean) * (x - mean) for x in means])
    return mean, squares + count * apart


def row_sum(x):
    return jnp.sum(x, axis=0, keepdims=True)


def greet(devices):
    barrier = pltpu.get_barrier_semaphore()
    for d in devices:
        pl.semaphore_signal(barrier, inc=1, device_id=d, device_id_type=MESH)
    pl.semaphore_wait(barrier, len(devices))


PLAN = (
    ("bh", [18]),
    ("center", [18]),
    ("center2", [19]),
    ("rims", [18]),
    ("bm", [19, 15, 16, 17]),
    ("bm2", [18]),
    ("tap0", [19, 15, 16, 17]),
    ("tap1", [18, 0, 2]),
    ("tap2", [1, 15, 16]),
    ("tap3", [17, 4]),
    ("tap4", [3, 5]),
    ("tap5", [18, 1, 6, 8]),
    ("tap6", [19, 0, 15, 7]),
    ("tap7", [16, 2, 3, 17, 10]),
    ("tap8", [4, 5, 1, 9, 11, 0]),
    ("tap9", [15, 6, 12, 14, 7]),
    ("taps", [16, 2, 13, 17]),
    ("tile0", [8, 4, 1, 19]),
    ("tile1", [0, 9, 3]),
    ("tile2", [2, 11]),
    ("tile3", [10]),
    ("tile4", [6, 5, 4, 16, 15, 1]),
    ("tile5", []),
    ("tile6", [0, 13, 12, 3, 8]),
    ("tile7", [2, 14]),
    ("tile8", [7, 6, 19, 17, 5]),
    ("tile9", [10, 9, 4]),
    ("tile10", [11, 3, 15, 8]),
    ("tile11", [0]),
    ("tile12", [16, 7, 12, 1, 6, 2, 13]),
    ("tile13", [5, 14]),
    ("tile14", [3, 10, 9]),
    ("tile15", [17, 0]),
    ("end0", [11, 4, 8, 2, 7, 1, 5, 12, 6, 13, 4, 14]),
    ("end1", [3, 7, 10, 8, 9, 6, 11, 5, 12, 13, 7, 8, 14, 10, 9, 12, 11, 13, 14, 10, 9, 12, 11, 14, 13]),
)


def main_body(dims, names, spans, *refs):
    nb, nm, na, T, S, CH, HC = dims
    C = 2 * CH
    HR = T * ROWS
    PR = S * ROWS
    rim = (DIL + 1) * ROWS
    r = types.SimpleNamespace(**dict(zip(names, refs, strict=True)))
    place = Place(nb, nm, na)
    b, m, a = place.b, place.m, place.a
    other = 1 - m
    total_in = float(HR * nb * nm * na)
    total_mid = float(PR * nb * nm * na)
    LANES = r.LANES
    RT = LANES.shape[0] // (C // 128)
    early = nb == 4

    def part(name, at=0, n=None):
        pool, start, rows = spans[name]
        return getattr(r, pool).at[pl.ds(start + at, rows if n is None else n)]

    def local(src, dst, i):
        return pltpu.make_async_copy(src, dst, r.lsem.at[i])

    def cross(src, dst, i):
        return remote(src, dst, r.csem_s.at[i], r.csem_r.at[i], place.partner)

    RAW, STO, X, CT, HM = part("RAW"), part("STO"), part("X"), part("CT"), part("HM")
    H0, H1, W, PW, DT = part("H0"), part("H1"), part("W"), part("PW"), part("DT")
    COT = [part("COTR", 0, PR), part("COTR", PR, PR)]
    vectors = [r.v0, r.v1, r.v2, r.v3, r.v4, r.v5]
    PAR, SEG, SEGX, MASK, ST = r.PAR, r.SEG, r.SEGX, r.MASK, r.ST
    half = lambda at, n: pl.ds(al(at + m * n, n), n)

    sig, cot = r.sig, r.cot
    mine, theirs = pl.ds(al(m * HR, HR), HR), pl.ds(al(other * HR, HR), HR)
    raw_mine = r.N.at[pl.ds(al(spans["RAW"][1] + m * HR, 16), HR)]
    cot_mine = r.N.at[pl.ds(al(spans["COTR"][1] + m * PR, 16), PR)]
    lanes = pl.ds(al(m * CH, CH), CH)
    w0, pw0, dt0 = spans["W"][1], spans["PW"][1], spans["DT"][1]
    HH = HC // 2

    def weight(k):
        return r.M.at[pl.ds(w0 + k * C, C), lanes]

    def tap_rows(k):
        return r.M.at[pl.ds(al(dt0 + k * HC + m * HH, 16), HH)]

    pw_mine = r.M.at[pl.ds(pw0, HC), lanes]
    ld_sto = local(sig.at[theirs], STO, 0)
    ld_raw = local(sig.at[mine], raw_mine, 1)
    ld_seg = local(r.seg, SEG, 2)
    ld_w = [local(r.wide.at[k], weight(k), 3 + k) for k in range(TAPS)]
    ld_d = [local(r.taps.at[k], tap_rows(k), 8 + k) for k in range(3)]
    ld_pw = local(r.pw, pw_mine, 11)
    ld_cot = local(cot.at[pl.ds(al(m * PR, PR), PR)], cot_mine, 12)
    for c in [ld_sto, ld_raw, ld_seg, *ld_w, *ld_d, ld_pw, ld_cot]:
        c.start()
    for i in range(4):
        PAR[m, i : i + 1, :] = vectors[i][...].reshape(1, CH)
    for i in range(4, 6):
        PAR[m, i : i + 1, 0:HH] = vectors[i][...].reshape(1, HH)
    if early:
        chips, chip = nb * na, b * na + a
        first = (m, nm, lambda q: (b, q, a))
        second = (chip, chips, lambda q: (q // na, m, lax.rem(q, na)))
    else:
        first = (place.q, place.layer, place.in_layer)
        second = (b, nb, place.in_bins)
    greet([g[2](q) for g in (first, second) for q in place.others(*g[:2])])
    x_sig = cross(sig.at[theirs], raw_mine, 0)
    x_par = cross(PAR.at[m], PAR.at[m], 1)
    x_w = [cross(r.wide.at[k], weight(k), 2 + k) for k in range(TAPS)]
    x_d = [cross(r.taps.at[k], tap_rows(k), 7 + k) for k in range(3)]
    x_pw = cross(r.pw, pw_mine, 10)
    x_cot = cross(cot.at[pl.ds(al(other * PR, PR), PR)], cot_mine, 11)
    crosses = [x_sig, x_par, *x_w, x_cot, x_pw, *x_d]
    for c in crosses:
        c.start()

    def exchange(i, name):
        one, two = (second, first) if early and i == 0 else (first, second)
        return (
            Exchange(getattr(r, name + "A"), *one, r.as_.at[i], r.ar_.at[i], place.others(*one[:2])),
            Exchange(getattr(r, name + "B"), *two, r.bs_.at[i], r.br_.at[i], place.others(*two[:2])),
        )

    def begin_stats(ex, mean, squares, count):
        ex[0].start(jnp.concatenate([mean, squares], axis=0))
        ex[1].start(jnp.concatenate(merged(ex[0].wait(), count), axis=0))

    def finish_stats(ex, count):
        return merged(ex[1].wait(), count * first[1])

    def begin_sums(ex, one, two):
        ex[0].start(jnp.concatenate([one, two], axis=0))
        ex[1].start(functools.reduce(jnp.add, ex[0].wait()))

    def finish_sums(ex):
        return functools.reduce(jnp.add, ex[1].wait())

    ex_in, ex_mid, ex_hid, ex_bh, ex_bm, ex_bi = exchanges = [
        exchange(i, n) for i, n in enumerate(["XI", "XM", "XH", "XG", "XD", "XS"])
    ]

    ps, pr, zr = r.ps, r.pr, r.zr
    N = r.N
    INNER = 4
    outer = nb // INNER
    inner = lax.rem(b, INNER)
    base = b - inner
    bits = (lax.rem(a, 2), a // 2)
    flip = ((b, m, a + 1 - 2 * bits[0]), (b, m, lax.rem(a + 2, 4)))
    PSLOTS = spans["PS"][2] // C

    class Piece:
        def __init__(self, p, stack, lanes, first, n, R, F, full=False):
            self.p = p
            self.stack = stack
            self.lanes = pl.ds(*lanes)
            self.first = first
            self.n = n
            HALF, QUART = n // 2, n // 4
            self.SMALL = n // 16
            self.full = full
            self.steps = [0, 1, 2, 3, 5, 6] if full else [0, 1, 2, 3, 4, 5, 6]
            b1, b2 = bits[self.first], bits[1 - self.first]
            self.n1, self.n2 = flip[self.first], flip[1 - self.first]
            self.k1 = b1 * HALF
            self.s1 = (1 - b1) * HALF
            self.k2 = b1 * HALF + b2 * QUART
            self.s2 = b1 * HALF + (1 - b2) * QUART
            self.HALF, self.QUART = HALF, QUART
            self.R, self.F = R, F
            self.XB, self.YB, self.ZB = [spans[f"{x}{stack}"][1] for x in ("XB", "YB", "ZB")]

        def rows(self, start, at, n):
            return N.at[pl.ds(al(start + at, 16), n), self.lanes]

        def get(self, start, at, n):
            return N[pl.ds(al(start + at, 16), n), self.lanes].astype(F32)

        def put(self, start, at, n, v):
            N[pl.ds(al(start + at, 16), n), self.lanes] = v.astype(BF)

        def describe(self, make, i, dev):
            return lambda: remote(*make(), ps.at[self.p], pr.at[self.p, i - 2], dev)

        def moves(self):
            F, R = self.F, self.R
            return {
                2: self.describe(lambda: (self.rows(R, self.s1, self.HALF), self.rows(self.XB, 0, self.HALF)), 2, self.n1),
                3: self.describe(lambda: (self.rows(R, self.s2, self.QUART), self.rows(self.YB, 0, self.QUART)), 3, self.n2),
                4: self.describe(lambda: (self.rows(F, self.k2, self.QUART),) * 2, 4, self.n2),
                5: self.describe(lambda: (self.rows(F, self.k1, self.HALF),) * 2, 5, self.n1),
            }

        def toward(self, which, i):
            j = lax.rem(inner + i, INNER)
            if self.full:
                src, dst = self.rows(self.R, self.k2, self.QUART), self.rows(self.ZB, inner * self.QUART, self.QUART)
            elif which == 0:
                src, dst = self.rows(self.R, self.k2 + j * self.SMALL, self.SMALL), self.rows(self.ZB, inner * self.SMALL, self.SMALL)
            else:
                src = dst = self.rows(self.F, self.k2 + inner * self.SMALL, self.SMALL)
            return remote(src, dst, ps.at[self.p], zr.at[self.p, which], (base + j, m, a))

        def gather(self, which):
            n = (INNER - 1) * (self.QUART if self.full else self.SMALL)
            ref = self.rows(self.ZB, 0, n) if which == 0 else self.rows(self.F, self.k2, n)
            remote(ref, ref, ps.at[self.p], zr.at[self.p, which], (base + lax.rem(inner + 1, INNER), m, a)).wait_recv()

        def drain(self):
            n = self.n + self.n // 2 + (INNER - 1) * (self.QUART if self.full else 2 * self.SMALL)
            ref = N.at[pl.ds(0, n), self.lanes]
            remote(ref, ref, ps.at[self.p], pr.at[self.p, 0], self.n1).wait_send()
            if outer > 1:
                for i in range(1, outer):
                    self.outward(i).wait_send()
            self.out().wait()

        def outward(self, i):
            mine = b // INNER
            q = lax.rem(mine + i, outer)
            ref = r.F.at[self.slot(mine), self.lanes]
            return remote(ref, ref, r.os_.at[self.p, q], r.or_.at[self.p, mine], (q * INNER + inner, m, a))

        def slot(self, q):
            return pl.ds(al(spans[f"OB{self.stack}"][1] + q * self.SMALL, 8), self.SMALL)

        def out(self):
            k = self.stack
            to = r.oR.at[ORDER[k], :, self.lanes] if k < TAPS else r.oDP.at[pl.ds(self.F - dp_at, self.n), self.lanes]
            return local(self.rows(self.F, 0, self.n), to, 15 + self.p)

        def step(self, ph):
            p, moves = self.p, self.moves()
            HALF, QUART, SMALL = self.HALF, self.QUART, self.SMALL
            if ph == 0:
                moves[2]().start()
            elif ph == 1:
                moves[2]().wait_recv()
                self.put(self.R, self.k1, HALF, self.get(self.R, self.k1, HALF) + self.get(self.XB, 0, HALF))
                moves[3]().start()
            elif ph == 2:
                moves[3]().wait_recv()
                self.put(self.R, self.k2, QUART, self.get(self.R, self.k2, QUART) + self.get(self.YB, 0, QUART))
                for i in range(1, INNER):
                    self.toward(0, i).start()
            elif ph == 3:
                self.gather(0)
                n = QUART if self.full else SMALL
                at = self.k2 if self.full else self.k2 + inner * SMALL
                v = self.get(self.R, at, n)
                for i in range(1, INNER):
                    v += self.get(self.ZB, lax.rem(inner + i, INNER) * n, n)
                if outer > 1:
                    mine = b // INNER
                    r.F[self.slot(mine), self.lanes] = v
                    for i in range(1, outer):
                        self.outward(i).start()
                    for i in range(1, outer):
                        q = lax.rem(mine + i, outer)
                        ref = r.F.at[self.slot(q), self.lanes]
                        remote(ref, ref, r.os_.at[p, q], r.or_.at[p, q], (q * INNER + inner, m, a)).wait_recv()
                    v = r.F[self.slot(0), self.lanes]
                    for j in range(1, outer):
                        v += r.F[self.slot(j), self.lanes]
                self.put(self.F, at, n, v)
                if self.full:
                    moves[4]().start()
                else:
                    for i in range(1, INNER):
                        self.toward(1, i).start()
            elif ph == 4:
                self.gather(1)
                moves[4]().start()
            elif ph == 5:
                moves[4]().wait_recv()
                moves[5]().start()
            elif ph == 6:
                moves[5]().wait_recv()
                self.out().start()

    ORDER = (2, 1, 3, 0, 4)
    r_at, dp_at = spans["R"][1], spans["FD"][1]
    dps_at, dpr_at = spans["DPS"][1], r_at + TAPS * C
    thirds = [(q * CH // 3, CH // 3) for q in range(3)]
    pieces = []
    for k in range(TAPS + 1):
        for q in range(3):
            R, F = r_at + k * C, spans[f"F{k}"][1] if k < TAPS else dp_at
            pieces.append(Piece(len(pieces), k, thirds[q], (k + q) % 2, C, R, F))
    late = len(pieces)
    if early:
        pieces.append(Piece(late, 6, (0, CH), 0, CH, r_at + 6 * C, dp_at + C, True))
        pieces.append(Piece(late + 1, 7, (0, CH), 1, CH, r_at + 6 * C + CH, dp_at + C + CH, True))
    else:
        pieces.append(Piece(late, 6, (0, CH), 0, C, r_at + 6 * C, dp_at + C))

    class Share:
        def __init__(self, sem, src, dst, own, to, n):
            self.sem, self.src, self.dst, self.own, self.to, self.n = sem, src, dst, own, to, n

        def copy(self):
            at = lambda start: N.at[pl.ds(al(start, 16), self.n)]
            return remote(at(self.src), at(self.dst), r.shs.at[self.sem], r.shr.at[self.sem], place.partner)

        def sum(self):
            self.copy().wait_recv()
            v = self.own() + N[pl.ds(al(self.dst, 16), self.n), :].astype(F32)
            N[pl.ds(al(self.to, 16), self.n), :] = v.astype(BF)

    def dil_share(sem, at, n):
        own = lambda: N[pl.ds(dpr_at + at, n), :].astype(F32)
        return Share(sem, dps_at + at, dp_at + at, own, dpr_at + at, n)

    share_rest, share_pw, share_mid = dil_share(10, 0, C), dil_share(11, C, CH), dil_share(12, C + CH, CH)

    left = [list(pc.steps) for pc in pieces]
    plan = {}
    for name, which in PLAN:
        if not early:
            which = [p for p in which if p < len(pieces) and not (p == late and name in ("bh", "center", "center2"))]
        plan[name] = [(p, left[p].pop(0)) for p in which if left[p]]
    while any(left):
        most = max(len(x) for x in left)
        plan["end1"] += [(p, x.pop(0)) for p, x in enumerate(left) if len(x) == most]

    def pump(where):
        for p, ph in plan[where]:
            pieces[p].step(ph)

    ld_sto.wait()
    ld_raw.wait()
    CHK = 128
    raw_at = spans["RAW"][1] + m * HR

    def own_raw(i):
        return r.N[pl.ds(al(raw_at + i * CHK, 16), CHK), :].astype(F32).reshape(CHK // 8, 8, CH)

    def sto(i):
        return STO[pl.ds(al(i * CHK, CHK), CHK), :].astype(F32).reshape(CHK // 8, 8, CH)

    def s1(i, acc):
        return acc + jnp.sum(own_raw(i), axis=0) + jnp.sum(sto(i), axis=0)

    acc = lax.fori_loop(0, HR // CHK, s1, jnp.zeros((8, CH), F32))
    mean = row_sum(acc) / float(2 * HR)

    def s2(i, acc):
        u = own_raw(i) - mean
        v = sto(i) - mean
        return acc + jnp.sum(u * u, axis=0) + jnp.sum(v * v, axis=0)

    acc = lax.fori_loop(0, HR // CHK, s2, jnp.zeros((8, CH), F32))
    ex_in[0].start(jnp.concatenate([mean, row_sum(acc)], axis=0))

    ld_seg.wait()
    blocks = SEG.shape[1] // 128

    def make_segs(i, _):
        at = b * (T // 128) - 1 + i
        v = SEG[pl.ds(al(m * ROWS, ROWS), ROWS), pl.ds(al(jnp.clip(at, 0, blocks - 1) * 128, 128), 128)].astype(F32)
        v = jnp.where(jnp.logical_and(at >= 0, at < blocks), v, -1.0)
        for j in range(128):
            SEGX[pl.ds(al(i * 1024 + j * 8, 8), 8), :] = jnp.broadcast_to(v[:, j : j + 1], (8, 128))
        return 0

    lax.fori_loop(0, T // 128 + 2, make_segs, 0)
    BIN0 = 128 * 8

    def make_masks(i, _):
        mid = SEGX[pl.ds(al(i * 128 + BIN0, 128), 128), :]
        for j, o in enumerate((-2, -1, 1, 2)):
            off = SEGX[pl.ds(al(i * 128 + BIN0 + o * 8, 8), 128), :]
            MASK[j, pl.ds(al(i * 128, 128), 128), :] = jnp.where(off == mid, 1.0, 0.0).astype(BF)
        return 0

    lax.fori_loop(0, HR // 128, make_masks, 0)
    x_sig.wait_recv()
    BB = RT // ROWS

    def turn(src, dst, i):
        for h in range(2):
            for row in range(ROWS):
                v = src(h, row).astype(F32)
                for j in range(CH // 128):
                    LANES[pl.ds((h * (CH // 128) + j) * RT + row, BB, stride=ROWS), :] = v[:, j * 128 : (j + 1) * 128]
        for j in range(C // 128):
            dst[pl.ds(al(i * RT, RT), RT), j * 128 : (j + 1) * 128] = LANES[j * RT : (j + 1) * RT, :].astype(BF)

    def turn_x(i, _):
        turn(lambda h, row: RAW[pl.ds(al(h * HR + row * T + i * BB, BB), BB), :], X, i)
        return 0

    lax.fori_loop(0, T // BB, turn_x, 0)
    keep_x = local(X, r.oX, 13)
    keep_x.start()
    x_par.wait_recv()

    def vec(i):
        return jnp.concatenate([PAR[0, i : i + 1, :], PAR[1, i : i + 1, :]], axis=1)

    def hvec(i):
        return jnp.concatenate([PAR[0, i : i + 1, 0:HH], PAR[1, i : i + 1, 0:HH]], axis=1)

    la = ex_in[0].wait()
    n_own = float(2 * HR)
    both = lambda x, y: jnp.concatenate([jnp.concatenate([x[i], y[i]], axis=1) for i in range(2)], axis=0)
    if early:
        ex_in[1].start(jnp.concatenate(merged(la, n_own), axis=0))
        lb = ex_in[1].wait()
        v = both((lb[0][0:1], lb[0][1:2]), (lb[1][0:1], lb[1][1:2]))
        mu_in, sq = v[0:1], v[1:2]
    else:
        ex_in[1].start(both(merged(la[0:na], n_own), merged(la[na : 2 * na], n_own)))
        mu_in, sq = merged(ex_in[1].wait(), n_own * na)
    inv_in = lax.rsqrt(sq / total_in + EPSILON)
    gain_in, shift_in = vec(0), vec(1)
    scale_in = gain_in * inv_in
    ST[0:1, :] = mu_in
    ST[1:2, :] = inv_in
    ST[2:3, :] = gain_in
    HB = 256

    def make_hidden(i, last):
        at = al(i * HB, HB)
        pre = (X[pl.ds(at, HB), :].astype(F32) - mu_in) * scale_in + shift_in
        h = gelu_up(pre)
        H0[pl.ds(al(at + 16, 16), HB), :] = h.astype(BF)
        H1[pl.ds(at, HB), :] = jnp.concatenate([last, h[: HB - 8]], axis=0).astype(BF)
        return h[HB - 8 :]

    lax.fori_loop(0, HR // HB, make_hidden, jnp.zeros((8, C), F32))
    hs, hr = r.hs, r.hr
    down = (jnp.maximum(b - 1, 0), m, a)
    up = (jnp.minimum(b + 1, nb - 1), m, a)
    has_down, has_up = b > 0, b < nb - 1

    def when_down(f):
        pl.when(has_down)(f)

    def when_up(f):
        pl.when(has_up)(f)

    class Rims:
        def __init__(self, to_down, from_up, to_up, from_down, i):
            self.down = remote(to_down, from_up, hs.at[i], hr.at[i], down)
            self.up = remote(to_up, from_down, hs.at[i + 1], hr.at[i + 1], up)

        def start_down(self):
            when_down(self.down.start)

        def start_up(self):
            when_up(self.up.start)

        def wait_from_up(self):
            when_up(self.down.wait_recv)

        def wait_from_down(self):
            when_down(self.up.wait_recv)

        def drain(self):
            when_down(self.down.wait_send)
            when_up(self.up.wait_send)

    def clear_halo(ref):
        @pl.when(jnp.logical_not(has_down))
        def _():
            ref[0:16, :] = jnp.zeros((16, C), BF)

        @pl.when(jnp.logical_not(has_up))
        def _():
            ref[pl.ds(HR + 16, 16), :] = jnp.zeros((16, C), BF)

    def halos(ref, i):
        return Rims(ref.at[pl.ds(16, 16)], ref.at[pl.ds(HR + 16, 16)], ref.at[pl.ds(HR, 16)], ref.at[pl.ds(0, 16)], i)

    h_halo = halos(H0, 0)
    h_halo.start_down()
    h_halo.start_up()
    clear_halo(H0)

    def by_one_bin(even, odd):
        v = even[0:32, :].astype(F32)
        odd[0:16, :] = v[8:24].astype(BF)
        v = even[pl.ds(HR, 32), :].astype(F32)
        odd[pl.ds(HR, 16), :] = v[8:24].astype(BF)

    MJ = {-2: 0, -1: 1, 1: 2, 2: 3}

    def shifted(even, odd, o, at, n):
        if o % 2 == 0:
            v = even[pl.ds(al(at + (o + 2) * 8, 16), n), :]
        else:
            v = odd[pl.ds(al(at + (o + 1) * 8, 16), n), :]
        if o != 0:
            v = v * wide(MASK[MJ[o], pl.ds(al(at, 16), n), :], C // 128)
        return v

    def w(k):
        return W[k * C : (k + 1) * C, :]

    def put_lanes(v, n):
        for j in range(C // 128):
            LANES[j * RT : j * RT + n, :] = v[:, j * 128 : (j + 1) * 128]

    def get_lanes(at, n):
        return jnp.concatenate([LANES[pl.ds(al(j * RT + at, 8), n), :] for j in range(C // 128)], axis=1)

    for c in (*ld_w,):
        c.wait()
    for c in x_w:
        c.wait_recv()
    POOL, DIFF, SUM = r.POOL, r.DIFF, r.SUM
    SUM[...] = jnp.zeros_like(SUM)

    def conv_tile(i):
        at = al(i * RT, RT)
        acc = None
        for k in range(TAPS):
            d = dot(shifted(H0, H1, k - 2, at, RT), w(k), 1, 0)
            acc = d if acc is None else acc + d
        put_lanes(acc, RT)

        def pool(j, s):
            v = get_lanes(j * 128, 128).reshape(8, 2, 8, C)
            c0, c1 = v[:, 0], v[:, 1]
            d = c0 - c1
            p = jnp.maximum(c0, c1) + jnp.log(1.0 + jnp.exp(-jnp.abs(d)))
            to = pl.ds(al(i * (RT // 2) + j * 64, 64), 64)
            POOL[to, :] = p.reshape(64, C)
            DIFF[to, :] = d.reshape(64, C)
            return s + jnp.sum(p, axis=0)

        SUM[...] += lax.fori_loop(0, RT // 128, pool, jnp.zeros((8, C), F32))

    NT = HR // RT

    def conv_loop(i, _):
        conv_tile(i)
        return 0

    lax.fori_loop(1, NT - 1, conv_loop, 0)
    h_halo.wait_from_up()
    h_halo.wait_from_down()
    by_one_bin(H0, H1)
    lax.fori_loop(0, 2, lambda i, _: (conv_tile(i * (NT - 1)), 0)[1], 0)

    mean = row_sum(SUM[...]) / float(PR)

    def m2_mid(i, acc):
        v = POOL[pl.ds(al(i * 128, 128), 128), :].reshape(16, 8, C) - mean
        return acc + jnp.sum(v * v, axis=0)

    acc = lax.fori_loop(0, PR // 128, m2_mid, jnp.zeros((8, C), F32))
    begin_stats(ex_mid, mean, row_sum(acc), float(PR))

    ld_cot.wait()
    x_cot.wait_recv()

    def turn_ct(i, _):
        turn(lambda h, row: COT[h][pl.ds(al(row * S + i * BB, BB), BB), :], CT, i)
        return 0

    lax.fori_loop(0, S // BB, turn_ct, 0)
    ld_pw.wait()
    x_pw.wait_recv()
    GT, DO, E0 = part("GT"), part("DO"), part("E0")
    E1, GML = part("GM"), [part("GM", 0, PR), part("GM", PR, PR)]

    def make_gt(i, _):
        at = pl.ds(al(i * 256, 256), 256)
        GT[at, :] = dot(CT[at, :], PW[...], 1, 1)
        return 0

    lax.fori_loop(0, PR // 256, make_gt, 0)
    for c in ld_d:
        c.wait()
    for c in x_d:
        c.wait_recv()

    def dt(k):
        return DT[k * HC : (k + 1) * HC, :]

    mu_mid, sq = finish_stats(ex_mid, float(PR))
    inv_mid = lax.rsqrt(sq / total_mid + EPSILON)
    gain_mid, shift_mid = vec(2), vec(3)
    scale_mid = gain_mid * inv_mid

    def make_mid(i, _):
        at = pl.ds(al(i * 128, 128), 128)
        HM[at, :] = gelu_up((POOL[at, :] - mu_mid) * scale_mid + shift_mid).astype(BF)
        return 0

    lax.fori_loop(0, PR // 128, make_mid, 0)

    packed = early
    WIN = 32 * ROWS
    nrim = WIN if packed else rim
    RS = [part("RS", 0, nrim), part("RS", rim, nrim)]
    RR = [part("RR", 0, nrim), part("RR", rim, nrim)]

    def ended(s):
        before = SEGX[pl.ds(al(BIN0 + (s - 33) * 16, 8), 8), :]
        after = SEGX[pl.ds(al(BIN0 + s * 16, 8), 8), :]
        return wide(jnp.where(before != after, 1.0, 0.0), HC // 128).reshape(1, ROWS, HC)

    ended_up, ended_down = ended(S), ended(0)

    def choose(flag, x, y):
        three = (WIN // ROWS, ROWS, HC)
        return jnp.where(flag > 0.5, x.reshape(three), y.reshape(three)).reshape(WIN, HC)

    def pack_up(start):
        at = lambda s: r.F[pl.ds(start + s * ROWS, WIN), :]
        return choose(ended_up, at(S - 32), at(S - DIL)).astype(BF)

    def pack_down(start):
        at = lambda s: r.F[pl.ds(start + s * ROWS, WIN), :]
        return choose(ended_down, at(DIL - 32), at(0)).astype(BF)

    def unpack(flag, ref, v, first):
        ref[...] = jnp.zeros((rim, HC), F32)
        a, c = first * ROWS, (first + DIL - 32) * ROWS
        ref[a : a + WIN, :] = choose(flag, jnp.zeros((WIN, HC), F32), v)
        ref[c : c + WIN, :] = choose(flag, v, ref[c : c + WIN, :])

    p_rims = Rims(RS[1], RR[1], RS[0], RR[0], 2)
    QR = PR // 2
    e0_at, e1_at, do_at, hm_at = spans["E0"][1], spans["GM"][1], spans["DO"][1], spans["HM"][1]

    def pick(i, table):
        v = jnp.int32(table[-1])
        for n in range(len(table) - 2, -1, -1):
            v = jnp.where(i == n, table[n], v)
        return v

    halves_of = (1, 0, 0, 1, 0, 1)
    taps_of = (0, 2, 0, 2, 1, 1)
    starts = [{0: e0_at + rim, 1: do_at, 2: e1_at}[k] + q * QR for k, q in zip(taps_of, halves_of)]

    def product(i, _):
        v = dot(
            r.M[pl.ds(al(hm_at + pick(i, halves_of) * QR, 16), QR), :],
            r.M[pl.ds(al(dt0 + pick(i, taps_of) * HC, 16), HC), :],
            1, 1,
        )
        r.F[pl.ds(al(pick(i, starts), 8), QR), :] = v

        @pl.when(i == 0)
        def _():
            RS[0][...] = pack_up(e0_at + rim) if packed else E0[PR : PR + rim, :].astype(BF)
            p_rims.start_up()

        @pl.when(i == 1)
        def _():
            RS[1][...] = pack_down(e1_at) if packed else E1[0:rim, :].astype(BF)
            p_rims.start_down()

        return 0

    lax.fori_loop(0, len(halves_of), product, 0)

    def take_rims(rims, low, high):
        rims.wait_from_down()
        rims.wait_from_up()

        @pl.when(has_down)
        def _():
            v = RR[0][...].astype(F32)
            if packed:
                unpack(ended_down, low, v, 1)
            else:
                low[...] = v

        @pl.when(jnp.logical_not(has_down))
        def _():
            low[...] = jnp.zeros((rim, HC), F32)

        @pl.when(has_up)
        def _():
            v = RR[1][...].astype(F32)
            if packed:
                unpack(ended_up, high, v, 0)
            else:
                high[...] = v

        @pl.when(jnp.logical_not(has_up))
        def _():
            high[...] = jnp.zeros((rim, HC), F32)

    take_rims(p_rims, part("E0", 0, rim), part("GM", PR, rim))

    def same(i, by):
        def pick(off):
            return SEGX[pl.ds(al(i * 256 + BIN0 + off * 16, 16), 256), :].reshape(16, 2, 8, 128)[:, 0]

        return wide(jnp.where(pick(0) == pick(by), 1.0, 0.0).reshape(128, 128), HC // 128)

    def add_dil(i, s):
        at = pl.ds(al(i * 128, 128), 128)
        v = DO[at, :]
        v += same(i, -DIL) * E0[pl.ds(al(i * 128 + 8, 8), 128), :]
        v += same(i, DIL) * E1[pl.ds(al(i * 128 + DIL * 8, 8), 128), :]
        DO[at, :] = v
        return s + jnp.sum(v.reshape(16, 8, HC), axis=0)

    acc = lax.fori_loop(0, PR // 128, add_dil, jnp.zeros((8, HC), F32))
    mean = row_sum(acc) / float(PR)

    def m2_hid(i, acc):
        v = DO[pl.ds(al(i * 128, 128), 128), :].reshape(16, 8, HC) - mean
        return acc + jnp.sum(v * v, axis=0)

    acc = lax.fori_loop(0, PR // 128, m2_hid, jnp.zeros((8, HC), F32))
    begin_stats(ex_hid, mean, row_sum(acc), float(PR))
    SL = [part("RAW", 0, PR), part("RAW", PR, PR)]

    def make_slope(i, _):
        at = pl.ds(al(i * 64, 64), 64)
        _, slope = gelu_both((POOL[at, :] - mu_mid) * scale_mid + shift_mid)
        SL[0][at, :] = slope[:, :CH].astype(BF)
        SL[1][at, :] = slope[:, CH:].astype(BF)
        return 0

    lax.fori_loop(0, PR // 64, make_slope, 0)


    def pool_weights(i, _):
        at = pl.ds(al(i * 64, 64), 64)
        DIFF[at, :] = 0.5 + 0.5 * jnp.tanh(0.5 * DIFF[at, :])
        return 0

    lax.fori_loop(0, PR // 64, pool_weights, 0)
    mu_hid, sq = finish_stats(ex_hid, float(PR))
    inv_hid = lax.rsqrt(sq / total_mid + EPSILON)
    gain_hid, shift_hid = hvec(4), hvec(5)
    HT = part("HT")

    def make_top(i, s):
        at = pl.ds(al(i * 128, 128), 128)
        xhat = (DO[at, :] - mu_hid) * inv_hid
        h, slope = gelu_both(xhat * gain_hid + shift_hid)
        HT[at, :] = h.astype(BF)
        da = slope * GT[at, :]
        GT[at, :] = da
        DO[at, :] = xhat
        return (
            s[0] + jnp.sum((da * xhat).reshape(16, 8, HC), axis=0),
            s[1] + jnp.sum(da.reshape(16, 8, HC), axis=0),
        )

    zero = jnp.zeros((8, HC), F32)
    sg, sb = lax.fori_loop(0, PR // 128, make_top, (zero, zero))
    begin_sums(ex_bh, row_sum(sg), row_sum(sb))

    OB = 256

    def make_out(i, _):
        at = pl.ds(al(i * OB, OB), OB)
        v = (POOL[at, :] + dot(HT[at, :], PW[...], 1, 0)).astype(BF)
        COT[0][at, :] = v[:, :CH]
        COT[1][at, :] = v[:, CH:]
        return 0

    lax.fori_loop(0, PR // OB, make_out, 0)
    cot_other = r.N.at[pl.ds(al(spans["COTR"][1] + other * PR, 16), PR)]
    o_own = local(cot_mine, r.oOUT.at[m], 14)
    o_own.start()
    o_cross = cross(cot_other, r.oOUT.at[m], 12)
    o_cross.start()
    gp = dot(HT[...], CT[...], 0, 0)
    N[dpr_at + C : dpr_at + C + HC, :] = jnp.where(m == 0, gp[:, :CH], gp[:, CH:]).astype(BF)
    N[dps_at + C : dps_at + C + HC, :] = jnp.where(m == 0, gp[:, CH:], gp[:, :CH]).astype(BF)
    share_pw.copy().start()

    share_pw.sum()
    pump("bh")
    v = finish_sums(ex_bh)
    ST[8:10, 0:HC] = v
    ST[8:10, HC:] = jnp.zeros((2, C - HC), F32)
    scale = gain_hid * inv_hid
    mg, mb = v[0:1] / total_mid, v[1:2] / total_mid
    GD = [part("GD", k * PR, PR) for k in range(3)]

    def make_gd(i, _):
        at = pl.ds(al(i * 128, 128), 128)
        g = (scale * (GT[at, :] - mb - DO[at, :] * mg)).astype(BF)
        GD[1][at, :] = g
        E0[pl.ds(al(i * 128 + rim, 16), 128), :] = g.astype(F32)
        return 0

    lax.fori_loop(0, PR // 128, make_gd, 0)
    p_rims.drain()
    if packed:
        RS[0][...] = pack_up(e0_at + rim)
        RS[1][...] = pack_down(e0_at + rim)
        g_rims = Rims(RS[1], RR[1], RS[0], RR[0], 4)
    else:
        g_rims = Rims(part("GD", PR, rim), RR[1], part("GD", 2 * PR - rim, rim), RR[0], 4)
    g_rims.start_up()
    g_rims.start_down()


    def to_gm(i, v, add):
        at = pl.ds(al(i * QR, QR), QR)
        for h in range(2):
            u = v[:, h * CH : (h + 1) * CH]
            GML[h][at, :] = GML[h][at, :] + u if add else u

    def mid_center(i, _):
        to_gm(i, dot(GD[1][pl.ds(al(i * QR, QR), QR), :], dt(1), 1, 0), False)
        return 0

    lax.fori_loop(0, 2, mid_center, 0)
    gd_at = spans["GD"][1]

    def dil_grad(k, to):
        g = dot(N[pl.ds(al(gd_at + k * PR, 16), PR), :], HM[...], 0, 0)
        own = jnp.where(m == 0, g[:HH], g[HH:]).astype(BF)
        for_partner = jnp.where(m == 0, g[HH:], g[:HH]).astype(BF)
        for h in range(2):
            at = to + h * HH
            N[pl.ds(al(dpr_at + at, 16), HH), :] = own[:, h * CH : (h + 1) * CH]
            N[pl.ds(al(dps_at + at, 16), HH), :] = for_partner[:, h * CH : (h + 1) * CH]

    dil_grad(1, C + CH)
    share_mid.copy().start()
    pump("center")
    share_mid.sum()
    pump("center2")
    gd_of = [spans["GD"][1], spans["GD"][1] + 2 * PR]

    def mid_side(by, i):
        g_at = gd_of[0 if by > 0 else 1]

        def body(j, _):
            n = i * (QR // 128) + j
            v = same(n, by) * E0[pl.ds(al(n * 128 + rim + by * 8, 8), 128), :]
            N[pl.ds(al(g_at + n * 128, 16), 128), :] = v.astype(BF)
            return 0

        lax.fori_loop(0, QR // 128, body, 0)
        g = N[pl.ds(al(g_at + i * QR, 16), QR), :]
        to_gm(i, dot(g, dt(0 if by > 0 else 2), 1, 0), True)

    mid_side(DIL, 0)
    mid_side(-DIL, 1)
    take_rims(g_rims, part("E0", 0, rim), part("E0", PR + rim, rim))
    pump("rims")
    mid_side(DIL, 1)
    mid_side(-DIL, 0)

    def gm(at):
        return jnp.concatenate([GML[0][at, :], GML[1][at, :]], axis=1)

    def make_dmid(i, s):
        at = pl.ds(al(i * 64, 64), 64)
        xhat = (POOL[at, :] - mu_mid) * inv_mid
        da = jnp.concatenate([SL[0][at, :], SL[1][at, :]], axis=1).astype(F32) * gm(at)
        GML[0][at, :] = da[:, :CH]
        GML[1][at, :] = da[:, CH:]
        return (
            s[0] + jnp.sum((da * xhat).reshape(8, 8, C), axis=0),
            s[1] + jnp.sum(da.reshape(8, 8, C), axis=0),
        )

    zero = jnp.zeros((8, C), F32)
    sg, sb = lax.fori_loop(0, PR // 64, make_dmid, (zero, zero))
    g_rims.drain()
    o_own.wait()
    o_cross.wait_send()
    keep_x.wait()
    begin_sums(ex_bm, row_sum(sg), row_sum(sb))

    lax.fori_loop(0, 2, lambda i, _: (dil_grad(2 * i, i * CH), 0)[1], 0)
    share_rest.copy().start()
    share_rest.sum()
    pump("bm")
    v = finish_sums(ex_bm)
    ST[6:8, :] = v
    mg, mb = v[0:1] / total_mid, v[1:2] / total_mid
    pump("bm2")
    GC0, GC1 = part("GC0"), H1

    def make_gc(i, last):
        at = pl.ds(al(i * 64, 64), 64)
        xhat = (POOL[at, :] - mu_mid) * inv_mid
        g = CT[at, :].astype(F32) + scale_mid * (gm(at) - mb - xhat * mg)
        g0 = g * DIFF[at, :]
        g1 = g - g0
        v = jnp.stack([g0.reshape(8, 8, C), g1.reshape(8, 8, C)], axis=1).reshape(128, C)
        GC0[pl.ds(al(i * 128 + 16, 16), 128), :] = v.astype(BF)
        GC1[pl.ds(al(i * 128, 128), 128), :] = jnp.concatenate([last, v[:120]], axis=0).astype(BF)
        return v[120:]

    lax.fori_loop(0, PR // 64, make_gc, jnp.zeros((8, C), F32))
    g_halo = halos(GC0, 6)
    g_halo.start_down()
    g_halo.start_up()
    clear_halo(GC0)
    XX = part("XX")
    back_x = local(r.oX, XX, 13)

    own_at = spans["GM"][1]
    h0_at = spans["H0"][1] + 16
    ps_at = spans["PS"][1]
    HALF = C // 2
    first_half = (1 - bits[0]) * HALF

    def tap_share(i, j):
        at = first_half if j == 0 else HALF - first_half
        own = lambda: r.F[pl.ds(al(own_at + i % 2 * PR + at, 8), HALF), :]
        return Share(2 * i + j, ps_at + i % PSLOTS * C + at, spans[f"F{i}"][1] + at, own, r_at + i * C + at, HALF)

    shares = [tap_share(i, j) for i in range(TAPS) for j in range(2)]

    def masked(k):
        def body(j, _):
            XX[pl.ds(al(j * 256, 256), 256), :] = shifted(GC0, GC1, 2 - k, j * 256, 256)
            return 0

        lax.fori_loop(0, HR // 256, body, 0)

    def half_tap(it, _):
        i, j = it // 2, lax.rem(it, 2)
        for n in range(TAPS):

            @pl.when(it == 2 * n)
            def _(n=n):
                if n == 1:
                    g_halo.wait_from_up()
                    g_halo.wait_from_down()
                    by_one_bin(GC0, GC1)
                if n >= PSLOTS:
                    for c in shares[2 * (n - PSLOTS) : 2 * (n - PSLOTS) + 2]:
                        c.copy().wait_send()
                masked(ORDER[n])

        odd = lax.rem(i, 2)
        at = jnp.where(j == 0, first_half, HALF - first_half)
        v = dot(r.M[h0_at : h0_at + HR, pl.ds(al(at, 128), HALF)], XX[...], 0, 0)
        r.F[pl.ds(al(own_at + odd * PR + at, 8), HALF), :] = jnp.where(m == 0, v[:, :CH], v[:, CH:])
        N[pl.ds(al(ps_at + lax.rem(i, PSLOTS) * C + at, 16), HALF), :] = jnp.where(m == 0, v[:, CH:], v[:, :CH]).astype(BF)
        for n in range(2 * TAPS):

            @pl.when(it == n)
            def _(n=n):
                shares[n].copy().start()
                if n:
                    shares[n - 1].sum()
                pump(f"tap{n}")

        return 0

    lax.fori_loop(0, 2 * TAPS, half_tap, 0)
    shares[-1].sum()
    pump("taps")

    back_x.start()
    for c in shares[2 * (TAPS - PSLOTS) :]:
        c.copy().wait_send()
    mu, inv, gain, shift = ST[0:1, :], ST[1:2, :], gain_in, shift_in
    RB = 256
    DA = [part("RAW", 0, HR), part("RAW", HR, HR)]

    def tile(i, s):
        at = i * RB
        acc = None
        for k in range(TAPS):
            d = dot(shifted(GC0, GC1, 2 - k, at, RB), w(k), 1, 1)
            acc = d if acc is None else acc + d
        put_lanes(acc, RB)
        for n in range(HR // RB):

            @pl.when(i == n)
            def _(n=n):
                pump(f"tile{2 * n}")
                if n == 0:
                    back_x.wait()


        def back(j, s):
            to = pl.ds(al(at + j * 64, 64), 64)
            xhat = (XX[to, :].astype(F32) - mu) * inv
            _, slope = gelu_both(xhat * gain + shift)
            da = slope * get_lanes(j * 64, 64)
            DA[0][to, :] = da[:, :CH].astype(BF)
            DA[1][to, :] = da[:, CH:].astype(BF)
            return (
                s[0] + jnp.sum((da * xhat).reshape(8, 8, C), axis=0),
                s[1] + jnp.sum(da.reshape(8, 8, C), axis=0),
            )

        s = lax.fori_loop(0, RB // 64, back, s)
        for n in range(HR // RB):

            @pl.when(i == n)
            def _(n=n):
                pump(f"tile{2 * n + 1}")

        return s

    s = lax.fori_loop(0, HR // RB, tile, (zero, zero))
    begin_sums(ex_bi, row_sum(s[0]), row_sum(s[1]))
    d_own = local(raw_mine, r.oDA.at[m], 12)
    d_own.start()
    d_cross = cross(r.N.at[pl.ds(al(spans["RAW"][1] + other * HR, 16), HR)], r.oDA.at[m], 13)
    d_cross.start()
    pump("end0")
    pump("end1")
    ST[4:6, :] = finish_sums(ex_bi)
    ST[3:4, :] = jnp.zeros((1, C), F32)
    ST[10:16, :] = jnp.zeros((6, C), F32)
    o_st = local(ST, r.oST, 14)
    o_st.start()
    for pc in pieces:
        pc.drain()
    for c in (share_rest, share_pw, share_mid):
        c.copy().wait_send()
    d_own.wait()
    o_st.wait()
    d_cross.wait()
    o_cross.wait_recv()
    for c in crosses:
        c.wait_send()
    for e in exchanges:
        e[0].drain()
        e[1].drain()
    h_halo.drain()
    g_halo.drain()


def call_main(axes, sig, seg, cot, wide_taps, taps, pw, vectors):
    nb, nm, na = axes
    CH = sig.shape[1]
    C = 2 * CH
    HC = pw.shape[0]
    assert HC == CH
    HR = sig.shape[0] // 2
    PR = cot.shape[0] // 2
    T, S = HR // ROWS, PR // ROWS
    rim = (DIL + 1) * ROWS
    RT = 512
    NA = nm * na
    early = nb == 4
    NP = 3 * (TAPS + 1) + (2 if early else 1)
    inputs = dict(sig=sig, seg=seg, cot=cot, wide=wide_taps, taps=taps, pw=pw)
    inputs.update({f"v{i}": v for i, v in enumerate(vectors)})
    sd = jax.ShapeDtypeStruct
    outs = dict(
        oX=sd((HR, C), BF),
        oDA=sd((2, HR, CH), BF),
        oOUT=sd((2, PR, CH), BF),
        oR=sd((TAPS, C, CH), BF),
        oDP=sd((2 * C, CH), BF),
        oST=sd((16, C), F32),
    )
    spans = {}

    def lay(pool, start, items):
        for name, n in items:
            spans[name] = (pool, start, n)
            start += n
        return start

    end = lay("N", 0, [("RAW", 2 * HR), ("STO", HR), ("COTR", 2 * PR), ("HT", PR), ("RS", 2 * rim), ("RR", 2 * rim)])
    lay("N", spans["STO"][1], [("DPS", 2 * C)])
    lay("N", spans["COTR"][1], [(f"XB{p}", C // 2) for p in range(TAPS)])
    lay("N", spans["HT"][1], [(f"YB{p}", C // 4) for p in range(TAPS)])
    lay("N", spans["RS"][1], [(f"F{p}", C) for p in range(2)])
    end = lay("N", end, [("GD", 3 * PR)])
    lay("N", spans["GD"][1], [("R", (TAPS + 2) * C)])
    end = max(end, spans["R"][1] + (TAPS + 2) * C)
    end = lay("N", end, [(f"F{p}", C) for p in range(2, TAPS)] + [("FD", 2 * C)])
    lay("N", spans["RAW"][1] + HR, [("PS", 2 * C)])
    sizes = {p: C for p in range(TAPS + 1)} | ({6: CH, 7: CH} if early else {6: C})
    rest = range(TAPS, len(sizes))
    end = lay("N", end, [(f"XB{p}", sizes[p] // 2) for p in rest] + [(f"YB{p}", sizes[p] // 4) for p in rest])
    n_rows = lay("N", end, [(f"ZB{p}", C // 2 if p > 5 and early else C // 4) for p in range(len(sizes))])
    end = lay("M", 0, [("X", HR), ("gap", 32), ("HM", PR), ("CT", PR), ("H0", HR + 32), ("H1", HR + 32)])
    lay("M", 0, [("GC0", HR + 32)])
    lay("M", spans["HM"][1], [("XX", HR)])
    m_rows = lay("M", end, [("W", TAPS * C), ("PW", HC), ("DT", 3 * HC)])
    f_rows = lay("F", 0, [("E0", PR + 2 * rim), ("GM", 2 * PR), ("DO", PR), ("GT", PR)])
    V = pltpu.VMEM
    DMA = pltpu.SemaphoreType.DMA
    scratch = dict(
        N=V((n_rows, CH), BF),
        M=V((m_rows, C), BF),
        F=V((f_rows, CH), F32),
        LANES=V((C // 128 * RT, 128), F32),
        MASK=V((4, HR, 128), BF),
        SEG=V(seg.shape, jnp.int32),
        SEGX=V(((T + 256) * ROWS, 128), F32),
        PAR=V((2, 8, CH), F32),
        ST=V((16, C), F32),
        SUM=V((8, C), F32),
        POOL=V((PR, C), F32),
        DIFF=V((PR, C), F32),
        lsem=DMA((15 + NP,)),
        shs=DMA((13,)), shr=DMA((13,)),
        csem_s=DMA((14,)), csem_r=DMA((14,)),
        as_=DMA((6,)), ar_=DMA((6,)),
        bs_=DMA((6,)), br_=DMA((6,)),
        hs=DMA((8,)), hr=DMA((8,)),
        ps=DMA((NP,)), pr=DMA((NP, 4)),
        zr=DMA((NP, 2)),
    )
    for i, (name, width) in enumerate([("XI", C), ("XM", C), ("XH", HC), ("XG", HC), ("XD", C), ("XS", C)]):
        if early:
            sizes_ab = (nb * na, nm) if i == 0 else (nm, nb * na)
            widths = (CH, CH) if i == 0 else (width, width)
        else:
            sizes_ab = (NA, nb)
            widths = (CH if i == 0 else width, width)
        for x, n, lanes in zip("AB", sizes_ab, widths):
            scratch[name + x] = V((n, 2, lanes), F32)
    outer = nb // 4
    if outer > 1:
        scratch.update(os_=DMA((NP, outer)), or_=DMA((NP, outer)))
        n = outer * (C // 16)
        assert lay("F", spans["E0"][1], [(f"OB{p}", n) for p in range(TAPS)]) <= spans["GM"][1]
        assert lay("F", spans["DO"][1], [(f"OB{p}", n) for p in range(TAPS, TAPS + 2)]) <= f_rows
    names = list(inputs) + list(outs) + list(scratch)
    anyspec = pl.BlockSpec(memory_space=pl.ANY)
    vmem = pl.BlockSpec(memory_space=pltpu.VMEM)
    res = pl.pallas_call(
        functools.partial(main_body, (nb, nm, na, T, S, CH, HC), names, spans),
        out_shape=list(outs.values()),
        in_specs=[vmem if n.startswith("v") else anyspec for n in inputs],
        out_specs=[anyspec] * len(outs),
        scratch_shapes=list(scratch.values()),
        compiler_params=pltpu.CompilerParams(
            collective_id=0, has_side_effects=True, vmem_limit_bytes=VMEM_BYTES
        ),
        cost_estimate=pl.CostEstimate(flops=44_000_000_000, bytes_accessed=40_000_000, transcendentals=8_000_000),
        name="forward_and_backward",
    )(*inputs.values())
    return dict(zip(outs, res, strict=True))


def last_body(dims, sig, da, out, rr, dp, stats, gs, oo, gw, dk, pw, g0, g1, g2, g3, g4, g5,
              sig_v, da_v, out_v, rr_v, dp_v, st_v, gs_v, oo_v, gw_v, dk_v, pw_v, lanes, ls, ss):
    CH, total_in = dims
    m = lax.axis_index("mp")
    taps = rr.shape[0]
    T, S = sig.shape[1], oo.shape[1]
    HH = g4.shape[0]
    copy = pltpu.make_async_copy

    def load(src, dst, i):
        return copy(src, dst, ls.at[i])

    def load_tap(k):
        return load(rr.at[k], rr_v.at[k], k)

    def load_half(h):
        rows = pl.ds(h * ROWS, ROWS)
        return [
            load(da.at[h], da_v.at[h], taps + 3 * h),
            load(sig.at[rows], sig_v.at[rows], taps + 3 * h + 1),
            load(out.at[h], out_v.at[h], taps + 3 * h + 2),
        ]

    ld_st = load(stats, st_v, taps + 6)
    ld_dp = load(dp, dp_v, taps + 7)
    ld_st.start()
    for h in range(2):
        for c in load_half(h):
            c.start()
    for k in range(taps):
        load_tap(k).start()
    ld_dp.start()

    def store_tap(k):
        return copy(gw_v.at[k], gw.at[k], ss.at[k])

    def tap(k, _):
        load_tap(k).wait()

        def part(i, _):
            at = pl.ds(al(i * 96, 96), 96)
            gw_v[k, at, :] = rr_v[k, at, :].astype(F32)
            return 0

        lax.fori_loop(0, rr.shape[1] // 96, part, 0)
        store_tap(k).start()
        return 0

    ld_st.wait()
    st = st_v[:, pl.ds(al(m * CH, CH), CH)]
    mu, inv, gain, gg, gb = [st[i : i + 1] for i in (0, 1, 2, 4, 5)]
    scale = gain * inv
    mg, mb = gg / total_in, gb / total_in
    BB = 64
    n = BB * ROWS

    def store_gs(h, c):
        at = (pl.ds(h * ROWS, ROWS), pl.ds(al(c * BB, BB), BB))
        return copy(gs_v.at[at], gs.at[at], ss.at[taps + h * (T // BB) + c])

    def store_oo(h):
        at = pl.ds(h * ROWS, ROWS)
        return copy(oo_v.at[at], oo.at[at], ss.at[taps + 2 * (T // BB) + h])

    def fill(v):
        for j in range(CH // 128):
            lanes[j * n : (j + 1) * n, :] = v[:, j * 128 : (j + 1) * 128].astype(F32)

    def half(h, _):
        for c in load_half(h):
            c.wait()

        def block(c, _):
            fill(da_v[h, pl.ds(al(c * n, n), n), :])
            bins = pl.ds(al(c * BB, BB), BB)
            for row in range(ROWS):
                for j in range(CH // 128):
                    l = slice(j * 128, (j + 1) * 128)
                    d = lanes[pl.ds(j * n + row, BB, stride=ROWS), :]
                    xhat = (sig_v[h * ROWS + row, bins, l].astype(F32) - mu[:, l]) * inv[:, l]
                    gs_v[h * ROWS + row, bins, l] = scale[:, l] * (d - mb[:, l] - xhat * mg[:, l])
            store_gs(h, c).start()
            return 0

        lax.fori_loop(0, T // BB, block, 0)

        def block2(c, _):
            fill(out_v[h, pl.ds(al(c * n, n), n), :])
            bins = pl.ds(al(c * BB, BB), BB)
            for row in range(ROWS):
                for j in range(CH // 128):
                    oo_v[h * ROWS + row, bins, j * 128 : (j + 1) * 128] = lanes[pl.ds(j * n + row, BB, stride=ROWS), :].astype(BF)
            return 0

        lax.fori_loop(0, S // BB, block2, 0)
        store_oo(h).start()
        return 0

    lax.fori_loop(0, 2, half, 0)
    lax.fori_loop(0, taps, tap, 0)
    ld_dp.wait()
    for k, at in enumerate((0, 6, 2)):
        for h in range(2):
            dk_v[k * HH : (k + 1) * HH, h * CH : (h + 1) * CH] = dp_v[(at + h) * HH : (at + h + 1) * HH, :].astype(F32)
    pw_v[...] = dp_v[4 * HH : 6 * HH, :].astype(F32)
    st_dk = copy(dk_v, dk, ss.at[taps + 2 * (T // BB) + 2])
    st_pw = copy(pw_v, pw, ss.at[taps + 2 * (T // BB) + 3])
    st_dk.start()
    st_pw.start()
    for ref, i in ((g0, 4), (g1, 5), (g2, 6), (g3, 7)):
        ref[...] = st[i : i + 1].reshape(CH)
    hid = st_v[8:10, : 2 * HH]
    hid = jnp.where(m == 0, hid[:, :HH], hid[:, HH:])
    g4[...] = hid[0:1].reshape(HH)
    g5[...] = hid[1:2].reshape(HH)
    for k in range(taps):
        store_tap(k).wait()
    for h in range(2):
        for c in range(T // BB):
            store_gs(h, c).wait()
        store_oo(h).wait()
    st_dk.wait()
    st_pw.wait()


def call_last(axes, sig, o):
    nb, nm, na = axes
    rows, T, CH = sig.shape
    S = T // 2
    C = 2 * CH
    HC = CH
    HH = HC // 2
    rr = o["oR"]
    total_in = float(rows * T * nb * na)
    sd = jax.ShapeDtypeStruct
    V = pltpu.VMEM
    anyspec = pl.BlockSpec(memory_space=pl.ANY)
    vmem = pl.BlockSpec(memory_space=pltpu.VMEM)
    inputs = (sig, o["oDA"], o["oOUT"], rr, o["oDP"], o["oST"])
    big = [sd((rows, T, CH), F32), sd((rows, S, CH), BF), sd(rr.shape, F32), sd((3 * HH, C), F32), sd((HC, CH), F32)]
    return pl.pallas_call(
        functools.partial(last_body, (CH, total_in)),
        out_shape=big + [sd((CH,), F32)] * 4 + [sd((HH,), F32)] * 2,
        in_specs=[anyspec] * len(inputs),
        out_specs=[anyspec] * len(big) + [vmem] * 6,
        scratch_shapes=[V(x.shape, x.dtype) for x in inputs]
        + [V(x.shape, x.dtype) for x in big]
        + [V((CH // 128 * 64 * ROWS, 128), F32), pltpu.SemaphoreType.DMA((rr.shape[0] + 8,)), pltpu.SemaphoreType.DMA((rr.shape[0] + T // 32 + 4,))],
        compiler_params=pltpu.CompilerParams(vmem_limit_bytes=VMEM_BYTES),
        name="last_pass",
    )(*inputs)


def on_device(axes, signal, seg, cotangent, conv_wide, taps, pointwise, *vectors):
    CH = signal.shape[2]
    o = call_main(
        axes, signal.reshape(-1, CH), seg, cotangent.reshape(-1, CH), conv_wide, jnp.swapaxes(taps, 1, 2), pointwise, vectors
    )
    gs, out, gw, dk, pw, *small = call_last(axes, signal, o)
    K, C, HH = taps.shape
    return (out, gs, gw.reshape(conv_wide.shape), jnp.swapaxes(dk.reshape(K, HH, C), 1, 2), pw, *small)


def solution(mesh):
    axes = (mesh.shape["bins"], mesh.shape["mp"], mesh.shape["batch"])
    cut = P("batch", "bins", "mp")
    tap = P(None, None, "mp")
    return jax.shard_map(
        functools.partial(on_device, axes),
        mesh=mesh,
        in_specs=(cut, P("batch", None), cut, tap, tap, P(None, "mp")) + (P("mp"),) * 6,
        out_specs=(cut, cut, tap, tap, P(None, "mp")) + (P("mp"),) * 6,
        check_vma=False,
    )
```
